32 devices in a mesh: grp: 2 (over y), ft: 4 (over z), bl: 4 (over x, core).
Axes of the slice: x: 2, y: 2, z: 4, core: 2. Of those that a mesh axis runs over, the one named last changes fastest.
Arguments:
- voltages: bfloat16 [2, 16384, 1024], P(None, ('grp', 'ft'), 'bl'), parts along dimension 1, may hold values from -11 to 11
- coefs: float32 [8, 2048], replicated, may hold values from -2 to 2
- block_ids: int32 [4], replicated, may hold values from 0 to 3, each once
- tile_owner: int32 [20], P('grp'), parts along dimension 0, may hold values from 0 to 3, as said below
Outputs:
- vis: float32 [2, 64, 20, 256, 256], P(None, ('grp', 'ft'), 'bl'), parts along dimension 1
The draws below stay inside these ranges and needn't reach their ends.
There are 2 independent parts, one for each index of `grp`. The reference program is written for one: setup_inputs(seed, part) draws one part's arguments, and reference() takes and returns one part's arrays. A program takes and returns all parts, laid end to end along the dimension named above; an argument that names none is the same for every part. Nothing has to cross between parts.
Inputs may be any that keep to these rules, and one draw needn't show every extreme that they name: tile_owner[t] is the index along bl of the device that owns tile t; one owner holds exactly 5 tiles, the others share the remaining tiles as evenly as counts allow.
All inputs are finite; a program needn't handle non-finite values.
Results may differ from the reference program's by a relative error of at most 0.00099.
Values may be sent and summed in bfloat16 or wider, within the bound.
No kernel may reach another device: no remote copies, remote signals or barrier semaphores. Data moves between devices by JAX's collectives and lax.ppermute only.
A program may use at most 128 MiB of HBM per device.

```python
import math
import jax
import jax.numpy as jnp
import numpy as np
from jax import lax

NIN = 1024
NCH = 2048
TAPS = 8
AVG = 64
SPECTRA = 4
TIME = 8192
NB = 4
BLK = 256
NTILES = 10
MAXT = 5
COARSE = 32


def draw_voltages(key, part):
    key_signal, key_delay, key_gain, key_noise = jax.random.split(key, 4)
    delay_span = 16
    signal = jnp.clip(jax.random.normal(key_signal, (2, TIME + delay_span), jnp.float32), -5.0, 5.0)
    delays = jax.random.randint(key_delay, (NIN,), 0, delay_span)
    gain_of = jax.random.uniform(key_gain, (NIN,), jnp.float32, 0.3, 1.0)
    noise_part = jnp.clip(jax.random.normal(key_noise, (2, TIME, NIN), jnp.float32), -5.0, 5.0)
    source_pos = jnp.arange(TIME, dtype=jnp.int32)[:, None] + (delay_span - delays)[None, :]
    delayed = signal[:, source_pos]
    return (gain_of[None, None, :] * delayed + noise_part).astype(jnp.bfloat16)


def draw_tile_owner(key, part):
    key_heavy, key_order, key_offset = jax.random.split(key, 3)
    heavy_owner = jax.random.randint(key_heavy, (), 0, NB)
    tile_order = jax.random.permutation(key_order, NTILES)
    position = jnp.argsort(tile_order)
    spread_offset = jax.random.randint(key_offset, (), 0, NB - 1)
    other_owner = (heavy_owner + 1 + (position - MAXT + spread_offset) % (NB - 1)) % NB
    return jnp.where(position < MAXT, heavy_owner, other_owner).astype(jnp.int32)


def gaussian(own_key, dims, deviation, most, held_as=jnp.bfloat16):
    values = jax.random.normal(own_key, dims, jnp.float32) * deviation
    return jnp.minimum(jnp.maximum(values, -most), most).astype(held_as)


def setup_inputs(seed: int = 0, part: int = 0) -> dict:
    key_list = jax.random.split(jax.random.key(seed), 5)
    part_keys = jax.random.split(jax.random.fold_in(key_list[4], part), 5)
    voltages = draw_voltages(jax.random.fold_in(jax.random.fold_in(key_list[4], part), 71), part)
    coefs = gaussian(key_list[1], (TAPS, NCH), TAPS ** -0.5, 2.0, jnp.float32)
    block_ids = jax.random.permutation(key_list[2], NB).astype(jnp.int32)
    tile_owner = draw_tile_owner(jax.random.fold_in(jax.random.fold_in(key_list[4], part), 71), part)
    return {"voltages": voltages, "coefs": coefs, "block_ids": block_ids, "tile_owner": tile_owner}


def reference(voltages, coefs, block_ids, tile_owner):
    by_block = voltages.reshape(2, SPECTRA, NCH, NB, BLK).transpose(3, 0, 1, 2, 4)

    def channelize(block_data):
        samples = block_data.astype(jnp.float32)
        padded = jnp.concatenate([jnp.zeros((2, TAPS - 1, NCH, BLK), jnp.float32), samples], axis=1)
        filtered = jnp.zeros((2, SPECTRA, NCH, BLK), jnp.float32)
        for tap_index in range(TAPS):
            filtered = filtered + coefs[tap_index][None, None, :, None] * padded[:, tap_index:tap_index + SPECTRA]
        complex_out = jnp.fft.fft(filtered[0] + 1j * filtered[1], axis=1) * (1.0 / math.sqrt(NCH))
        return jnp.stack([jnp.real(complex_out), jnp.imag(complex_out)]).astype(jnp.bfloat16)
    spectra = lax.map(channelize, by_block)
    spectra_all = spectra.reshape(NB, 2, SPECTRA, COARSE, AVG, BLK)
    labels = jnp.arange(NB, dtype=jnp.int32)
    shard_of = lax.optimization_barrier(jnp.sum(jnp.where(block_ids[None, :] == labels[:, None], labels[None, :], 0), axis=1)).astype(jnp.int32)
    row_table = np.array([first_id for first_id in range(NB) for second_id in range(first_id, NB)], dtype=np.int32)
    col_table = np.array([second_id for first_id in range(NB) for second_id in range(first_id, NB)], dtype=np.int32)
    pair_ids = jnp.stack([jnp.asarray(row_table), jnp.asarray(col_table)], axis=1)

    def correlate(pair_row):
        row_data = spectra_all[shard_of[pair_row[0]]].astype(jnp.float32)
        col_data = spectra_all[shard_of[pair_row[1]]].astype(jnp.float32)
        products = jnp.einsum('pscax,qscay->cpqxy', row_data, col_data, precision=lax.Precision.HIGHEST)
        real_part = products[:, 0, 0] + products[:, 1, 1]
        imag_part = products[:, 1, 0] - products[:, 0, 1]
        return jnp.stack([real_part, imag_part]) * (1.0 / (AVG * SPECTRA))
    tiles = lax.map(correlate, pair_ids)
    tile_pos = jnp.arange(NTILES, dtype=jnp.int32)
    same_owner = tile_owner[None, :] == tile_owner[:, None]
    before_mask = tile_pos[None, :] < tile_pos[:, None]
    slot_rank = lax.optimization_barrier(jnp.sum((same_owner & before_mask).astype(jnp.int32), axis=1)).astype(jnp.int32)
    dest_slot = (tile_owner * MAXT + slot_rank).astype(jnp.int32)
    vis = jnp.zeros((2, COARSE, NB * MAXT, BLK, BLK), jnp.float32)
    return vis.at[:, :, dest_slot].set(tiles.transpose(1, 2, 0, 3, 4))
```

```python
import functools
import math

import jax
import jax.numpy as jnp
import ml_dtypes
import numpy as np
from jax import lax
from jax.experimental import pallas as pl
from jax.experimental.pallas import tpu as pltpu
from jax.sharding import PartitionSpec as P

AVG = 64
MXU = 256
LANES = 128
ROWS16 = 16
VMEM_BYTES = 48 * 1024 * 1024


def split_bf16(table):
    high = table.astype(ml_dtypes.bfloat16)
    low = (table - high.astype(np.float64)).astype(ml_dtypes.bfloat16)
    return high, low


def matrix_tables(inner_len):
    steps = np.arange(inner_len)
    angles = 2.0 * np.pi * (np.outer(steps, steps) % inner_len) / inner_len
    cos_part, sin_part = np.cos(angles), np.sin(angles)
    return split_bf16(np.block([[cos_part, -sin_part], [sin_part, cos_part]]))


def twiddle_tables(radix, inner_len):
    chan_count = radix * inner_len
    angles = 2.0 * np.pi * np.outer(np.arange(radix), np.arange(inner_len)) / chan_count
    scale = 1.0 / math.sqrt(chan_count)
    return np.stack([np.cos(angles) * scale, np.sin(angles) * scale]).astype(np.float32)


def rotate(real, imag, step, count):
    step = step % count
    if step == 0:
        return real, imag
    if 4 * step == count:
        return imag, -real
    if 2 * step == count:
        return -real, -imag
    if 4 * step == 3 * count:
        return -imag, real
    cos_step = math.cos(2.0 * math.pi * step / count)
    sin_step = math.sin(2.0 * math.pi * step / count)
    if 8 * step == count:
        return cos_step * (real + imag), cos_step * (imag - real)
    return cos_step * real + sin_step * imag, cos_step * imag - sin_step * real


def butterflies(parts):
    count = len(parts)
    if count == 1:
        return parts
    half = count // 2
    sums, diffs = [], []
    for k in range(half):
        (ar, ai), (br, bi) = parts[k], parts[k + half]
        sums.append((ar + br, ai + bi))
        diffs.append(rotate(ar - br, ai - bi, k, count))
    even, odd = butterflies(sums), butterflies(diffs)
    out = []
    for k in range(half):
        out += [even[k], odd[k]]
    return out


def pack_kernel(radix, v_ref, o_ref, wide):
    dests, _, rows, _ = o_ref.shape
    inner = v_ref.shape[1] // radix
    wide[...] = v_ref[0].astype(jnp.float32)
    for phase in range(radix):
        part = wide[pl.ds(phase, inner, stride=radix), :]
        turned = part.T.astype(jnp.bfloat16)
        for dest in range(dests):
            o_ref[dest, 0, :, phase * inner : (phase + 1) * inner] = turned[
                dest * rows : (dest + 1) * rows
            ]


def pack(voltages, chunk, dests, radix):
    _, samples, _ = voltages.shape
    rows = LANES // dests
    return pl.pallas_call(
        functools.partial(pack_kernel, radix),
        grid=(2,),
        in_specs=[pl.BlockSpec((1, samples, LANES), lambda p: (p, 0, chunk))],
        out_specs=pl.BlockSpec((dests, 1, rows, samples), lambda p: (0, p, 0, 0)),
        out_shape=jax.ShapeDtypeStruct((dests, 2, rows, samples), jnp.bfloat16),
        scratch_shapes=[pltpu.VMEM((samples, LANES), jnp.float32)],
        compiler_params=pltpu.CompilerParams(vmem_limit_bytes=VMEM_BYTES),
        name="pack_inputs",
    )(voltages)


def transform_kernel(radix, v_ref, c_ref, gh_ref, gl_ref, tw_ref, *rest):
    out_refs, (split, prod) = rest[:-2], rest[-2:]
    spectra, _, rows, samples = v_ref.shape
    taps = c_ref.shape[0]
    inner = samples // radix
    group = spectra * rows

    @pl.loop(0, radix)
    def _(phase):
        lane0 = pl.multiple_of(phase * inner, inner)
        row0 = pl.multiple_of(phase * group, group)
        for part in range(2):
            for sub in range(0, rows, ROWS16):
                blocks = [
                    v_ref[b, part, pl.ds(sub, ROWS16), pl.ds(lane0, inner)].astype(jnp.float32)
                    for b in range(spectra)
                ]
                for s in range(spectra):
                    total = None
                    for b in range(max(0, s - taps + 1), s + 1):
                        term = c_ref[taps - 1 - s + b, pl.ds(phase, 1), :] * blocks[b]
                        total = term if total is None else total + term
                    high = total.astype(jnp.bfloat16)
                    low = (total - high.astype(jnp.float32)).astype(jnp.bfloat16)
                    at = pl.ds(pl.multiple_of(row0 + s * rows + sub, ROWS16), ROWS16)
                    split[at, part * inner : (part + 1) * inner] = high
                    split[at, (2 + part) * inner : (3 + part) * inner] = low

    high = split[:, : 2 * inner]
    prod[...] = (
        jnp.dot(high, gh_ref[...], preferred_element_type=jnp.float32)
        + jnp.dot(high, gl_ref[...], preferred_element_type=jnp.float32)
        + jnp.dot(split[:, 2 * inner :], gh_ref[...], preferred_element_type=jnp.float32)
    )

    halves = len(out_refs)

    @pl.loop(0, spectra)
    def _(s):
        for sub in range(0, rows, ROWS16):
            for lane in range(0, inner, LANES):
                parts = []
                for phase in range(radix):
                    at = pl.ds(pl.multiple_of(phase * group + s * rows + sub, ROWS16), ROWS16)
                    yr = prod[at, lane : lane + LANES]
                    yi = prod[at, inner + lane : inner + lane + LANES]
                    cos_here = tw_ref[0, phase : phase + 1, lane : lane + LANES]
                    sin_here = tw_ref[1, phase : phase + 1, lane : lane + LANES]
                    if phase == 0:
                        parts.append((yr * cos_here, yi * cos_here))
                    else:
                        parts.append(
                            (yr * cos_here + yi * sin_here, yi * cos_here - yr * sin_here)
                        )
                for high_step, pair in enumerate(butterflies(parts)):
                    out = out_refs[high_step % halves]
                    for part in range(2):
                        out[
                            high_step // halves, part, s, sub : sub + ROWS16, lane : lane + LANES
                        ] = pair[part].astype(jnp.bfloat16)


def transform_chunk(blocks, coef_table, radix, dests):
    spectra, _, rows, samples = blocks.shape
    inner = samples // radix
    halves = radix // dests
    g_high, g_low = matrix_tables(inner)
    vmem = pl.BlockSpec(memory_space=pltpu.VMEM)
    total = radix * spectra * rows
    return pl.pallas_call(
        functools.partial(transform_kernel, radix),
        in_specs=[vmem] * 5,
        out_specs=[vmem] * halves,
        out_shape=[
            jax.ShapeDtypeStruct((dests, 2, spectra, rows, inner), jnp.bfloat16)
        ]
        * halves,
        scratch_shapes=[
            pltpu.VMEM((total, 4 * inner), jnp.bfloat16),
            pltpu.VMEM((total, 2 * inner), jnp.float32),
        ],
        cost_estimate=pl.CostEstimate(
            flops=3 * 2 * total * 4 * inner * inner, bytes_accessed=6 << 20, transcendentals=0
        ),
        compiler_params=pltpu.CompilerParams(vmem_limit_bytes=VMEM_BYTES),
        name="filter_transform",
    )(blocks, coef_table, jnp.asarray(g_high), jnp.asarray(g_low), twiddle_tables(radix, inner))


def correlate_kernel(chunks, scale, table_ref, *rest):
    g_refs, o_ref, left = rest[:chunks], rest[-2], rest[-1]
    blocks, senders, _, spectra, rows, inner = g_refs[0].shape
    slots = o_ref.shape[2]
    coarse = inner // AVG
    side = chunks * senders * rows
    step = pl.program_id(0)

    @pl.when(step == 0)
    def _():
        @pl.loop(0, blocks)
        def _(block):
            for chunk in range(chunks):
                for sender in range(senders):
                    row = (chunk * senders + sender) * rows
                    for part in range(2):
                        pieces = [g_refs[chunk][block, sender, part, s] for s in range(spectra)]
                        for c in range(coarse):
                            line = jnp.concatenate(
                                [piece[:, c * AVG : (c + 1) * AVG] for piece in pieces], axis=1
                            )
                            width = line.shape[1]
                            left[c, block, row : row + rows, part * width : (part + 1) * width] = (
                                line
                            )
                            left[
                                c,
                                block,
                                side + row : side + row + rows,
                                (1 - part) * width : (2 - part) * width,
                            ] = -line if part == 0 else line

    count = table_ref[2 * slots]
    for slot in range(slots):

        @pl.when(slot < count)
        def _(slot=slot):
            rows_of = left[step, table_ref[slot]]
            cols_of = left[step, table_ref[slots + slot], pl.ds(0, side), :]
            tile = (
                lax.dot_general(
                    rows_of,
                    cols_of,
                    (((1,), (1,)), ((), ())),
                    preferred_element_type=jnp.float32,
                )
                * scale
            )
            o_ref[0, 0, slot] = tile[:side]
            o_ref[1, 0, slot] = tile[side:]

        @pl.when(slot >= count)
        def _(slot=slot):
            o_ref[:, 0, slot] = jnp.zeros((2, side, side), jnp.float32)


def correlate(table, gathered, part_index, part_count, slots, vis):
    chunks = len(gathered)
    blocks, senders, _, spectra, rows, inner = gathered[0].shape
    coarse = inner // AVG
    side = chunks * senders * rows
    scale = 1.0 / (AVG * spectra)
    in_specs = [
        pl.BlockSpec(part.shape, lambda c, t: (0,) * 6, pipeline_mode=pl.Buffered(1))
        for part in gathered
    ]
    args = [table, *gathered]
    aliases = {}
    if vis is not None:
        in_specs.append(pl.BlockSpec(memory_space=pl.ANY))
        args.append(vis)
        aliases = {len(args) - 1: 0}
    return pl.pallas_call(
        functools.partial(correlate_kernel, chunks, scale),
        grid_spec=pltpu.PrefetchScalarGridSpec(
            num_scalar_prefetch=1,
            grid=(coarse,),
            in_specs=in_specs,
            out_specs=pl.BlockSpec(
                (2, 1, slots, side, side), lambda c, t: (0, part_index * coarse + c, 0, 0, 0)
            ),
            scratch_shapes=[
                pltpu.VMEM((coarse, blocks, 2 * side, 2 * spectra * AVG), jnp.bfloat16)
            ],
        ),
        out_shape=jax.ShapeDtypeStruct(
            (2, part_count * coarse, slots, side, side), jnp.float32
        ),
        input_output_aliases=aliases,
        cost_estimate=pl.CostEstimate(
            flops=coarse * slots * 2 * 4 * side * side * spectra * AVG,
            bytes_accessed=16 << 20,
            transcendentals=0,
        ),
        compiler_params=pltpu.CompilerParams(vmem_limit_bytes=VMEM_BYTES),
        name="correlate_tiles",
    )(*args)


def tile_tables(block_ids, tile_owner):
    block_count = lax.axis_size("bl")
    tile_count = block_count * (block_count + 1) // 2
    slot_cap = 2 * tile_count // block_count
    pairs = [(i, j) for i in range(block_count) for j in range(i, block_count)]
    row_table = np.array([i for i, _ in pairs], np.int32)
    col_table = np.array([j for _, j in pairs], np.int32)
    mine = (tile_owner == lax.axis_index("bl")).astype(jnp.int32)
    earlier = np.tril(np.ones((tile_count, tile_count), np.int32), -1)
    rank = jnp.sum(earlier * mine[None, :], axis=1)
    labels = np.arange(block_count, dtype=np.int32)
    shard_of = jnp.sum(jnp.where(block_ids[None, :] == labels[:, None], labels[None, :], 0), axis=1)
    row_shard = jnp.sum(
        jnp.where(row_table[:, None] == labels[None, :], shard_of[None, :], 0), axis=1
    )
    col_shard = jnp.sum(
        jnp.where(col_table[:, None] == labels[None, :], shard_of[None, :], 0), axis=1
    )
    here = (mine[None, :] == 1) & (rank[None, :] == np.arange(slot_cap, dtype=np.int32)[:, None])
    rows = jnp.sum(jnp.where(here, row_shard[None, :], 0), axis=1)
    cols = jnp.sum(jnp.where(here, col_shard[None, :], 0), axis=1)
    table = jnp.concatenate([rows, cols, jnp.sum(mine, keepdims=True)]).astype(jnp.int32)
    return table, slot_cap


def takes_kernels(mesh, voltages, coefs):
    dests = mesh.shape["ft"]
    inputs = voltages.shape[2] // mesh.shape["bl"]
    per_dev = voltages.shape[1] // (mesh.shape["grp"] * dests)
    chan_count = coefs.shape[1]
    radix = chan_count // MXU
    return (
        per_dev == chan_count
        and chan_count % MXU == 0
        and radix & (radix - 1) == 0
        and radix % dests == 0
        and radix <= 8
        and inputs % LANES == 0
        and LANES % dests == 0
        and (LANES // dests) % ROWS16 == 0
        and (dests * AVG) % LANES == 0
    )


def per_device_kernels(voltages, coefs, block_ids, tile_owner):
    dests = lax.axis_size("ft")
    taps, chan_count = coefs.shape
    radix = chan_count // MXU
    chunk_count = voltages.shape[2] // LANES
    halves = radix // dests
    coef_table = coefs.reshape(taps, MXU, radix).transpose(0, 2, 1)
    table, slot_cap = tile_tables(block_ids, tile_owner)
    arrived = []
    for chunk in range(chunk_count):
        packed = pack(voltages, chunk, dests, radix)
        arrived.append(lax.all_to_all(packed, "ft", split_axis=0, concat_axis=0, tiled=True))
    gathered = [[] for _ in range(halves)]
    for chunk in range(chunk_count):
        for half, part in enumerate(transform_chunk(arrived[chunk], coef_table, radix, dests)):
            turned = lax.all_to_all(part, "ft", split_axis=0, concat_axis=0, tiled=True)
            gathered[half].append(lax.all_gather(turned, "bl", axis=0, tiled=False))
    vis = None
    for half in range(halves):
        vis = correlate(table, gathered[half], half, halves, slot_cap, vis)
    return vis


def tile_product(row_part, col_part, norm_scale):
    products = jnp.einsum(
        "pscax,qscay->cpqxy", row_part, col_part, preferred_element_type=jnp.float32
    )
    real_part = products[:, 0, 0] + products[:, 1, 1]
    imag_part = products[:, 1, 0] - products[:, 0, 1]
    return jnp.stack([real_part, imag_part]) * norm_scale


def dft_tables(order_len):
    steps_one = jnp.arange(order_len, dtype=jnp.int32)
    phase_grid = steps_one[:, None] * steps_one[None, :] % order_len
    angles = phase_grid.astype(jnp.float32) * (2.0 * math.pi / order_len)
    return (jnp.cos(angles), jnp.sin(angles))


def transform(filtered):
    per_dev = filtered.shape[1]
    chan_count = filtered.shape[2]
    rows_here = filtered.shape[3]
    outer_len = math.isqrt(chan_count)
    while chan_count % outer_len != 0:
        outer_len = outer_len - 1
    inner_len = chan_count // outer_len
    highest = lax.Precision.HIGHEST
    reshaped = filtered.reshape(2, per_dev, outer_len, inner_len, rows_here)
    real_in = reshaped[0]
    imag_in = reshaped[1]
    cos_outer, sin_outer = dft_tables(outer_len)
    section_re = jnp.einsum("snkb,nm->smkb", real_in, cos_outer, precision=highest) + jnp.einsum(
        "snkb,nm->smkb", imag_in, sin_outer, precision=highest
    )
    section_im = jnp.einsum("snkb,nm->smkb", imag_in, cos_outer, precision=highest) - jnp.einsum(
        "snkb,nm->smkb", real_in, sin_outer, precision=highest
    )
    twiddle_grid = (
        jnp.arange(outer_len, dtype=jnp.int32)[:, None]
        * jnp.arange(inner_len, dtype=jnp.int32)[None, :]
        % chan_count
    )
    twiddle_angles = twiddle_grid.astype(jnp.float32) * (2.0 * math.pi / chan_count)
    cos_twiddle = jnp.cos(twiddle_angles)[None, :, :, None]
    sin_twiddle = jnp.sin(twiddle_angles)[None, :, :, None]
    rot_re = section_re * cos_twiddle + section_im * sin_twiddle
    rot_im = section_im * cos_twiddle - section_re * sin_twiddle
    cos_inner, sin_inner = dft_tables(inner_len)
    final_re = jnp.einsum("smkb,kq->sqmb", rot_re, cos_inner, precision=highest) + jnp.einsum(
        "smkb,kq->sqmb", rot_im, sin_inner, precision=highest
    )
    final_im = jnp.einsum("smkb,kq->sqmb", rot_im, cos_inner, precision=highest) - jnp.einsum(
        "smkb,kq->sqmb", rot_re, sin_inner, precision=highest
    )
    stacked = jnp.stack([final_re, final_im]).reshape(2, per_dev, chan_count, rows_here)
    return (stacked * (1.0 / math.sqrt(chan_count))).astype(jnp.bfloat16)


def apply_taps(window, coef_part, taps_count, out_len):
    filtered = jnp.zeros((2, out_len, window.shape[2], window.shape[3]), jnp.float32)
    for tap_index in range(taps_count):
        filtered = filtered + coef_part[tap_index][None, None, :, None] * window[
            :, tap_index : tap_index + out_len
        ].astype(jnp.float32)
    return filtered


def per_device(voltages, coefs, block_ids, tile_owner):
    taps_count = coefs.shape[0]
    chan_count = coefs.shape[1]
    rows_here = voltages.shape[2]
    per_dev = voltages.shape[1] // chan_count
    volt_blocks = voltages.reshape(2, per_dev, chan_count, rows_here)
    phase_block = lax.all_to_all(volt_blocks, "ft", split_axis=2, concat_axis=1, tiled=True)
    spectra_count = phase_block.shape[1]
    phase_here = phase_block.shape[2]
    coef_part = lax.dynamic_slice_in_dim(coefs, lax.axis_index("ft") * phase_here, phase_here, 1)
    zero_front = jnp.zeros((2, taps_count - 1, phase_here, rows_here), phase_block.dtype)
    long_window = jnp.concatenate([zero_front, phase_block], axis=1)
    phase_filtered = apply_taps(long_window, coef_part, taps_count, spectra_count)
    filtered = lax.all_to_all(phase_filtered, "ft", split_axis=1, concat_axis=2, tiled=True)
    spectra = transform(filtered)
    turned = lax.all_to_all(spectra, "ft", split_axis=2, concat_axis=1, tiled=True)
    spectra_all = turned.shape[1]
    chan_here = turned.shape[2]
    coarse_here = chan_here // AVG
    coarse_view = turned.reshape(2, spectra_all, coarse_here, AVG, rows_here)
    norm_scale = 1.0 / (AVG * spectra_all)
    block_count = lax.axis_size("bl")
    my_index = lax.axis_index("bl")
    tile_count = block_count * (block_count + 1) // 2
    slot_cap = 2 * tile_count // block_count
    row_table = jnp.asarray(
        np.array(
            [
                first_id
                for first_id in range(block_count)
                for second_id in range(first_id, block_count)
            ],
            dtype=np.int32,
        )
    )
    col_table = jnp.asarray(
        np.array(
            [
                second_id
                for first_id in range(block_count)
                for second_id in range(first_id, block_count)
            ],
            dtype=np.int32,
        )
    )
    tile_pos = jnp.arange(tile_count, dtype=jnp.int32)
    same_owner = tile_owner[None, :] == tile_owner[:, None]
    before_mask = tile_pos[None, :] < tile_pos[:, None]
    slot_rank = jnp.sum((same_owner & before_mask).astype(jnp.int32), axis=1)
    labels = jnp.arange(block_count, dtype=jnp.int32)
    shard_of = jnp.sum(jnp.where(block_ids[None, :] == labels[:, None], labels[None, :], 0), axis=1)
    gathered = lax.all_gather(coarse_view[None], "bl", axis=0, tiled=True)
    mine_mask = tile_owner == my_index
    own_count = jnp.sum(mine_mask.astype(jnp.int32))
    slot_steps = jnp.arange(slot_cap, dtype=jnp.int32)
    slot_tile = jnp.sum(
        jnp.where(
            mine_mask[None, :] & (slot_rank[None, :] == slot_steps[:, None]), tile_pos[None, :], 0
        ),
        axis=1,
    )

    def one_tile(slot_pos, result_tiles):
        tile_id = slot_tile[slot_pos]
        row_block = gathered[shard_of[row_table[tile_id]]]
        col_block = gathered[shard_of[col_table[tile_id]]]
        tile = tile_product(row_block, col_block, norm_scale)
        return lax.dynamic_update_slice(result_tiles, tile[:, :, None], (0, 0, slot_pos, 0, 0))

    empty_tiles = jnp.zeros((2, coarse_here, slot_cap, rows_here, rows_here), jnp.float32)
    return lax.fori_loop(0, own_count, one_tile, empty_tiles)


def solution(mesh):
    def correlator(voltages, coefs, block_ids, tile_owner):
        fits = takes_kernels(mesh, voltages, coefs)
        return jax.shard_map(
            per_device_kernels if fits else per_device,
            mesh=mesh,
            in_specs=(P(None, ("grp", "ft"), "bl"), P(), P(), P("grp")),
            out_specs=P(None, ("grp", "ft"), "bl", None, None),
            check_vma=False,
        )(voltages, coefs, block_ids, tile_owner)

    return correlator
```

```python
import functools
import math

import jax
import jax.numpy as jnp
import ml_dtypes
import numpy as np
from jax import lax
from jax.experimental import pallas as pl
from jax.experimental.pallas import tpu as pltpu
from jax.sharding import PartitionSpec as P

AVG = 64
MXU = 256
LANES = 128
ROWS16 = 16
VMEM_BYTES = 48 * 1024 * 1024


def split_bf16(table):
    high = table.astype(ml_dtypes.bfloat16)
    low = (table - high.astype(np.float64)).astype(ml_dtypes.bfloat16)
    return high, low


def matrix_tables(inner_len):
    steps = np.arange(inner_len)
    angles = 2.0 * np.pi * (np.outer(steps, steps) % inner_len) / inner_len
    cos_part, sin_part = np.cos(angles), np.sin(angles)
    return split_bf16(np.block([[cos_part, -sin_part], [sin_part, cos_part]]))


def twiddle_tables(radix, inner_len):
    chan_count = radix * inner_len
    angles = 2.0 * np.pi * np.outer(np.arange(radix), np.arange(inner_len)) / chan_count
    scale = 1.0 / math.sqrt(chan_count)
    return np.stack([np.cos(angles) * scale, np.sin(angles) * scale]).astype(np.float32)


def rotate(real, imag, step, count):
    step = step % count
    if step == 0:
        return real, imag
    if 4 * step == count:
        return imag, -real
    if 2 * step == count:
        return -real, -imag
    if 4 * step == 3 * count:
        return -imag, real
    cos_step = math.cos(2.0 * math.pi * step / count)
    sin_step = math.sin(2.0 * math.pi * step / count)
    if 8 * step == count:
        return cos_step * (real + imag), cos_step * (imag - real)
    return cos_step * real + sin_step * imag, cos_step * imag - sin_step * real


def butterflies(parts):
    count = len(parts)
    if count == 1:
        return parts
    half = count // 2
    sums, diffs = [], []
    for k in range(half):
        (ar, ai), (br, bi) = parts[k], parts[k + half]
        sums.append((ar + br, ai + bi))
        diffs.append(rotate(ar - br, ai - bi, k, count))
    even, odd = butterflies(sums), butterflies(diffs)
    out = []
    for k in range(half):
        out += [even[k], odd[k]]
    return out


def pack_kernel(radix, v_ref, o_ref, wide):
    dests, _, rows, _ = o_ref.shape
    inner = v_ref.shape[1] // radix
    wide[...] = v_ref[0].astype(jnp.float32)
    for phase in range(radix):
        part = wide[pl.ds(phase, inner, stride=radix), :]
        turned = part.T.astype(jnp.bfloat16)
        for dest in range(dests):
            o_ref[dest, 0, :, phase * inner : (phase + 1) * inner] = turned[
                dest * rows : (dest + 1) * rows
            ]


def pack(voltages, chunk, dests, radix):
    _, samples, _ = voltages.shape
    rows = LANES // dests
    return pl.pallas_call(
        functools.partial(pack_kernel, radix),
        grid=(2,),
        in_specs=[pl.BlockSpec((1, samples, LANES), lambda p: (p, 0, chunk))],
        out_specs=pl.BlockSpec((dests, 1, rows, samples), lambda p: (0, p, 0, 0)),
        out_shape=jax.ShapeDtypeStruct((dests, 2, rows, samples), jnp.bfloat16),
        scratch_shapes=[pltpu.VMEM((samples, LANES), jnp.float32)],
        compiler_params=pltpu.CompilerParams(vmem_limit_bytes=VMEM_BYTES),
        name="pack_inputs",
    )(voltages)


def transform_kernel(radix, v_ref, c_ref, gh_ref, gl_ref, tw_ref, *rest):
    out_refs, (split, prod) = rest[:-2], rest[-2:]
    spectra, _, rows, samples = v_ref.shape
    taps = c_ref.shape[0]
    inner = samples // radix
    group = spectra * rows

    @pl.loop(0, radix)
    def _(phase):
        lane0 = pl.multiple_of(phase * inner, inner)
        row0 = pl.multiple_of(phase * group, group)
        for part in range(2):
            for sub in range(0, rows, ROWS16):
                blocks = [
                    v_ref[b, part, pl.ds(sub, ROWS16), pl.ds(lane0, inner)].astype(jnp.float32)
                    for b in range(spectra)
                ]
                for s in range(spectra):
                    total = None
                    for b in range(max(0, s - taps + 1), s + 1):
                        term = c_ref[taps - 1 - s + b, pl.ds(phase, 1), :] * blocks[b]
                        total = term if total is None else total + term
                    high = total.astype(jnp.bfloat16)
                    low = (total - high.astype(jnp.float32)).astype(jnp.bfloat16)
                    at = pl.ds(pl.multiple_of(row0 + s * rows + sub, ROWS16), ROWS16)
                    split[at, part * inner : (part + 1) * inner] = high
                    split[at, (2 + part) * inner : (3 + part) * inner] = low

    high = split[:, : 2 * inner]
    prod[...] = (
        jnp.dot(high, gh_ref[...], preferred_element_type=jnp.float32)
        + jnp.dot(high, gl_ref[...], preferred_element_type=jnp.float32)
        + jnp.dot(split[:, 2 * inner :], gh_ref[...], preferred_element_type=jnp.float32)
    )

    halves = len(out_refs)

    @pl.loop(0, spectra)
    def _(s):
        for sub in range(0, rows, ROWS16):
            for lane in range(0, inner, LANES):
                parts = []
                for phase in range(radix):
                    at = pl.ds(pl.multiple_of(phase * group + s * rows + sub, ROWS16), ROWS16)
                    yr = prod[at, lane : lane + LANES]
                    yi = prod[at, inner + lane : inner + lane + LANES]
                    cos_here = tw_ref[0, phase : phase + 1, lane : lane + LANES]
                    sin_here = tw_ref[1, phase : phase + 1, lane : lane + LANES]
                    if phase == 0:
                        parts.append((yr * cos_here, yi * cos_here))
                    else:
                        parts.append(
                            (yr * cos_here + yi * sin_here, yi * cos_here - yr * sin_here)
                        )
                for high_step, pair in enumerate(butterflies(parts)):
                    out = out_refs[high_step % halves]
                    for part in range(2):
                        out[
                            high_step // halves, part, s, sub : sub + ROWS16, lane : lane + LANES
                        ] = pair[part].astype(jnp.bfloat16)


def transform_chunk(blocks, coef_table, radix, dests):
    spectra, _, rows, samples = blocks.shape
    inner = samples // radix
    halves = radix // dests
    g_high, g_low = matrix_tables(inner)
    vmem = pl.BlockSpec(memory_space=pltpu.VMEM)
    total = radix * spectra * rows
    return pl.pallas_call(
        functools.partial(transform_kernel, radix),
        in_specs=[vmem] * 5,
        out_specs=[vmem] * halves,
        out_shape=[
            jax.ShapeDtypeStruct((dests, 2, spectra, rows, inner), jnp.bfloat16)
        ]
        * halves,
        scratch_shapes=[
            pltpu.VMEM((total, 4 * inner), jnp.bfloat16),
            pltpu.VMEM((total, 2 * inner), jnp.float32),
        ],
        cost_estimate=pl.CostEstimate(
            flops=3 * 2 * total * 4 * inner * inner, bytes_accessed=6 << 20, transcendentals=0
        ),
        compiler_params=pltpu.CompilerParams(vmem_limit_bytes=VMEM_BYTES),
        name="filter_transform",
    )(blocks, coef_table, jnp.asarray(g_high), jnp.asarray(g_low), twiddle_tables(radix, inner))


def correlate_kernel(chunks, blocks, scale, table_ref, *rest):
    g_refs, o_ref, left = rest[: chunks * blocks], rest[-2], rest[-1]
    senders, _, spectra, rows, inner = g_refs[0].shape
    slots = o_ref.shape[2]
    coarse = inner // AVG
    side = chunks * senders * rows
    step = pl.program_id(0)

    @pl.when(step == 0)
    def _():
        for chunk in range(chunks):
            for block in range(blocks):
                source = g_refs[chunk * blocks + block]

                @pl.loop(0, senders)
                def _(sender, chunk=chunk, block=block, source=source):
                    row = pl.multiple_of((chunk * senders + sender) * rows, rows)
                    for part in range(2):
                        pieces = [source[sender, part, s] for s in range(spectra)]
                        for c in range(coarse):
                            line = jnp.concatenate(
                                [piece[:, c * AVG : (c + 1) * AVG] for piece in pieces], axis=1
                            )
                            width = line.shape[1]
                            left[
                                c, block, pl.ds(row, rows), part * width : (part + 1) * width
                            ] = line
                            left[
                                c,
                                block,
                                pl.ds(pl.multiple_of(side + row, rows), rows),
                                (1 - part) * width : (2 - part) * width,
                            ] = -line if part == 0 else line

    count = table_ref[2 * slots]
    for slot in range(slots):

        @pl.when(slot < count)
        def _(slot=slot):
            rows_of = left[step, table_ref[slot]]
            cols_of = left[step, table_ref[slots + slot], pl.ds(0, side), :]
            tile = (
                lax.dot_general(
                    rows_of,
                    cols_of,
                    (((1,), (1,)), ((), ())),
                    preferred_element_type=jnp.float32,
                )
                * scale
            )
            o_ref[0, 0, slot] = tile[:side]
            o_ref[1, 0, slot] = tile[side:]

        @pl.when(slot >= count)
        def _(slot=slot):
            o_ref[:, 0, slot] = jnp.zeros((2, side, side), jnp.float32)


def correlate(table, gathered, part_index, part_count, slots, vis):
    chunks, blocks = len(gathered), len(gathered[0])
    senders, _, spectra, rows, inner = gathered[0][0].shape
    coarse = inner // AVG
    side = chunks * senders * rows
    scale = 1.0 / (AVG * spectra)
    parts = [block for chunk in gathered for block in chunk]
    in_specs = [
        pl.BlockSpec(part.shape, lambda c, t: (0,) * 5, pipeline_mode=pl.Buffered(1))
        for part in parts
    ]
    args = [table, *parts]
    aliases = {}
    if vis is not None:
        in_specs.append(pl.BlockSpec(memory_space=pl.ANY))
        args.append(vis)
        aliases = {len(args) - 1: 0}
    return pl.pallas_call(
        functools.partial(correlate_kernel, chunks, blocks, scale),
        grid_spec=pltpu.PrefetchScalarGridSpec(
            num_scalar_prefetch=1,
            grid=(coarse,),
            in_specs=in_specs,
            out_specs=pl.BlockSpec(
                (2, 1, slots, side, side), lambda c, t: (0, part_index * coarse + c, 0, 0, 0)
            ),
            scratch_shapes=[
                pltpu.VMEM((coarse, blocks, 2 * side, 2 * spectra * AVG), jnp.bfloat16)
            ],
        ),
        out_shape=jax.ShapeDtypeStruct(
            (2, part_count * coarse, slots, side, side), jnp.float32
        ),
        input_output_aliases=aliases,
        cost_estimate=pl.CostEstimate(
            flops=coarse * slots * 2 * 4 * side * side * spectra * AVG,
            bytes_accessed=16 << 20,
            transcendentals=0,
        ),
        compiler_params=pltpu.CompilerParams(vmem_limit_bytes=VMEM_BYTES),
        name="correlate_tiles",
    )(*args)


def gather_blocks(own):
    count = lax.axis_size("bl")
    held = {0: own}
    bit = count // 2
    while bit:
        for r in list(held):
            held[r ^ bit] = lax.ppermute(held[r], "bl", [(i, i ^ bit) for i in range(count)])
        bit //= 2
    return [held[r] for r in range(count)]


def tile_tables(block_ids, tile_owner):
    block_count = lax.axis_size("bl")
    tile_count = block_count * (block_count + 1) // 2
    slot_cap = 2 * tile_count // block_count
    pairs = [(i, j) for i in range(block_count) for j in range(i, block_count)]
    row_table = np.array([i for i, _ in pairs], np.int32)
    col_table = np.array([j for _, j in pairs], np.int32)
    mine = (tile_owner == lax.axis_index("bl")).astype(jnp.int32)
    earlier = np.tril(np.ones((tile_count, tile_count), np.int32), -1)
    rank = jnp.sum(earlier * mine[None, :], axis=1)
    labels = np.arange(block_count, dtype=np.int32)
    shard_of = jnp.sum(jnp.where(block_ids[None, :] == labels[:, None], labels[None, :], 0), axis=1)
    row_shard = jnp.sum(
        jnp.where(row_table[:, None] == labels[None, :], shard_of[None, :], 0), axis=1
    )
    col_shard = jnp.sum(
        jnp.where(col_table[:, None] == labels[None, :], shard_of[None, :], 0), axis=1
    )
    here = (mine[None, :] == 1) & (rank[None, :] == np.arange(slot_cap, dtype=np.int32)[:, None])
    rows = jnp.sum(jnp.where(here, row_shard[None, :], 0), axis=1)
    cols = jnp.sum(jnp.where(here, col_shard[None, :], 0), axis=1)
    index = lax.axis_index("bl")
    table = jnp.concatenate([rows ^ index, cols ^ index, jnp.sum(mine, keepdims=True)])
    table = table.astype(jnp.int32)
    return table, slot_cap


def takes_kernels(mesh, voltages, coefs):
    dests = mesh.shape["ft"]
    inputs = voltages.shape[2] // mesh.shape["bl"]
    per_dev = voltages.shape[1] // (mesh.shape["grp"] * dests)
    chan_count = coefs.shape[1]
    radix = chan_count // MXU
    return (
        per_dev == chan_count
        and chan_count % MXU == 0
        and radix & (radix - 1) == 0
        and radix % dests == 0
        and radix <= 8
        and mesh.shape["bl"] & (mesh.shape["bl"] - 1) == 0
        and inputs % LANES == 0
        and LANES % dests == 0
        and (LANES // dests) % ROWS16 == 0
        and (dests * AVG) % LANES == 0
    )


def per_device_kernels(voltages, coefs, block_ids, tile_owner):
    dests = lax.axis_size("ft")
    taps, chan_count = coefs.shape
    radix = chan_count // MXU
    chunk_count = voltages.shape[2] // LANES
    halves = radix // dests
    coef_table = coefs.reshape(taps, MXU, radix).transpose(0, 2, 1)
    table, slot_cap = tile_tables(block_ids, tile_owner)
    arrived = []
    for chunk in range(chunk_count):
        packed = pack(voltages, chunk, dests, radix)
        arrived.append(lax.all_to_all(packed, "ft", split_axis=0, concat_axis=0, tiled=True))
    gathered = [[] for _ in range(halves)]
    for chunk in range(chunk_count):
        for half, part in enumerate(transform_chunk(arrived[chunk], coef_table, radix, dests)):
            turned = lax.all_to_all(part, "ft", split_axis=0, concat_axis=0, tiled=True)
            gathered[half].append(gather_blocks(turned))
    vis = None
    for half in range(halves):
        vis = correlate(table, gathered[half], half, halves, slot_cap, vis)
    return vis


def tile_product(row_part, col_part, norm_scale):
    products = jnp.einsum(
        "pscax,qscay->cpqxy", row_part, col_part, preferred_element_type=jnp.float32
    )
    real_part = products[:, 0, 0] + products[:, 1, 1]
    imag_part = products[:, 1, 0] - products[:, 0, 1]
    return jnp.stack([real_part, imag_part]) * norm_scale


def dft_tables(order_len):
    steps_one = jnp.arange(order_len, dtype=jnp.int32)
    phase_grid = steps_one[:, None] * steps_one[None, :] % order_len
    angles = phase_grid.astype(jnp.float32) * (2.0 * math.pi / order_len)
    return (jnp.cos(angles), jnp.sin(angles))


def transform(filtered):
    per_dev = filtered.shape[1]
    chan_count = filtered.shape[2]
    rows_here = filtered.shape[3]
    outer_len = math.isqrt(chan_count)
    while chan_count % outer_len != 0:
        outer_len = outer_len - 1
    inner_len = chan_count // outer_len
    highest = lax.Precision.HIGHEST
    reshaped = filtered.reshape(2, per_dev, outer_len, inner_len, rows_here)
    real_in = reshaped[0]
    imag_in = reshaped[1]
    cos_outer, sin_outer = dft_tables(outer_len)
    section_re = jnp.einsum("snkb,nm->smkb", real_in, cos_outer, precision=highest) + jnp.einsum(
        "snkb,nm->smkb", imag_in, sin_outer, precision=highest
    )
    section_im = jnp.einsum("snkb,nm->smkb", imag_in, cos_outer, precision=highest) - jnp.einsum(
        "snkb,nm->smkb", real_in, sin_outer, precision=highest
    )
    twiddle_grid = (
        jnp.arange(outer_len, dtype=jnp.int32)[:, None]
        * jnp.arange(inner_len, dtype=jnp.int32)[None, :]
        % chan_count
    )
    twiddle_angles = twiddle_grid.astype(jnp.float32) * (2.0 * math.pi / chan_count)
    cos_twiddle = jnp.cos(twiddle_angles)[None, :, :, None]
    sin_twiddle = jnp.sin(twiddle_angles)[None, :, :, None]
    rot_re = section_re * cos_twiddle + section_im * sin_twiddle
    rot_im = section_im * cos_twiddle - section_re * sin_twiddle
    cos_inner, sin_inner = dft_tables(inner_len)
    final_re = jnp.einsum("smkb,kq->sqmb", rot_re, cos_inner, precision=highest) + jnp.einsum(
        "smkb,kq->sqmb", rot_im, sin_inner, precision=highest
    )
    final_im = jnp.einsum("smkb,kq->sqmb", rot_im, cos_inner, precision=highest) - jnp.einsum(
        "smkb,kq->sqmb", rot_re, sin_inner, precision=highest
    )
    stacked = jnp.stack([final_re, final_im]).reshape(2, per_dev, chan_count, rows_here)
    return (stacked * (1.0 / math.sqrt(chan_count))).astype(jnp.bfloat16)


def apply_taps(window, coef_part, taps_count, out_len):
    filtered = jnp.zeros((2, out_len, window.shape[2], window.shape[3]), jnp.float32)
    for tap_index in range(taps_count):
        filtered = filtered + coef_part[tap_index][None, None, :, None] * window[
            :, tap_index : tap_index + out_len
        ].astype(jnp.float32)
    return filtered


def per_device(voltages, coefs, block_ids, tile_owner):
    taps_count = coefs.shape[0]
    chan_count = coefs.shape[1]
    rows_here = voltages.shape[2]
    per_dev = voltages.shape[1] // chan_count
    volt_blocks = voltages.reshape(2, per_dev, chan_count, rows_here)
    phase_block = lax.all_to_all(volt_blocks, "ft", split_axis=2, concat_axis=1, tiled=True)
    spectra_count = phase_block.shape[1]
    phase_here = phase_block.shape[2]
    coef_part = lax.dynamic_slice_in_dim(coefs, lax.axis_index("ft") * phase_here, phase_here, 1)
    zero_front = jnp.zeros((2, taps_count - 1, phase_here, rows_here), phase_block.dtype)
    long_window = jnp.concatenate([zero_front, phase_block], axis=1)
    phase_filtered = apply_taps(long_window, coef_part, taps_count, spectra_count)
    filtered = lax.all_to_all(phase_filtered, "ft", split_axis=1, concat_axis=2, tiled=True)
    spectra = transform(filtered)
    turned = lax.all_to_all(spectra, "ft", split_axis=2, concat_axis=1, tiled=True)
    spectra_all = turned.shape[1]
    chan_here = turned.shape[2]
    coarse_here = chan_here // AVG
    coarse_view = turned.reshape(2, spectra_all, coarse_here, AVG, rows_here)
    norm_scale = 1.0 / (AVG * spectra_all)
    block_count = lax.axis_size("bl")
    my_index = lax.axis_index("bl")
    tile_count = block_count * (block_count + 1) // 2
    slot_cap = 2 * tile_count // block_count
    row_table = jnp.asarray(
        np.array(
            [
                first_id
                for first_id in range(block_count)
                for second_id in range(first_id, block_count)
            ],
            dtype=np.int32,
        )
    )
    col_table = jnp.asarray(
        np.array(
            [
                second_id
                for first_id in range(block_count)
                for second_id in range(first_id, block_count)
            ],
            dtype=np.int32,
        )
    )
    tile_pos = jnp.arange(tile_count, dtype=jnp.int32)
    same_owner = tile_owner[None, :] == tile_owner[:, None]
    before_mask = tile_pos[None, :] < tile_pos[:, None]
    slot_rank = jnp.sum((same_owner & before_mask).astype(jnp.int32), axis=1)
    labels = jnp.arange(block_count, dtype=jnp.int32)
    shard_of = jnp.sum(jnp.where(block_ids[None, :] == labels[:, None], labels[None, :], 0), axis=1)
    gathered = lax.all_gather(coarse_view[None], "bl", axis=0, tiled=True)
    mine_mask = tile_owner == my_index
    own_count = jnp.sum(mine_mask.astype(jnp.int32))
    slot_steps = jnp.arange(slot_cap, dtype=jnp.int32)
    slot_tile = jnp.sum(
        jnp.where(
            mine_mask[None, :] & (slot_rank[None, :] == slot_steps[:, None]), tile_pos[None, :], 0
        ),
        axis=1,
    )

    def one_tile(slot_pos, result_tiles):
        tile_id = slot_tile[slot_pos]
        row_block = gathered[shard_of[row_table[tile_id]]]
        col_block = gathered[shard_of[col_table[tile_id]]]
        tile = tile_product(row_block, col_block, norm_scale)
        return lax.dynamic_update_slice(result_tiles, tile[:, :, None], (0, 0, slot_pos, 0, 0))

    empty_tiles = jnp.zeros((2, coarse_here, slot_cap, rows_here, rows_here), jnp.float32)
    return lax.fori_loop(0, own_count, one_tile, empty_tiles)


def solution(mesh):
    def correlator(voltages, coefs, block_ids, tile_owner):
        fits = takes_kernels(mesh, voltages, coefs)
        return jax.shard_map(
            per_device_kernels if fits else per_device,
            mesh=mesh,
            in_specs=(P(None, ("grp", "ft"), "bl"), P(), P(), P("grp")),
            out_specs=P(None, ("grp", "ft"), "bl", None, None),
            check_vma=False,
        )(voltages, coefs, block_ids, tile_owner)

    return correlator
```

```python
import functools
import math

import jax
import jax.numpy as jnp
import ml_dtypes
import numpy as np
from jax import lax
from jax.experimental import pallas as pl
from jax.experimental.pallas import tpu as pltpu
from jax.sharding import PartitionSpec as P

AVG = 64
MXU = 256
LANES = 128
ROWS16 = 16
VMEM_BYTES = 48 * 1024 * 1024


def split_bf16(table):
    high = table.astype(ml_dtypes.bfloat16)
    low = (table - high.astype(np.float64)).astype(ml_dtypes.bfloat16)
    return high, low


def matrix_tables(inner_len):
    steps = np.arange(inner_len)
    angles = 2.0 * np.pi * (np.outer(steps, steps) % inner_len) / inner_len
    cos_part, sin_part = np.cos(angles), np.sin(angles)
    return split_bf16(np.block([[cos_part, -sin_part], [sin_part, cos_part]]))


def twiddle_tables(radix, inner_len):
    chan_count = radix * inner_len
    angles = 2.0 * np.pi * np.outer(np.arange(radix), np.arange(inner_len)) / chan_count
    scale = 1.0 / math.sqrt(chan_count)
    return np.stack([np.cos(angles) * scale, np.sin(angles) * scale]).astype(np.float32)


def rotate(real, imag, step, count):
    step = step % count
    if step == 0:
        return real, imag
    if 4 * step == count:
        return imag, -real
    if 2 * step == count:
        return -real, -imag
    if 4 * step == 3 * count:
        return -imag, real
    cos_step = math.cos(2.0 * math.pi * step / count)
    sin_step = math.sin(2.0 * math.pi * step / count)
    if 8 * step == count:
        return cos_step * (real + imag), cos_step * (imag - real)
    return cos_step * real + sin_step * imag, cos_step * imag - sin_step * real


def butterflies(parts):
    count = len(parts)
    if count == 1:
        return parts
    half = count // 2
    sums, diffs = [], []
    for k in range(half):
        (ar, ai), (br, bi) = parts[k], parts[k + half]
        sums.append((ar + br, ai + bi))
        diffs.append(rotate(ar - br, ai - bi, k, count))
    even, odd = butterflies(sums), butterflies(diffs)
    out = []
    for k in range(half):
        out += [even[k], odd[k]]
    return out


def pack_kernel(radix, place_ref, v_ref, *rest):
    o_refs, (wide, turned) = rest[:-2], rest[-2:]
    dests, rows, samples = turned.shape
    inner = samples // radix
    wide[...] = v_ref[0].astype(jnp.float32)
    for phase in range(radix):
        part = wide[pl.ds(phase, inner, stride=radix), :].T.astype(jnp.bfloat16)
        for dest in range(dests):
            turned[dest, :, phase * inner : (phase + 1) * inner] = part[
                dest * rows : (dest + 1) * rows
            ]
    for shift in range(dests):
        o_refs[shift][0] = turned[place_ref[shift]]


def pack(voltages, place, chunk, dests, radix):
    _, samples, _ = voltages.shape
    rows = LANES // dests
    return pl.pallas_call(
        functools.partial(pack_kernel, radix),
        grid_spec=pltpu.PrefetchScalarGridSpec(
            num_scalar_prefetch=1,
            grid=(2,),
            in_specs=[pl.BlockSpec((1, samples, LANES), lambda p, t: (p, 0, chunk))],
            out_specs=[pl.BlockSpec((1, rows, samples), lambda p, t: (p, 0, 0))] * dests,
            scratch_shapes=[
                pltpu.VMEM((samples, LANES), jnp.float32),
                pltpu.VMEM((dests, rows, samples), jnp.bfloat16),
            ],
        ),
        out_shape=[jax.ShapeDtypeStruct((2, rows, samples), jnp.bfloat16)] * dests,
        compiler_params=pltpu.CompilerParams(vmem_limit_bytes=VMEM_BYTES),
        name="pack_inputs",
    )(place, voltages)


def transform_kernel(radix, dests, place_ref, *rest):
    v_refs = rest[:dests]
    c_ref, gh_ref, gl_ref, tw_ref = rest[dests : dests + 4]
    out_refs, (held, split, prod) = rest[dests + 4 : -3], rest[-3:]
    spectra, _, rows, samples = held.shape
    taps = c_ref.shape[0]
    inner = samples // radix
    group = spectra * rows
    for shift in range(dests):
        held[place_ref[dests + shift]] = v_refs[shift][...]

    @pl.loop(0, radix)
    def _(phase):
        lane0 = pl.multiple_of(phase * inner, inner)
        row0 = pl.multiple_of(phase * group, group)
        for part in range(2):
            for sub in range(0, rows, ROWS16):
                blocks = [
                    held[b, part, pl.ds(sub, ROWS16), pl.ds(lane0, inner)].astype(jnp.float32)
                    for b in range(spectra)
                ]
                for s in range(spectra):
                    total = None
                    for b in range(max(0, s - taps + 1), s + 1):
                        term = c_ref[taps - 1 - s + b, pl.ds(phase, 1), :] * blocks[b]
                        total = term if total is None else total + term
                    high = total.astype(jnp.bfloat16)
                    low = (total - high.astype(jnp.float32)).astype(jnp.bfloat16)
                    at = pl.ds(pl.multiple_of(row0 + s * rows + sub, ROWS16), ROWS16)
                    split[at, part * inner : (part + 1) * inner] = high
                    split[at, (2 + part) * inner : (3 + part) * inner] = low

    high = split[:, : 2 * inner]
    prod[...] = (
        jnp.dot(high, gh_ref[...], preferred_element_type=jnp.float32)
        + jnp.dot(high, gl_ref[...], preferred_element_type=jnp.float32)
        + jnp.dot(split[:, 2 * inner :], gh_ref[...], preferred_element_type=jnp.float32)
    )

    halves = len(out_refs)

    @pl.loop(0, spectra)
    def _(s):
        for sub in range(0, rows, ROWS16):
            for lane in range(0, inner, LANES):
                parts = []
                for phase in range(radix):
                    at = pl.ds(pl.multiple_of(phase * group + s * rows + sub, ROWS16), ROWS16)
                    yr = prod[at, lane : lane + LANES]
                    yi = prod[at, inner + lane : inner + lane + LANES]
                    cos_here = tw_ref[0, phase : phase + 1, lane : lane + LANES]
                    sin_here = tw_ref[1, phase : phase + 1, lane : lane + LANES]
                    if phase == 0:
                        parts.append((yr * cos_here, yi * cos_here))
                    else:
                        parts.append(
                            (yr * cos_here + yi * sin_here, yi * cos_here - yr * sin_here)
                        )
                for step, pair in enumerate(butterflies(parts)):
                    for part in range(2):
                        out_refs[step % halves][
                            step // halves, part, s, sub : sub + ROWS16, lane : lane + LANES
                        ] = pair[part].astype(jnp.bfloat16)


def transform_chunk(blocks, place, coef_table, radix):
    dests = len(blocks)
    _, rows, samples = blocks[0].shape
    spectra = dests
    inner = samples // radix
    halves = radix // dests
    g_high, g_low = matrix_tables(inner)
    vmem = pl.BlockSpec(memory_space=pltpu.VMEM)
    total = radix * spectra * rows
    return pl.pallas_call(
        functools.partial(transform_kernel, radix, dests),
        grid_spec=pltpu.PrefetchScalarGridSpec(
            num_scalar_prefetch=1,
            grid=(),
            in_specs=[vmem] * (dests + 4),
            out_specs=[vmem] * halves,
            scratch_shapes=[
                pltpu.VMEM((spectra, 2, rows, samples), jnp.bfloat16),
                pltpu.VMEM((total, 4 * inner), jnp.bfloat16),
                pltpu.VMEM((total, 2 * inner), jnp.float32),
            ],
        ),
        out_shape=[jax.ShapeDtypeStruct((dests, 2, spectra, rows, inner), jnp.bfloat16)]
        * halves,
        cost_estimate=pl.CostEstimate(
            flops=3 * 2 * total * 4 * inner * inner, bytes_accessed=6 << 20, transcendentals=0
        ),
        compiler_params=pltpu.CompilerParams(vmem_limit_bytes=VMEM_BYTES),
        name="filter_transform",
    )(
        place,
        *blocks,
        coef_table,
        jnp.asarray(g_high),
        jnp.asarray(g_low),
        twiddle_tables(radix, inner),
    )


def correlate_kernel(chunks, blocks, scale, table_ref, *rest):
    g_refs, o_ref, left = rest[: chunks * blocks], rest[-2], rest[-1]
    senders, _, spectra, rows, inner = g_refs[0].shape
    slots = o_ref.shape[2]
    coarse = inner // AVG
    side = chunks * senders * rows
    step = pl.program_id(0)

    @pl.when(step == 0)
    def _():
        for chunk in range(chunks):
            for block in range(blocks):
                source = g_refs[chunk * blocks + block]

                @pl.loop(0, senders)
                def _(shift, chunk=chunk, block=block, source=source):
                    sender = shift
                    row = pl.multiple_of((chunk * senders + sender) * rows, rows)
                    for part in range(2):
                        pieces = [source[shift, part, s] for s in range(spectra)]
                        for c in range(coarse):
                            line = jnp.concatenate(
                                [piece[:, c * AVG : (c + 1) * AVG] for piece in pieces], axis=1
                            )
                            width = line.shape[1]
                            left[
                                c, block, pl.ds(row, rows), part * width : (part + 1) * width
                            ] = line
                            left[
                                c,
                                block,
                                pl.ds(pl.multiple_of(side + row, rows), rows),
                                (1 - part) * width : (2 - part) * width,
                            ] = -line if part == 0 else line

    count = table_ref[2 * slots]
    for slot in range(slots):

        @pl.when(slot < count)
        def _(slot=slot):
            rows_of = left[step, table_ref[slot]]
            cols_of = left[step, table_ref[slots + slot], pl.ds(0, side), :]
            tile = (
                lax.dot_general(
                    rows_of,
                    cols_of,
                    (((1,), (1,)), ((), ())),
                    preferred_element_type=jnp.float32,
                )
                * scale
            )
            o_ref[0, 0, slot] = tile[:side]
            o_ref[1, 0, slot] = tile[side:]

        @pl.when(slot >= count)
        def _(slot=slot):
            o_ref[:, 0, slot] = jnp.zeros((2, side, side), jnp.float32)


def correlate(table, gathered, part_index, part_count, slots, vis):
    chunks, blocks = len(gathered), len(gathered[0])
    senders, _, spectra, rows, inner = gathered[0][0].shape
    coarse = inner // AVG
    side = chunks * senders * rows
    scale = 1.0 / (AVG * spectra)
    parts = [block for chunk in gathered for block in chunk]
    in_specs = [
        pl.BlockSpec(part.shape, lambda c, t: (0,) * 5, pipeline_mode=pl.Buffered(1))
        for part in parts
    ]
    args = [table, *parts]
    aliases = {}
    if vis is not None:
        in_specs.append(pl.BlockSpec(memory_space=pl.ANY))
        args.append(vis)
        aliases = {len(args) - 1: 0}
    return pl.pallas_call(
        functools.partial(correlate_kernel, chunks, blocks, scale),
        grid_spec=pltpu.PrefetchScalarGridSpec(
            num_scalar_prefetch=1,
            grid=(coarse,),
            in_specs=in_specs,
            out_specs=pl.BlockSpec(
                (2, 1, slots, side, side), lambda c, t: (0, part_index * coarse + c, 0, 0, 0)
            ),
            scratch_shapes=[
                pltpu.VMEM((coarse, blocks, 2 * side, 2 * spectra * AVG), jnp.bfloat16)
            ],
        ),
        out_shape=jax.ShapeDtypeStruct(
            (2, part_count * coarse, slots, side, side), jnp.float32
        ),
        input_output_aliases=aliases,
        cost_estimate=pl.CostEstimate(
            flops=coarse * slots * 2 * 4 * side * side * spectra * AVG,
            bytes_accessed=16 << 20,
            transcendentals=0,
        ),
        compiler_params=pltpu.CompilerParams(vmem_limit_bytes=VMEM_BYTES),
        name="correlate_tiles",
    )(*args)


def places(count):
    steps = np.arange(count, dtype=np.int32)
    index = lax.axis_index("ft").astype(jnp.int32)
    return jnp.concatenate([(index + steps) % count, (index + count - steps) % count])


def spread(pieces):
    count = len(pieces)
    return [pieces[0]] + [
        lax.ppermute(pieces[d], "ft", [(i, (i + d) % count) for i in range(count)])
        for d in range(1, count)
    ]


def gather_blocks(own):
    count = lax.axis_size("bl")
    held = {0: own}
    bit = count // 2
    while bit:
        for r in list(held):
            held[r ^ bit] = lax.ppermute(held[r], "bl", [(i, i ^ bit) for i in range(count)])
        bit //= 2
    return [held[r] for r in range(count)]


def tile_tables(block_ids, tile_owner, place):
    block_count = lax.axis_size("bl")
    tile_count = block_count * (block_count + 1) // 2
    slot_cap = 2 * tile_count // block_count
    pairs = [(i, j) for i in range(block_count) for j in range(i, block_count)]
    row_table = np.array([i for i, _ in pairs], np.int32)
    col_table = np.array([j for _, j in pairs], np.int32)
    mine = (tile_owner == lax.axis_index("bl")).astype(jnp.int32)
    earlier = np.tril(np.ones((tile_count, tile_count), np.int32), -1)
    rank = jnp.sum(earlier * mine[None, :], axis=1)
    labels = np.arange(block_count, dtype=np.int32)
    shard_of = jnp.sum(jnp.where(block_ids[None, :] == labels[:, None], labels[None, :], 0), axis=1)
    row_shard = jnp.sum(
        jnp.where(row_table[:, None] == labels[None, :], shard_of[None, :], 0), axis=1
    )
    col_shard = jnp.sum(
        jnp.where(col_table[:, None] == labels[None, :], shard_of[None, :], 0), axis=1
    )
    here = (mine[None, :] == 1) & (rank[None, :] == np.arange(slot_cap, dtype=np.int32)[:, None])
    rows = jnp.sum(jnp.where(here, row_shard[None, :], 0), axis=1)
    cols = jnp.sum(jnp.where(here, col_shard[None, :], 0), axis=1)
    index = lax.axis_index("bl")
    table = jnp.concatenate(
        [rows ^ index, cols ^ index, jnp.sum(mine, keepdims=True), place]
    ).astype(jnp.int32)
    return table, slot_cap


def takes_kernels(mesh, voltages, coefs):
    dests = mesh.shape["ft"]
    blocks = mesh.shape["bl"]
    inputs = voltages.shape[2] // mesh.shape["bl"]
    per_dev = voltages.shape[1] // (mesh.shape["grp"] * dests)
    chan_count = coefs.shape[1]
    radix = chan_count // MXU
    return (
        per_dev == chan_count
        and chan_count % MXU == 0
        and radix & (radix - 1) == 0
        and radix % dests == 0
        and radix <= 8
        and blocks & (blocks - 1) == 0
        and inputs % LANES == 0
        and LANES % dests == 0
        and (LANES // dests) % ROWS16 == 0
        and (dests * AVG) % LANES == 0
    )


def per_device_kernels(voltages, coefs, block_ids, tile_owner):
    dests = lax.axis_size("ft")
    taps, chan_count = coefs.shape
    radix = chan_count // MXU
    chunk_count = voltages.shape[2] // LANES
    halves = radix // dests
    coef_table = coefs.reshape(taps, MXU, radix).transpose(0, 2, 1)
    place = places(dests)
    table, slot_cap = tile_tables(block_ids, tile_owner, place)
    arrived = [
        spread(pack(voltages, place, chunk, dests, radix)) for chunk in range(chunk_count)
    ]
    gathered = [[] for _ in range(halves)]
    for chunk in range(chunk_count):
        for half, parts in enumerate(transform_chunk(arrived[chunk], place, coef_table, radix)):
            turned = lax.all_to_all(parts, "ft", split_axis=0, concat_axis=0, tiled=True)
            gathered[half].append(gather_blocks(turned))
    vis = None
    for half in range(halves):
        vis = correlate(table, gathered[half], half, halves, slot_cap, vis)
    return vis


def tile_product(row_part, col_part, norm_scale):
    products = jnp.einsum(
        "pscax,qscay->cpqxy", row_part, col_part, preferred_element_type=jnp.float32
    )
    real_part = products[:, 0, 0] + products[:, 1, 1]
    imag_part = products[:, 1, 0] - products[:, 0, 1]
    return jnp.stack([real_part, imag_part]) * norm_scale


def dft_tables(order_len):
    steps_one = jnp.arange(order_len, dtype=jnp.int32)
    phase_grid = steps_one[:, None] * steps_one[None, :] % order_len
    angles = phase_grid.astype(jnp.float32) * (2.0 * math.pi / order_len)
    return (jnp.cos(angles), jnp.sin(angles))


def transform(filtered):
    per_dev = filtered.shape[1]
    chan_count = filtered.shape[2]
    rows_here = filtered.shape[3]
    outer_len = math.isqrt(chan_count)
    while chan_count % outer_len != 0:
        outer_len = outer_len - 1
    inner_len = chan_count // outer_len
    highest = lax.Precision.HIGHEST
    reshaped = filtered.reshape(2, per_dev, outer_len, inner_len, rows_here)
    real_in = reshaped[0]
    imag_in = reshaped[1]
    cos_outer, sin_outer = dft_tables(outer_len)
    section_re = jnp.einsum("snkb,nm->smkb", real_in, cos_outer, precision=highest) + jnp.einsum(
        "snkb,nm->smkb", imag_in, sin_outer, precision=highest
    )
    section_im = jnp.einsum("snkb,nm->smkb", imag_in, cos_outer, precision=highest) - jnp.einsum(
        "snkb,nm->smkb", real_in, sin_outer, precision=highest
    )
    twiddle_grid = (
        jnp.arange(outer_len, dtype=jnp.int32)[:, None]
        * jnp.arange(inner_len, dtype=jnp.int32)[None, :]
        % chan_count
    )
    twiddle_angles = twiddle_grid.astype(jnp.float32) * (2.0 * math.pi / chan_count)
    cos_twiddle = jnp.cos(twiddle_angles)[None, :, :, None]
    sin_twiddle = jnp.sin(twiddle_angles)[None, :, :, None]
    rot_re = section_re * cos_twiddle + section_im * sin_twiddle
    rot_im = section_im * cos_twiddle - section_re * sin_twiddle
    cos_inner, sin_inner = dft_tables(inner_len)
    final_re = jnp.einsum("smkb,kq->sqmb", rot_re, cos_inner, precision=highest) + jnp.einsum(
        "smkb,kq->sqmb", rot_im, sin_inner, precision=highest
    )
    final_im = jnp.einsum("smkb,kq->sqmb", rot_im, cos_inner, precision=highest) - jnp.einsum(
        "smkb,kq->sqmb", rot_re, sin_inner, precision=highest
    )
    stacked = jnp.stack([final_re, final_im]).reshape(2, per_dev, chan_count, rows_here)
    return (stacked * (1.0 / math.sqrt(chan_count))).astype(jnp.bfloat16)


def apply_taps(window, coef_part, taps_count, out_len):
    filtered = jnp.zeros((2, out_len, window.shape[2], window.shape[3]), jnp.float32)
    for tap_index in range(taps_count):
        filtered = filtered + coef_part[tap_index][None, None, :, None] * window[
            :, tap_index : tap_index + out_len
        ].astype(jnp.float32)
    return filtered


def per_device(voltages, coefs, block_ids, tile_owner):
    taps_count = coefs.shape[0]
    chan_count = coefs.shape[1]
    rows_here = voltages.shape[2]
    per_dev = voltages.shape[1] // chan_count
    volt_blocks = voltages.reshape(2, per_dev, chan_count, rows_here)
    phase_block = lax.all_to_all(volt_blocks, "ft", split_axis=2, concat_axis=1, tiled=True)
    spectra_count = phase_block.shape[1]
    phase_here = phase_block.shape[2]
    coef_part = lax.dynamic_slice_in_dim(coefs, lax.axis_index("ft") * phase_here, phase_here, 1)
    zero_front = jnp.zeros((2, taps_count - 1, phase_here, rows_here), phase_block.dtype)
    long_window = jnp.concatenate([zero_front, phase_block], axis=1)
    phase_filtered = apply_taps(long_window, coef_part, taps_count, spectra_count)
    filtered = lax.all_to_all(phase_filtered, "ft", split_axis=1, concat_axis=2, tiled=True)
    spectra = transform(filtered)
    turned = lax.all_to_all(spectra, "ft", split_axis=2, concat_axis=1, tiled=True)
    spectra_all = turned.shape[1]
    chan_here = turned.shape[2]
    coarse_here = chan_here // AVG
    coarse_view = turned.reshape(2, spectra_all, coarse_here, AVG, rows_here)
    norm_scale = 1.0 / (AVG * spectra_all)
    block_count = lax.axis_size("bl")
    my_index = lax.axis_index("bl")
    tile_count = block_count * (block_count + 1) // 2
    slot_cap = 2 * tile_count // block_count
    row_table = jnp.asarray(
        np.array(
            [
                first_id
                for first_id in range(block_count)
                for second_id in range(first_id, block_count)
            ],
            dtype=np.int32,
        )
    )
    col_table = jnp.asarray(
        np.array(
            [
                second_id
                for first_id in range(block_count)
                for second_id in range(first_id, block_count)
            ],
            dtype=np.int32,
        )
    )
    tile_pos = jnp.arange(tile_count, dtype=jnp.int32)
    same_owner = tile_owner[None, :] == tile_owner[:, None]
    before_mask = tile_pos[None, :] < tile_pos[:, None]
    slot_rank = jnp.sum((same_owner & before_mask).astype(jnp.int32), axis=1)
    labels = jnp.arange(block_count, dtype=jnp.int32)
    shard_of = jnp.sum(jnp.where(block_ids[None, :] == labels[:, None], labels[None, :], 0), axis=1)
    gathered = lax.all_gather(coarse_view[None], "bl", axis=0, tiled=True)
    mine_mask = tile_owner == my_index
    own_count = jnp.sum(mine_mask.astype(jnp.int32))
    slot_steps = jnp.arange(slot_cap, dtype=jnp.int32)
    slot_tile = jnp.sum(
        jnp.where(
            mine_mask[None, :] & (slot_rank[None, :] == slot_steps[:, None]), tile_pos[None, :], 0
        ),
        axis=1,
    )

    def one_tile(slot_pos, result_tiles):
        tile_id = slot_tile[slot_pos]
        row_block = gathered[shard_of[row_table[tile_id]]]
        col_block = gathered[shard_of[col_table[tile_id]]]
        tile = tile_product(row_block, col_block, norm_scale)
        return lax.dynamic_update_slice(result_tiles, tile[:, :, None], (0, 0, slot_pos, 0, 0))

    empty_tiles = jnp.zeros((2, coarse_here, slot_cap, rows_here, rows_here), jnp.float32)
    return lax.fori_loop(0, own_count, one_tile, empty_tiles)


def solution(mesh):
    def correlator(voltages, coefs, block_ids, tile_owner):
        fits = takes_kernels(mesh, voltages, coefs)
        return jax.shard_map(
            per_device_kernels if fits else per_device,
            mesh=mesh,
            in_specs=(P(None, ("grp", "ft"), "bl"), P(), P(), P("grp")),
            out_specs=P(None, ("grp", "ft"), "bl", None, None),
            check_vma=False,
        )(voltages, coefs, block_ids, tile_owner)

    return correlator
```

```python
import functools
import math

import jax
import jax.numpy as jnp
import ml_dtypes
import numpy as np
from jax import lax
from jax.experimental import pallas as pl
from jax.experimental.pallas import tpu as pltpu
from jax.sharding import PartitionSpec as P

AVG = 64
MXU = 256
LANES = 128
ROWS16 = 16
VMEM_BYTES = 48 * 1024 * 1024


def split_bf16(table):
    high = table.astype(ml_dtypes.bfloat16)
    low = (table - high.astype(np.float64)).astype(ml_dtypes.bfloat16)
    return high, low


def matrix_tables(inner_len):
    steps = np.arange(inner_len)
    angles = 2.0 * np.pi * (np.outer(steps, steps) % inner_len) / inner_len
    cos_part, sin_part = np.cos(angles), np.sin(angles)
    return split_bf16(np.block([[cos_part, -sin_part], [sin_part, cos_part]]))


def twiddle_tables(radix, inner_len):
    chan_count = radix * inner_len
    angles = 2.0 * np.pi * np.outer(np.arange(radix), np.arange(inner_len)) / chan_count
    scale = 1.0 / math.sqrt(chan_count)
    return np.stack([np.cos(angles) * scale, np.sin(angles) * scale]).astype(np.float32)


def rotate(real, imag, step, count):
    step = step % count
    if step == 0:
        return real, imag
    if 4 * step == count:
        return imag, -real
    if 2 * step == count:
        return -real, -imag
    if 4 * step == 3 * count:
        return -imag, real
    cos_step = math.cos(2.0 * math.pi * step / count)
    sin_step = math.sin(2.0 * math.pi * step / count)
    if 8 * step == count:
        return cos_step * (real + imag), cos_step * (imag - real)
    return cos_step * real + sin_step * imag, cos_step * imag - sin_step * real


def butterflies(parts):
    count = len(parts)
    if count == 1:
        return parts
    half = count // 2
    sums, diffs = [], []
    for k in range(half):
        (ar, ai), (br, bi) = parts[k], parts[k + half]
        sums.append((ar + br, ai + bi))
        diffs.append(rotate(ar - br, ai - bi, k, count))
    even, odd = butterflies(sums), butterflies(diffs)
    out = []
    for k in range(half):
        out += [even[k], odd[k]]
    return out


def pack_kernel(radix, place_ref, v_ref, *rest):
    o_refs, (wide, turned) = rest[:-2], rest[-2:]
    dests, rows, samples = turned.shape
    inner = samples // radix
    wide[...] = v_ref[0].astype(jnp.float32)
    for phase in range(radix):
        part = wide[pl.ds(phase, inner, stride=radix), :].T.astype(jnp.bfloat16)
        for dest in range(dests):
            turned[dest, :, phase * inner : (phase + 1) * inner] = part[
                dest * rows : (dest + 1) * rows
            ]
    for shift in range(dests):
        o_refs[shift][0] = turned[place_ref[shift]]


def pack(voltages, place, chunk, dests, radix):
    _, samples, _ = voltages.shape
    rows = LANES // dests
    return pl.pallas_call(
        functools.partial(pack_kernel, radix),
        grid_spec=pltpu.PrefetchScalarGridSpec(
            num_scalar_prefetch=1,
            grid=(2,),
            in_specs=[pl.BlockSpec((1, samples, LANES), lambda p, t: (p, 0, chunk))],
            out_specs=[pl.BlockSpec((1, rows, samples), lambda p, t: (p, 0, 0))] * dests,
            scratch_shapes=[
                pltpu.VMEM((samples, LANES), jnp.float32),
                pltpu.VMEM((dests, rows, samples), jnp.bfloat16),
            ],
        ),
        out_shape=[jax.ShapeDtypeStruct((2, rows, samples), jnp.bfloat16)] * dests,
        compiler_params=pltpu.CompilerParams(vmem_limit_bytes=VMEM_BYTES),
        name="pack_inputs",
    )(place, voltages)


def transform_kernel(radix, dests, place_ref, *rest):
    v_refs = rest[:dests]
    c_ref, gh_ref, gl_ref, tw_ref = rest[dests : dests + 4]
    out_refs, (held, split, prod, made) = rest[dests + 4 : -4], rest[-4:]
    spectra, _, rows, samples = held.shape
    taps = c_ref.shape[0]
    inner = samples // radix
    group = spectra * rows
    for shift in range(dests):
        held[place_ref[dests + shift]] = v_refs[shift][...]

    @pl.loop(0, radix)
    def _(phase):
        lane0 = pl.multiple_of(phase * inner, inner)
        row0 = pl.multiple_of(phase * group, group)
        for part in range(2):
            for sub in range(0, rows, ROWS16):
                blocks = [
                    held[b, part, pl.ds(sub, ROWS16), pl.ds(lane0, inner)].astype(jnp.float32)
                    for b in range(spectra)
                ]
                for s in range(spectra):
                    total = None
                    for b in range(max(0, s - taps + 1), s + 1):
                        term = c_ref[taps - 1 - s + b, pl.ds(phase, 1), :] * blocks[b]
                        total = term if total is None else total + term
                    high = total.astype(jnp.bfloat16)
                    low = (total - high.astype(jnp.float32)).astype(jnp.bfloat16)
                    at = pl.ds(pl.multiple_of(row0 + s * rows + sub, ROWS16), ROWS16)
                    split[at, part * inner : (part + 1) * inner] = high
                    split[at, (2 + part) * inner : (3 + part) * inner] = low

    high = split[:, : 2 * inner]
    prod[...] = (
        jnp.dot(high, gh_ref[...], preferred_element_type=jnp.float32)
        + jnp.dot(high, gl_ref[...], preferred_element_type=jnp.float32)
        + jnp.dot(split[:, 2 * inner :], gh_ref[...], preferred_element_type=jnp.float32)
    )

    halves = made.shape[1]

    @pl.loop(0, spectra)
    def _(s):
        for sub in range(0, rows, ROWS16):
            for lane in range(0, inner, LANES):
                parts = []
                for phase in range(radix):
                    at = pl.ds(pl.multiple_of(phase * group + s * rows + sub, ROWS16), ROWS16)
                    yr = prod[at, lane : lane + LANES]
                    yi = prod[at, inner + lane : inner + lane + LANES]
                    cos_here = tw_ref[0, phase : phase + 1, lane : lane + LANES]
                    sin_here = tw_ref[1, phase : phase + 1, lane : lane + LANES]
                    if phase == 0:
                        parts.append((yr * cos_here, yi * cos_here))
                    else:
                        parts.append(
                            (yr * cos_here + yi * sin_here, yi * cos_here - yr * sin_here)
                        )
                for step, pair in enumerate(butterflies(parts)):
                    for part in range(2):
                        made[
                            step // halves,
                            step % halves,
                            part,
                            s,
                            sub : sub + ROWS16,
                            lane : lane + LANES,
                        ] = pair[part].astype(jnp.bfloat16)

    for shift in range(dests):
        first = 0
        for out in out_refs[shift::dests]:
            some = out.shape[0]
            out[...] = made[place_ref[shift], first : first + some]
            first += some


def transform_chunk(blocks, place, coef_table, radix, cuts):
    dests = len(blocks)
    _, rows, samples = blocks[0].shape
    spectra = dests
    inner = samples // radix
    halves = radix // dests
    g_high, g_low = matrix_tables(inner)
    vmem = pl.BlockSpec(memory_space=pltpu.VMEM)
    total = radix * spectra * rows
    made = pl.pallas_call(
        functools.partial(transform_kernel, radix, dests),
        grid_spec=pltpu.PrefetchScalarGridSpec(
            num_scalar_prefetch=1,
            grid=(),
            in_specs=[vmem] * (dests + 4),
            out_specs=[vmem] * (len(cuts) * dests),
            scratch_shapes=[
                pltpu.VMEM((spectra, 2, rows, samples), jnp.bfloat16),
                pltpu.VMEM((total, 4 * inner), jnp.bfloat16),
                pltpu.VMEM((total, 2 * inner), jnp.float32),
                pltpu.VMEM((dests, halves, 2, spectra, rows, inner), jnp.bfloat16),
            ],
        ),
        out_shape=[
            jax.ShapeDtypeStruct((some, 2, spectra, rows, inner), jnp.bfloat16)
            for some in cuts
            for _ in range(dests)
        ],
        cost_estimate=pl.CostEstimate(
            flops=3 * 2 * total * 4 * inner * inner, bytes_accessed=6 << 20, transcendentals=0
        ),
        compiler_params=pltpu.CompilerParams(vmem_limit_bytes=VMEM_BYTES),
        name="filter_transform",
    )(
        place,
        *blocks,
        coef_table,
        jnp.asarray(g_high),
        jnp.asarray(g_low),
        twiddle_tables(radix, inner),
    )
    return [made[cut * dests : (cut + 1) * dests] for cut in range(len(cuts))]


def join_kernel(place_ref, *rest):
    for shift, piece in enumerate(rest[:-1]):
        rest[-1][place_ref[len(rest) - 1 + shift]] = piece[...]


def join(pieces, place):
    vmem = pl.BlockSpec(memory_space=pltpu.VMEM)
    return pl.pallas_call(
        join_kernel,
        grid_spec=pltpu.PrefetchScalarGridSpec(
            num_scalar_prefetch=1, grid=(), in_specs=[vmem] * len(pieces), out_specs=vmem
        ),
        out_shape=jax.ShapeDtypeStruct((len(pieces), *pieces[0].shape), pieces[0].dtype),
        compiler_params=pltpu.CompilerParams(vmem_limit_bytes=VMEM_BYTES // 4),
        name="join_pieces",
    )(place, *pieces)


def correlate_kernel(chunks, blocks, scale, table_ref, *rest):
    g_refs, o_ref, left = rest[: chunks * blocks], rest[-2], rest[-1]
    senders, _, _, spectra, rows, inner = g_refs[0].shape
    slots = o_ref.shape[2]
    coarse = inner // AVG
    side = chunks * senders * rows
    step = pl.program_id(0)

    @pl.when(step == 0)
    def _():
        for chunk in range(chunks):
            for block in range(blocks):
                source = g_refs[chunk * blocks + block]

                @pl.loop(0, senders)
                def _(sender, chunk=chunk, block=block, source=source):
                    row = pl.multiple_of((chunk * senders + sender) * rows, rows)
                    for part in range(2):
                        pieces = [source[sender, 0, part, s] for s in range(spectra)]
                        for c in range(coarse):
                            line = jnp.concatenate(
                                [piece[:, c * AVG : (c + 1) * AVG] for piece in pieces], axis=1
                            )
                            width = line.shape[1]
                            left[
                                c, block, pl.ds(row, rows), part * width : (part + 1) * width
                            ] = line
                            left[
                                c,
                                block,
                                pl.ds(pl.multiple_of(side + row, rows), rows),
                                (1 - part) * width : (2 - part) * width,
                            ] = -line if part == 0 else line

    count = table_ref[2 * slots]
    for slot in range(slots):

        @pl.when(slot < count)
        def _(slot=slot):
            rows_of = left[step, table_ref[slot]]
            cols_of = left[step, table_ref[slots + slot], pl.ds(0, side), :]
            tile = (
                lax.dot_general(
                    rows_of,
                    cols_of,
                    (((1,), (1,)), ((), ())),
                    preferred_element_type=jnp.float32,
                )
                * scale
            )
            o_ref[0, 0, slot] = tile[:side]
            o_ref[1, 0, slot] = tile[side:]

        @pl.when(slot >= count)
        def _(slot=slot):
            o_ref[:, 0, slot] = jnp.zeros((2, side, side), jnp.float32)


def correlate(table, gathered, part_index, part_count, slots, vis):
    chunks, blocks = len(gathered), len(gathered[0][1])
    senders, _, _, spectra, rows, inner = gathered[0][1][0].shape
    coarse = inner // AVG
    side = chunks * senders * rows
    scale = 1.0 / (AVG * spectra)
    parts = [block for _, chunk in gathered for block in chunk]
    in_specs = [
        pl.BlockSpec(
            (senders, 1, 2, spectra, rows, inner),
            lambda c, t, at=at: (0, at, 0, 0, 0, 0),
            pipeline_mode=pl.Buffered(1),
        )
        for at, chunk in gathered
        for _ in chunk
    ]
    args = [table, *parts]
    aliases = {}
    if vis is not None:
        in_specs.append(pl.BlockSpec(memory_space=pl.ANY))
        args.append(vis)
        aliases = {len(args) - 1: 0}
    return pl.pallas_call(
        functools.partial(correlate_kernel, chunks, blocks, scale),
        grid_spec=pltpu.PrefetchScalarGridSpec(
            num_scalar_prefetch=1,
            grid=(coarse,),
            in_specs=in_specs,
            out_specs=pl.BlockSpec(
                (2, 1, slots, side, side), lambda c, t: (0, part_index * coarse + c, 0, 0, 0)
            ),
            scratch_shapes=[
                pltpu.VMEM((coarse, blocks, 2 * side, 2 * spectra * AVG), jnp.bfloat16)
            ],
        ),
        out_shape=jax.ShapeDtypeStruct(
            (2, part_count * coarse, slots, side, side), jnp.float32
        ),
        input_output_aliases=aliases,
        cost_estimate=pl.CostEstimate(
            flops=coarse * slots * 2 * 4 * side * side * spectra * AVG,
            bytes_accessed=16 << 20,
            transcendentals=0,
        ),
        compiler_params=pltpu.CompilerParams(vmem_limit_bytes=VMEM_BYTES),
        name="correlate_tiles",
    )(*args)


def places(count):
    steps = np.arange(count, dtype=np.int32)
    index = lax.axis_index("ft").astype(jnp.int32)
    return jnp.concatenate([(index + steps) % count, (index + count - steps) % count])


def spread(pieces):
    count = len(pieces)
    return [pieces[0]] + [
        lax.ppermute(pieces[d], "ft", [(i, (i + d) % count) for i in range(count)])
        for d in range(1, count)
    ]


def gather_blocks(own):
    count = lax.axis_size("bl")
    held = {0: own}
    bit = count // 2
    while bit:
        for r in list(held):
            held[r ^ bit] = lax.ppermute(held[r], "bl", [(i, i ^ bit) for i in range(count)])
        bit //= 2
    return [held[r] for r in range(count)]


def tile_tables(block_ids, tile_owner):
    block_count = lax.axis_size("bl")
    tile_count = block_count * (block_count + 1) // 2
    slot_cap = 2 * tile_count // block_count
    pairs = [(i, j) for i in range(block_count) for j in range(i, block_count)]
    row_table = np.array([i for i, _ in pairs], np.int32)
    col_table = np.array([j for _, j in pairs], np.int32)
    mine = (tile_owner == lax.axis_index("bl")).astype(jnp.int32)
    earlier = np.tril(np.ones((tile_count, tile_count), np.int32), -1)
    rank = jnp.sum(earlier * mine[None, :], axis=1)
    labels = np.arange(block_count, dtype=np.int32)
    shard_of = jnp.sum(jnp.where(block_ids[None, :] == labels[:, None], labels[None, :], 0), axis=1)
    row_shard = jnp.sum(
        jnp.where(row_table[:, None] == labels[None, :], shard_of[None, :], 0), axis=1
    )
    col_shard = jnp.sum(
        jnp.where(col_table[:, None] == labels[None, :], shard_of[None, :], 0), axis=1
    )
    here = (mine[None, :] == 1) & (rank[None, :] == np.arange(slot_cap, dtype=np.int32)[:, None])
    rows = jnp.sum(jnp.where(here, row_shard[None, :], 0), axis=1)
    cols = jnp.sum(jnp.where(here, col_shard[None, :], 0), axis=1)
    index = lax.axis_index("bl")
    table = jnp.concatenate(
        [rows ^ index, cols ^ index, jnp.sum(mine, keepdims=True)]
    ).astype(jnp.int32)
    return table, slot_cap


def takes_kernels(mesh, voltages, coefs):
    dests = mesh.shape["ft"]
    blocks = mesh.shape["bl"]
    inputs = voltages.shape[2] // mesh.shape["bl"]
    per_dev = voltages.shape[1] // (mesh.shape["grp"] * dests)
    chan_count = coefs.shape[1]
    radix = chan_count // MXU
    return (
        per_dev == chan_count
        and chan_count % MXU == 0
        and radix & (radix - 1) == 0
        and radix % dests == 0
        and radix <= 8
        and blocks & (blocks - 1) == 0
        and inputs % LANES == 0
        and LANES % dests == 0
        and (LANES // dests) % ROWS16 == 0
        and (dests * AVG) % LANES == 0
    )


def per_device_kernels(voltages, coefs, block_ids, tile_owner):
    dests = lax.axis_size("ft")
    taps, chan_count = coefs.shape
    radix = chan_count // MXU
    chunk_count = voltages.shape[2] // LANES
    halves = radix // dests
    coef_table = coefs.reshape(taps, MXU, radix).transpose(0, 2, 1)
    place = places(dests)
    table, slot_cap = tile_tables(block_ids, tile_owner)
    arrived = [
        spread(pack(voltages, place, chunk, dests, radix)) for chunk in range(chunk_count)
    ]
    gathered = [[] for _ in range(halves)]
    for chunk in range(chunk_count):
        last = chunk == chunk_count - 1
        cuts = (1,) * halves if last else (halves,)
        half = 0
        for some, parts in zip(
            cuts, transform_chunk(arrived[chunk], place, coef_table, radix, cuts)
        ):
            blocks = gather_blocks(join(spread(parts), place))
            for at in range(some):
                gathered[half].append((at, blocks))
                half += 1
    vis = None
    for half in range(halves):
        vis = correlate(table, gathered[half], half, halves, slot_cap, vis)
    return vis


def tile_product(row_part, col_part, norm_scale):
    products = jnp.einsum(
        "pscax,qscay->cpqxy", row_part, col_part, preferred_element_type=jnp.float32
    )
    real_part = products[:, 0, 0] + products[:, 1, 1]
    imag_part = products[:, 1, 0] - products[:, 0, 1]
    return jnp.stack([real_part, imag_part]) * norm_scale


def dft_tables(order_len):
    steps_one = jnp.arange(order_len, dtype=jnp.int32)
    phase_grid = steps_one[:, None] * steps_one[None, :] % order_len
    angles = phase_grid.astype(jnp.float32) * (2.0 * math.pi / order_len)
    return (jnp.cos(angles), jnp.sin(angles))


def transform(filtered):
    per_dev = filtered.shape[1]
    chan_count = filtered.shape[2]
    rows_here = filtered.shape[3]
    outer_len = math.isqrt(chan_count)
    while chan_count % outer_len != 0:
        outer_len = outer_len - 1
    inner_len = chan_count // outer_len
    highest = lax.Precision.HIGHEST
    reshaped = filtered.reshape(2, per_dev, outer_len, inner_len, rows_here)
    real_in = reshaped[0]
    imag_in = reshaped[1]
    cos_outer, sin_outer = dft_tables(outer_len)
    section_re = jnp.einsum("snkb,nm->smkb", real_in, cos_outer, precision=highest) + jnp.einsum(
        "snkb,nm->smkb", imag_in, sin_outer, precision=highest
    )
    section_im = jnp.einsum("snkb,nm->smkb", imag_in, cos_outer, precision=highest) - jnp.einsum(
        "snkb,nm->smkb", real_in, sin_outer, precision=highest
    )
    twiddle_grid = (
        jnp.arange(outer_len, dtype=jnp.int32)[:, None]
        * jnp.arange(inner_len, dtype=jnp.int32)[None, :]
        % chan_count
    )
    twiddle_angles = twiddle_grid.astype(jnp.float32) * (2.0 * math.pi / chan_count)
    cos_twiddle = jnp.cos(twiddle_angles)[None, :, :, None]
    sin_twiddle = jnp.sin(twiddle_angles)[None, :, :, None]
    rot_re = section_re * cos_twiddle + section_im * sin_twiddle
    rot_im = section_im * cos_twiddle - section_re * sin_twiddle
    cos_inner, sin_inner = dft_tables(inner_len)
    final_re = jnp.einsum("smkb,kq->sqmb", rot_re, cos_inner, precision=highest) + jnp.einsum(
        "smkb,kq->sqmb", rot_im, sin_inner, precision=highest
    )
    final_im = jnp.einsum("smkb,kq->sqmb", rot_im, cos_inner, precision=highest) - jnp.einsum(
        "smkb,kq->sqmb", rot_re, sin_inner, precision=highest
    )
    stacked = jnp.stack([final_re, final_im]).reshape(2, per_dev, chan_count, rows_here)
    return (stacked * (1.0 / math.sqrt(chan_count))).astype(jnp.bfloat16)


def apply_taps(window, coef_part, taps_count, out_len):
    filtered = jnp.zeros((2, out_len, window.shape[2], window.shape[3]), jnp.float32)
    for tap_index in range(taps_count):
        filtered = filtered + coef_part[tap_index][None, None, :, None] * window[
            :, tap_index : tap_index + out_len
        ].astype(jnp.float32)
    return filtered


def per_device(voltages, coefs, block_ids, tile_owner):
    taps_count = coefs.shape[0]
    chan_count = coefs.shape[1]
    rows_here = voltages.shape[2]
    per_dev = voltages.shape[1] // chan_count
    volt_blocks = voltages.reshape(2, per_dev, chan_count, rows_here)
    phase_block = lax.all_to_all(volt_blocks, "ft", split_axis=2, concat_axis=1, tiled=True)
    spectra_count = phase_block.shape[1]
    phase_here = phase_block.shape[2]
    coef_part = lax.dynamic_slice_in_dim(coefs, lax.axis_index("ft") * phase_here, phase_here, 1)
    zero_front = jnp.zeros((2, taps_count - 1, phase_here, rows_here), phase_block.dtype)
    long_window = jnp.concatenate([zero_front, phase_block], axis=1)
    phase_filtered = apply_taps(long_window, coef_part, taps_count, spectra_count)
    filtered = lax.all_to_all(phase_filtered, "ft", split_axis=1, concat_axis=2, tiled=True)
    spectra = transform(filtered)
    turned = lax.all_to_all(spectra, "ft", split_axis=2, concat_axis=1, tiled=True)
    spectra_all = turned.shape[1]
    chan_here = turned.shape[2]
    coarse_here = chan_here // AVG
    coarse_view = turned.reshape(2, spectra_all, coarse_here, AVG, rows_here)
    norm_scale = 1.0 / (AVG * spectra_all)
    block_count = lax.axis_size("bl")
    my_index = lax.axis_index("bl")
    tile_count = block_count * (block_count + 1) // 2
    slot_cap = 2 * tile_count // block_count
    row_table = jnp.asarray(
        np.array(
            [
                first_id
                for first_id in range(block_count)
                for second_id in range(first_id, block_count)
            ],
            dtype=np.int32,
        )
    )
    col_table = jnp.asarray(
        np.array(
            [
                second_id
                for first_id in range(block_count)
                for second_id in range(first_id, block_count)
            ],
            dtype=np.int32,
        )
    )
    tile_pos = jnp.arange(tile_count, dtype=jnp.int32)
    same_owner = tile_owner[None, :] == tile_owner[:, None]
    before_mask = tile_pos[None, :] < tile_pos[:, None]
    slot_rank = jnp.sum((same_owner & before_mask).astype(jnp.int32), axis=1)
    labels = jnp.arange(block_count, dtype=jnp.int32)
    shard_of = jnp.sum(jnp.where(block_ids[None, :] == labels[:, None], labels[None, :], 0), axis=1)
    gathered = lax.all_gather(coarse_view[None], "bl", axis=0, tiled=True)
    mine_mask = tile_owner == my_index
    own_count = jnp.sum(mine_mask.astype(jnp.int32))
    slot_steps = jnp.arange(slot_cap, dtype=jnp.int32)
    slot_tile = jnp.sum(
        jnp.where(
            mine_mask[None, :] & (slot_rank[None, :] == slot_steps[:, None]), tile_pos[None, :], 0
        ),
        axis=1,
    )

    def one_tile(slot_pos, result_tiles):
        tile_id = slot_tile[slot_pos]
        row_block = gathered[shard_of[row_table[tile_id]]]
        col_block = gathered[shard_of[col_table[tile_id]]]
        tile = tile_product(row_block, col_block, norm_scale)
        return lax.dynamic_update_slice(result_tiles, tile[:, :, None], (0, 0, slot_pos, 0, 0))

    empty_tiles = jnp.zeros((2, coarse_here, slot_cap, rows_here, rows_here), jnp.float32)
    return lax.fori_loop(0, own_count, one_tile, empty_tiles)


def solution(mesh):
    def correlator(voltages, coefs, block_ids, tile_owner):
        fits = takes_kernels(mesh, voltages, coefs)
        return jax.shard_map(
            per_device_kernels if fits else per_device,
            mesh=mesh,
            in_specs=(P(None, ("grp", "ft"), "bl"), P(), P(), P("grp")),
            out_specs=P(None, ("grp", "ft"), "bl", None, None),
            check_vma=False,
        )(voltages, coefs, block_ids, tile_owner)

    return correlator
```

```python
import functools
import math

import jax
import jax.numpy as jnp
import ml_dtypes
import numpy as np
from jax import lax
from jax.experimental import pallas as pl
from jax.experimental.pallas import tpu as pltpu
from jax.sharding import PartitionSpec as P

AVG = 64
MXU = 256
LANES = 128
ROWS16 = 16
VMEM_BYTES = 48 * 1024 * 1024


def split_bf16(table):
    high = table.astype(ml_dtypes.bfloat16)
    low = (table - high.astype(np.float64)).astype(ml_dtypes.bfloat16)
    return high, low


def matrix_tables(inner_len):
    steps = np.arange(inner_len)
    angles = 2.0 * np.pi * (np.outer(steps, steps) % inner_len) / inner_len
    cos_part, sin_part = np.cos(angles), np.sin(angles)
    return split_bf16(np.block([[cos_part, -sin_part], [sin_part, cos_part]]))


def twiddle_tables(radix, inner_len):
    chan_count = radix * inner_len
    angles = 2.0 * np.pi * np.outer(np.arange(radix), np.arange(inner_len)) / chan_count
    scale = 1.0 / math.sqrt(chan_count)
    return np.stack([np.cos(angles) * scale, np.sin(angles) * scale]).astype(np.float32)


def rotate(real, imag, step, count):
    step = step % count
    if step == 0:
        return real, imag
    if 4 * step == count:
        return imag, -real
    if 2 * step == count:
        return -real, -imag
    if 4 * step == 3 * count:
        return -imag, real
    cos_step = math.cos(2.0 * math.pi * step / count)
    sin_step = math.sin(2.0 * math.pi * step / count)
    if 8 * step == count:
        return cos_step * (real + imag), cos_step * (imag - real)
    return cos_step * real + sin_step * imag, cos_step * imag - sin_step * real


def butterflies(parts):
    count = len(parts)
    if count == 1:
        return parts
    half = count // 2
    sums, diffs = [], []
    for k in range(half):
        (ar, ai), (br, bi) = parts[k], parts[k + half]
        sums.append((ar + br, ai + bi))
        diffs.append(rotate(ar - br, ai - bi, k, count))
    even, odd = butterflies(sums), butterflies(diffs)
    out = []
    for k in range(half):
        out += [even[k], odd[k]]
    return out


def pack_kernel(radix, place_ref, v_ref, *rest):
    o_refs, (wide, turned) = rest[:-2], rest[-2:]
    dests, rows, samples = turned.shape
    inner = samples // radix
    wide[...] = v_ref[0].astype(jnp.float32)
    for phase in range(radix):
        part = wide[pl.ds(phase, inner, stride=radix), :].T.astype(jnp.bfloat16)
        for dest in range(dests):
            turned[dest, :, phase * inner : (phase + 1) * inner] = part[
                dest * rows : (dest + 1) * rows
            ]
    for shift in range(dests):
        o_refs[shift][0] = turned[place_ref[shift]]


def pack(voltages, place, dests, radix):
    _, samples, inputs = voltages.shape
    chunks = inputs // LANES
    rows = LANES // dests
    return pl.pallas_call(
        functools.partial(pack_kernel, radix),
        grid_spec=pltpu.PrefetchScalarGridSpec(
            num_scalar_prefetch=1,
            grid=(2, chunks),
            in_specs=[pl.BlockSpec((1, samples, LANES), lambda p, h, t: (p, 0, h))],
            out_specs=[pl.BlockSpec((1, rows, samples), lambda p, h, t: (p, h, 0))] * dests,
            scratch_shapes=[
                pltpu.VMEM((samples, LANES), jnp.float32),
                pltpu.VMEM((dests, rows, samples), jnp.bfloat16),
            ],
        ),
        out_shape=[jax.ShapeDtypeStruct((2, chunks * rows, samples), jnp.bfloat16)] * dests,
        compiler_params=pltpu.CompilerParams(vmem_limit_bytes=VMEM_BYTES),
        name="pack_inputs",
    )(place, voltages)


def transform_kernel(radix, dests, units, place_ref, *rest):
    v_refs = rest[:dests]
    c_ref, tw_ref, gh_any, gl_any = rest[dests : dests + 4]
    out_refs = rest[dests + 5 : -8]
    held, split, prod, made, gh_ref, gl_ref, sem_h, sem_l = rest[-8:]
    spectra, _, rows, samples = held.shape
    taps = c_ref.shape[0]
    inner = samples // radix
    group = spectra * rows
    fetch_h = pltpu.make_async_copy(gh_any, gh_ref, sem_h)
    fetch_l = pltpu.make_async_copy(gl_any, gl_ref, sem_l)
    fetch_h.start()
    fetch_l.start()
    for shift in range(dests):
        held[place_ref[dests + shift]] = v_refs[shift][...]

    @pl.loop(0, radix)
    def _(phase):
        lane0 = pl.multiple_of(phase * inner, inner)
        row0 = pl.multiple_of(phase * group, group)
        for part in range(2):
            for sub in range(0, rows, ROWS16):
                blocks = [
                    held[b, part, pl.ds(sub, ROWS16), pl.ds(lane0, inner)].astype(jnp.float32)
                    for b in range(spectra)
                ]
                for s in range(spectra):
                    total = None
                    for b in range(max(0, s - taps + 1), s + 1):
                        term = c_ref[taps - 1 - s + b, pl.ds(phase, 1), :] * blocks[b]
                        total = term if total is None else total + term
                    high = total.astype(jnp.bfloat16)
                    low = (total - high.astype(jnp.float32)).astype(jnp.bfloat16)
                    at = pl.ds(pl.multiple_of(row0 + s * rows + sub, ROWS16), ROWS16)
                    split[at, part * inner : (part + 1) * inner] = high
                    split[at, (2 + part) * inner : (3 + part) * inner] = low

    fetch_h.wait()
    fetch_l.wait()

    @pl.loop(0, radix // 2)
    def _(pair):
        at = pl.ds(pl.multiple_of(pair * 2 * group, 2 * group), 2 * group)
        high = split[at, : 2 * inner]
        low = split[at, 2 * inner :]
        prod[at, :] = (
            jnp.dot(high, gh_ref[...], preferred_element_type=jnp.float32)
            + jnp.dot(high, gl_ref[...], preferred_element_type=jnp.float32)
            + jnp.dot(low, gh_ref[...], preferred_element_type=jnp.float32)
        )

    halves = radix // dests
    lane_cuts = inner // LANES

    @pl.loop(0, spectra)
    def _(s):
        for sub in range(0, rows, ROWS16):
            for cut in range(lane_cuts):
                lane = cut * LANES
                parts = []
                for phase in range(radix):
                    at = pl.ds(pl.multiple_of(phase * group + s * rows + sub, ROWS16), ROWS16)
                    yr = prod[at, lane : lane + LANES]
                    yi = prod[at, inner + lane : inner + lane + LANES]
                    cos_here = tw_ref[0, phase : phase + 1, lane : lane + LANES]
                    sin_here = tw_ref[1, phase : phase + 1, lane : lane + LANES]
                    if phase == 0:
                        parts.append((yr * cos_here, yi * cos_here))
                    else:
                        parts.append(
                            (yr * cos_here + yi * sin_here, yi * cos_here - yr * sin_here)
                        )
                for step, pair in enumerate(butterflies(parts)):
                    unit = step % halves * lane_cuts + cut
                    for part in range(2):
                        made[step // halves, unit, part, s, sub : sub + ROWS16, :] = pair[
                            part
                        ].astype(jnp.bfloat16)

    for shift in range(dests):
        for unit in range(units):
            out_refs[unit * dests + shift][...] = made[place_ref[shift], unit]


def transform_all(blocks, place, coef_table, radix, after):
    dests = len(blocks)
    _, rows, samples = blocks[0].shape
    spectra = dests
    inner = samples // radix
    units = samples // dests // LANES
    g_high, g_low = matrix_tables(inner)
    anywhere = pl.BlockSpec(memory_space=pl.ANY)
    vmem = pl.BlockSpec(memory_space=pltpu.VMEM)
    total = radix * spectra * rows
    made = pl.pallas_call(
        functools.partial(transform_kernel, radix, dests, units),
        grid_spec=pltpu.PrefetchScalarGridSpec(
            num_scalar_prefetch=1,
            grid=(),
            in_specs=[vmem] * (dests + 2) + [anywhere] * 3,
            out_specs=[vmem] * (units * dests),
            scratch_shapes=[
                pltpu.VMEM((spectra, 2, rows, samples), jnp.bfloat16),
                pltpu.VMEM((total, 4 * inner), jnp.bfloat16),
                pltpu.VMEM((total, 2 * inner), jnp.float32),
                pltpu.VMEM((dests, units, 2, spectra, rows, LANES), jnp.bfloat16),
                pltpu.VMEM((2 * inner, 2 * inner), jnp.bfloat16),
                pltpu.VMEM((2 * inner, 2 * inner), jnp.bfloat16),
                pltpu.SemaphoreType.DMA,
                pltpu.SemaphoreType.DMA,
            ],
        ),
        out_shape=[jax.ShapeDtypeStruct((2, spectra, rows, LANES), jnp.bfloat16)]
        * (units * dests),
        cost_estimate=pl.CostEstimate(
            flops=3 * 2 * total * 4 * inner * inner, bytes_accessed=6 << 20, transcendentals=0
        ),
        compiler_params=pltpu.CompilerParams(vmem_limit_bytes=VMEM_BYTES),
        name="filter_transform",
    )(
        place,
        *blocks,
        coef_table,
        twiddle_tables(radix, inner),
        jnp.asarray(g_high),
        jnp.asarray(g_low),
        after,
    )
    return [made[unit * dests : (unit + 1) * dests] for unit in range(units)]


def join_kernel(place_ref, *rest):
    for shift, piece in enumerate(rest[:-1]):
        rest[-1][place_ref[len(rest) - 1 + shift]] = piece[...]


def join(pieces, place):
    vmem = pl.BlockSpec(memory_space=pltpu.VMEM)
    return pl.pallas_call(
        join_kernel,
        grid_spec=pltpu.PrefetchScalarGridSpec(
            num_scalar_prefetch=1, grid=(), in_specs=[vmem] * len(pieces), out_specs=vmem
        ),
        out_shape=jax.ShapeDtypeStruct((len(pieces), *pieces[0].shape), pieces[0].dtype),
        compiler_params=pltpu.CompilerParams(vmem_limit_bytes=VMEM_BYTES // 4),
        name="join_pieces",
    )(place, *pieces)


def correlate_kernel(chunks, blocks, scale, table_ref, *rest):
    g_refs, o_ref, left = rest[:blocks], rest[-2], rest[-1]
    senders, _, spectra, rows, lanes = g_refs[0].shape
    slots = o_ref.shape[2]
    coarse = lanes // AVG
    side = senders * rows
    run = rows // chunks
    step = pl.program_id(0)

    @pl.when(step == 0)
    def _():
        for block in range(blocks):
            source = g_refs[block]

            @pl.loop(0, senders)
            def _(sender, block=block, source=source):
                for part in range(2):
                    for chunk in range(chunks):
                        row = pl.multiple_of((chunk * senders + sender) * run, run)
                        pieces = [
                            source[sender, part, s, chunk * run : (chunk + 1) * run]
                            for s in range(spectra)
                        ]
                        for c in range(coarse):
                            line = jnp.concatenate(
                                [piece[:, c * AVG : (c + 1) * AVG] for piece in pieces], axis=1
                            )
                            width = line.shape[1]
                            left[
                                c, block, pl.ds(row, run), part * width : (part + 1) * width
                            ] = line
                            left[
                                c,
                                block,
                                pl.ds(pl.multiple_of(side + row, run), run),
                                (1 - part) * width : (2 - part) * width,
                            ] = -line if part == 0 else line

    count = table_ref[2 * slots]
    for slot in range(slots):

        @pl.when(slot < count)
        def _(slot=slot):
            rows_of = left[step, table_ref[slot]]
            cols_of = left[step, table_ref[slots + slot], pl.ds(0, side), :]
            tile = (
                lax.dot_general(
                    rows_of,
                    cols_of,
                    (((1,), (1,)), ((), ())),
                    preferred_element_type=jnp.float32,
                )
                * scale
            )
            o_ref[0, 0, slot] = tile[:side]
            o_ref[1, 0, slot] = tile[side:]

        @pl.when(slot >= count)
        def _(slot=slot):
            o_ref[:, 0, slot] = jnp.zeros((2, side, side), jnp.float32)


def correlate(table, gathered, unit, units, chunks, slots, vis):
    blocks = len(gathered)
    senders, _, spectra, rows, lanes = gathered[0].shape
    coarse = lanes // AVG
    side = senders * rows
    scale = 1.0 / (AVG * spectra)
    in_specs = [
        pl.BlockSpec(block.shape, lambda c, t: (0,) * 5, pipeline_mode=pl.Buffered(1))
        for block in gathered
    ]
    args = [table, *gathered]
    aliases = {}
    if vis is not None:
        in_specs.append(pl.BlockSpec(memory_space=pl.ANY))
        args.append(vis)
        aliases = {len(args) - 1: 0}
    return pl.pallas_call(
        functools.partial(correlate_kernel, chunks, blocks, scale),
        grid_spec=pltpu.PrefetchScalarGridSpec(
            num_scalar_prefetch=1,
            grid=(coarse,),
            in_specs=in_specs,
            out_specs=pl.BlockSpec(
                (2, 1, slots, side, side), lambda c, t: (0, unit * coarse + c, 0, 0, 0)
            ),
            scratch_shapes=[
                pltpu.VMEM((coarse, blocks, 2 * side, 2 * spectra * AVG), jnp.bfloat16)
            ],
        ),
        out_shape=jax.ShapeDtypeStruct((2, units * coarse, slots, side, side), jnp.float32),
        input_output_aliases=aliases,
        cost_estimate=pl.CostEstimate(
            flops=coarse * slots * 2 * 4 * side * side * spectra * AVG,
            bytes_accessed=8 << 20,
            transcendentals=0,
        ),
        compiler_params=pltpu.CompilerParams(vmem_limit_bytes=VMEM_BYTES),
        name="correlate_tiles",
    )(*args)


def places(count):
    steps = np.arange(count, dtype=np.int32)
    index = lax.axis_index("ft").astype(jnp.int32)
    return jnp.concatenate([(index + steps) % count, (index + count - steps) % count])


def spread(pieces):
    count = len(pieces)
    return [pieces[0]] + [
        lax.ppermute(pieces[d], "ft", [(i, (i + d) % count) for i in range(count)])
        for d in range(1, count)
    ]


def gather_blocks(own):
    count = lax.axis_size("bl")
    held = {0: own}
    bit = count // 2
    while bit:
        for r in list(held):
            held[r ^ bit] = lax.ppermute(held[r], "bl", [(i, i ^ bit) for i in range(count)])
        bit //= 2
    return [held[r] for r in range(count)]


def tile_tables(block_ids, tile_owner):
    block_count = lax.axis_size("bl")
    tile_count = block_count * (block_count + 1) // 2
    slot_cap = 2 * tile_count // block_count
    pairs = [(i, j) for i in range(block_count) for j in range(i, block_count)]
    row_table = np.array([i for i, _ in pairs], np.int32)
    col_table = np.array([j for _, j in pairs], np.int32)
    mine = (tile_owner == lax.axis_index("bl")).astype(jnp.int32)
    earlier = np.tril(np.ones((tile_count, tile_count), np.int32), -1)
    rank = jnp.sum(earlier * mine[None, :], axis=1)
    labels = np.arange(block_count, dtype=np.int32)
    shard_of = jnp.sum(jnp.where(block_ids[None, :] == labels[:, None], labels[None, :], 0), axis=1)
    row_shard = jnp.sum(
        jnp.where(row_table[:, None] == labels[None, :], shard_of[None, :], 0), axis=1
    )
    col_shard = jnp.sum(
        jnp.where(col_table[:, None] == labels[None, :], shard_of[None, :], 0), axis=1
    )
    here = (mine[None, :] == 1) & (rank[None, :] == np.arange(slot_cap, dtype=np.int32)[:, None])
    rows = jnp.sum(jnp.where(here, row_shard[None, :], 0), axis=1)
    cols = jnp.sum(jnp.where(here, col_shard[None, :], 0), axis=1)
    index = lax.axis_index("bl")
    table = jnp.concatenate(
        [rows ^ index, cols ^ index, jnp.sum(mine, keepdims=True)]
    ).astype(jnp.int32)
    return table, slot_cap


def takes_kernels(mesh, voltages, coefs):
    dests = mesh.shape["ft"]
    blocks = mesh.shape["bl"]
    inputs = voltages.shape[2] // mesh.shape["bl"]
    per_dev = voltages.shape[1] // (mesh.shape["grp"] * dests)
    chan_count = coefs.shape[1]
    radix = chan_count // MXU
    return (
        per_dev == chan_count
        and chan_count % MXU == 0
        and radix & (radix - 1) == 0
        and radix % dests == 0
        and radix <= 8
        and blocks & (blocks - 1) == 0
        and inputs % LANES == 0
        and LANES % dests == 0
        and (LANES // dests) % ROWS16 == 0
        and (dests * AVG) % LANES == 0
    )


def per_device_kernels(voltages, coefs, block_ids, tile_owner):
    dests = lax.axis_size("ft")
    taps, chan_count = coefs.shape
    radix = chan_count // MXU
    chunks = voltages.shape[2] // LANES
    coef_table = coefs.reshape(taps, MXU, radix).transpose(0, 2, 1)
    place = places(dests)
    table, slot_cap = tile_tables(block_ids, tile_owner)
    arrived = spread(pack(voltages, place, dests, radix))
    made = transform_all(arrived, place, coef_table, radix, table)
    joined = []
    for unit, parts in enumerate(made):
        if unit > 1:
            parts, joined[unit - 2] = lax.optimization_barrier((parts, joined[unit - 2]))
        joined.append(join(spread(parts), place))
    vis = None
    for unit, own in enumerate(joined):
        vis = correlate(table, gather_blocks(own), unit, len(made), chunks, slot_cap, vis)
    return vis


def tile_product(row_part, col_part, norm_scale):
    products = jnp.einsum(
        "pscax,qscay->cpqxy", row_part, col_part, preferred_element_type=jnp.float32
    )
    real_part = products[:, 0, 0] + products[:, 1, 1]
    imag_part = products[:, 1, 0] - products[:, 0, 1]
    return jnp.stack([real_part, imag_part]) * norm_scale


def dft_tables(order_len):
    steps_one = jnp.arange(order_len, dtype=jnp.int32)
    phase_grid = steps_one[:, None] * steps_one[None, :] % order_len
    angles = phase_grid.astype(jnp.float32) * (2.0 * math.pi / order_len)
    return (jnp.cos(angles), jnp.sin(angles))


def transform(filtered):
    per_dev = filtered.shape[1]
    chan_count = filtered.shape[2]
    rows_here = filtered.shape[3]
    outer_len = math.isqrt(chan_count)
    while chan_count % outer_len != 0:
        outer_len = outer_len - 1
    inner_len = chan_count // outer_len
    highest = lax.Precision.HIGHEST
    reshaped = filtered.reshape(2, per_dev, outer_len, inner_len, rows_here)
    real_in = reshaped[0]
    imag_in = reshaped[1]
    cos_outer, sin_outer = dft_tables(outer_len)
    section_re = jnp.einsum("snkb,nm->smkb", real_in, cos_outer, precision=highest) + jnp.einsum(
        "snkb,nm->smkb", imag_in, sin_outer, precision=highest
    )
    section_im = jnp.einsum("snkb,nm->smkb", imag_in, cos_outer, precision=highest) - jnp.einsum(
        "snkb,nm->smkb", real_in, sin_outer, precision=highest
    )
    twiddle_grid = (
        jnp.arange(outer_len, dtype=jnp.int32)[:, None]
        * jnp.arange(inner_len, dtype=jnp.int32)[None, :]
        % chan_count
    )
    twiddle_angles = twiddle_grid.astype(jnp.float32) * (2.0 * math.pi / chan_count)
    cos_twiddle = jnp.cos(twiddle_angles)[None, :, :, None]
    sin_twiddle = jnp.sin(twiddle_angles)[None, :, :, None]
    rot_re = section_re * cos_twiddle + section_im * sin_twiddle
    rot_im = section_im * cos_twiddle - section_re * sin_twiddle
    cos_inner, sin_inner = dft_tables(inner_len)
    final_re = jnp.einsum("smkb,kq->sqmb", rot_re, cos_inner, precision=highest) + jnp.einsum(
        "smkb,kq->sqmb", rot_im, sin_inner, precision=highest
    )
    final_im = jnp.einsum("smkb,kq->sqmb", rot_im, cos_inner, precision=highest) - jnp.einsum(
        "smkb,kq->sqmb", rot_re, sin_inner, precision=highest
    )
    stacked = jnp.stack([final_re, final_im]).reshape(2, per_dev, chan_count, rows_here)
    return (stacked * (1.0 / math.sqrt(chan_count))).astype(jnp.bfloat16)


def apply_taps(window, coef_part, taps_count, out_len):
    filtered = jnp.zeros((2, out_len, window.shape[2], window.shape[3]), jnp.float32)
    for tap_index in range(taps_count):
        filtered = filtered + coef_part[tap_index][None, None, :, None] * window[
            :, tap_index : tap_index + out_len
        ].astype(jnp.float32)
    return filtered


def per_device(voltages, coefs, block_ids, tile_owner):
    taps_count = coefs.shape[0]
    chan_count = coefs.shape[1]
    rows_here = voltages.shape[2]
    per_dev = voltages.shape[1] // chan_count
    volt_blocks = voltages.reshape(2, per_dev, chan_count, rows_here)
    phase_block = lax.all_to_all(volt_blocks, "ft", split_axis=2, concat_axis=1, tiled=True)
    spectra_count = phase_block.shape[1]
    phase_here = phase_block.shape[2]
    coef_part = lax.dynamic_slice_in_dim(coefs, lax.axis_index("ft") * phase_here, phase_here, 1)
    zero_front = jnp.zeros((2, taps_count - 1, phase_here, rows_here), phase_block.dtype)
    long_window = jnp.concatenate([zero_front, phase_block], axis=1)
    phase_filtered = apply_taps(long_window, coef_part, taps_count, spectra_count)
    filtered = lax.all_to_all(phase_filtered, "ft", split_axis=1, concat_axis=2, tiled=True)
    spectra = transform(filtered)
    turned = lax.all_to_all(spectra, "ft", split_axis=2, concat_axis=1, tiled=True)
    spectra_all = turned.shape[1]
    chan_here = turned.shape[2]
    coarse_here = chan_here // AVG
    coarse_view = turned.reshape(2, spectra_all, coarse_here, AVG, rows_here)
    norm_scale = 1.0 / (AVG * spectra_all)
    block_count = lax.axis_size("bl")
    my_index = lax.axis_index("bl")
    tile_count = block_count * (block_count + 1) // 2
    slot_cap = 2 * tile_count // block_count
    row_table = jnp.asarray(
        np.array(
            [
                first_id
                for first_id in range(block_count)
                for second_id in range(first_id, block_count)
            ],
            dtype=np.int32,
        )
    )
    col_table = jnp.asarray(
        np.array(
            [
                second_id
                for first_id in range(block_count)
                for second_id in range(first_id, block_count)
            ],
            dtype=np.int32,
        )
    )
    tile_pos = jnp.arange(tile_count, dtype=jnp.int32)
    same_owner = tile_owner[None, :] == tile_owner[:, None]
    before_mask = tile_pos[None, :] < tile_pos[:, None]
    slot_rank = jnp.sum((same_owner & before_mask).astype(jnp.int32), axis=1)
    labels = jnp.arange(block_count, dtype=jnp.int32)
    shard_of = jnp.sum(jnp.where(block_ids[None, :] == labels[:, None], labels[None, :], 0), axis=1)
    gathered = lax.all_gather(coarse_view[None], "bl", axis=0, tiled=True)
    mine_mask = tile_owner == my_index
    own_count = jnp.sum(mine_mask.astype(jnp.int32))
    slot_steps = jnp.arange(slot_cap, dtype=jnp.int32)
    slot_tile = jnp.sum(
        jnp.where(
            mine_mask[None, :] & (slot_rank[None, :] == slot_steps[:, None]), tile_pos[None, :], 0
        ),
        axis=1,
    )

    def one_tile(slot_pos, result_tiles):
        tile_id = slot_tile[slot_pos]
        row_block = gathered[shard_of[row_table[tile_id]]]
        col_block = gathered[shard_of[col_table[tile_id]]]
        tile = tile_product(row_block, col_block, norm_scale)
        return lax.dynamic_update_slice(result_tiles, tile[:, :, None], (0, 0, slot_pos, 0, 0))

    empty_tiles = jnp.zeros((2, coarse_here, slot_cap, rows_here, rows_here), jnp.float32)
    return lax.fori_loop(0, own_count, one_tile, empty_tiles)


def solution(mesh):
    def correlator(voltages, coefs, block_ids, tile_owner):
        fits = takes_kernels(mesh, voltages, coefs)
        return jax.shard_map(
            per_device_kernels if fits else per_device,
            mesh=mesh,
            in_specs=(P(None, ("grp", "ft"), "bl"), P(), P(), P("grp")),
            out_specs=P(None, ("grp", "ft"), "bl", None, None),
            check_vma=False,
        )(voltages, coefs, block_ids, tile_owner)

    return correlator
```

```python
import functools
import math

import jax
import jax.numpy as jnp
import ml_dtypes
import numpy as np
from jax import lax
from jax.experimental import pallas as pl
from jax.experimental.pallas import tpu as pltpu
from jax.sharding import PartitionSpec as P

AVG = 64
MXU = 256
LANES = 128
ROWS16 = 16
VMEM_BYTES = 48 * 1024 * 1024


def split_bf16(table):
    high = table.astype(ml_dtypes.bfloat16)
    low = (table - high.astype(np.float64)).astype(ml_dtypes.bfloat16)
    return high, low


def matrix_tables(inner_len):
    steps = np.arange(inner_len)
    angles = 2.0 * np.pi * (np.outer(steps, steps) % inner_len) / inner_len
    cos_part, sin_part = np.cos(angles), np.sin(angles)
    return split_bf16(np.block([[cos_part, -sin_part], [sin_part, cos_part]]))


def twiddle_tables(radix, inner_len):
    chan_count = radix * inner_len
    angles = 2.0 * np.pi * np.outer(np.arange(radix), np.arange(inner_len)) / chan_count
    scale = 1.0 / math.sqrt(chan_count)
    return np.stack([np.cos(angles) * scale, np.sin(angles) * scale]).astype(np.float32)


def rotate(real, imag, step, count):
    step = step % count
    if step == 0:
        return real, imag
    if 4 * step == count:
        return imag, -real
    if 2 * step == count:
        return -real, -imag
    if 4 * step == 3 * count:
        return -imag, real
    cos_step = math.cos(2.0 * math.pi * step / count)
    sin_step = math.sin(2.0 * math.pi * step / count)
    if 8 * step == count:
        return cos_step * (real + imag), cos_step * (imag - real)
    return cos_step * real + sin_step * imag, cos_step * imag - sin_step * real


def butterflies(parts):
    count = len(parts)
    if count == 1:
        return parts
    half = count // 2
    sums, diffs = [], []
    for k in range(half):
        (ar, ai), (br, bi) = parts[k], parts[k + half]
        sums.append((ar + br, ai + bi))
        diffs.append(rotate(ar - br, ai - bi, k, count))
    even, odd = butterflies(sums), butterflies(diffs)
    out = []
    for k in range(half):
        out += [even[k], odd[k]]
    return out


def pack_kernel(radix, place_ref, v_ref, *rest):
    o_refs, (wide, turned) = rest[:-2], rest[-2:]
    dests, rows, samples = turned.shape
    inner = samples // radix
    wide[...] = v_ref[0].astype(jnp.float32)
    for phase in range(radix):
        part = wide[pl.ds(phase, inner, stride=radix), :].T.astype(jnp.bfloat16)
        for dest in range(dests):
            turned[dest, :, phase * inner : (phase + 1) * inner] = part[
                dest * rows : (dest + 1) * rows
            ]
    for shift in range(dests):
        o_refs[shift][0] = turned[place_ref[shift]]


def pack(voltages, place, dests, radix):
    _, samples, inputs = voltages.shape
    chunks = inputs // LANES
    rows = LANES // dests
    return pl.pallas_call(
        functools.partial(pack_kernel, radix),
        grid_spec=pltpu.PrefetchScalarGridSpec(
            num_scalar_prefetch=1,
            grid=(2, chunks),
            in_specs=[pl.BlockSpec((1, samples, LANES), lambda p, h, t: (p, 0, h))],
            out_specs=[pl.BlockSpec((1, rows, samples), lambda p, h, t: (p, h, 0))] * dests,
            scratch_shapes=[
                pltpu.VMEM((samples, LANES), jnp.float32),
                pltpu.VMEM((dests, rows, samples), jnp.bfloat16),
            ],
        ),
        out_shape=[jax.ShapeDtypeStruct((2, chunks * rows, samples), jnp.bfloat16)] * dests,
        compiler_params=pltpu.CompilerParams(vmem_limit_bytes=VMEM_BYTES),
        name="pack_inputs",
    )(place, voltages)


def stage_kernel(*refs):
    half = len(refs) // 2
    for source, target in zip(refs[:half], refs[half:]):
        target[...] = source[...]


def stage(*tables):
    vmem = pl.BlockSpec(memory_space=pltpu.VMEM)
    return pl.pallas_call(
        stage_kernel,
        in_specs=[vmem] * len(tables),
        out_specs=[vmem] * len(tables),
        out_shape=[jax.ShapeDtypeStruct(table.shape, table.dtype) for table in tables],
        compiler_params=pltpu.CompilerParams(vmem_limit_bytes=VMEM_BYTES // 4),
        name="stage_tables",
    )(*tables)


def transform_kernel(radix, dests, units, place_ref, *rest):
    v_refs = rest[:dests]
    c_ref, tw_ref, gh_ref, gl_ref = rest[dests : dests + 4]
    out_refs = rest[dests + 5 : -4]
    held, split, prod, made = rest[-4:]
    spectra, _, rows, samples = held.shape
    taps = c_ref.shape[0]
    inner = samples // radix
    group = spectra * rows
    for shift in range(dests):
        held[place_ref[dests + shift]] = v_refs[shift][...]

    @pl.loop(0, radix)
    def _(phase):
        lane0 = pl.multiple_of(phase * inner, inner)
        row0 = pl.multiple_of(phase * group, group)
        for part in range(2):
            for sub in range(0, rows, ROWS16):
                blocks = [
                    held[b, part, pl.ds(sub, ROWS16), pl.ds(lane0, inner)].astype(jnp.float32)
                    for b in range(spectra)
                ]
                for s in range(spectra):
                    total = None
                    for b in range(max(0, s - taps + 1), s + 1):
                        term = c_ref[taps - 1 - s + b, pl.ds(phase, 1), :] * blocks[b]
                        total = term if total is None else total + term
                    high = total.astype(jnp.bfloat16)
                    low = (total - high.astype(jnp.float32)).astype(jnp.bfloat16)
                    at = pl.ds(pl.multiple_of(row0 + s * rows + sub, ROWS16), ROWS16)
                    split[at, part * inner : (part + 1) * inner] = high
                    split[at, (2 + part) * inner : (3 + part) * inner] = low

    @pl.loop(0, radix // 2)
    def _(pair):
        at = pl.ds(pl.multiple_of(pair * 2 * group, 2 * group), 2 * group)
        high = split[at, : 2 * inner]
        low = split[at, 2 * inner :]
        prod[at, :] = (
            jnp.dot(high, gh_ref[...], preferred_element_type=jnp.float32)
            + jnp.dot(high, gl_ref[...], preferred_element_type=jnp.float32)
            + jnp.dot(low, gh_ref[...], preferred_element_type=jnp.float32)
        )

    halves = radix // dests
    lane_cuts = inner // LANES

    @pl.loop(0, spectra)
    def _(s):
        for sub in range(0, rows, ROWS16):
            for cut in range(lane_cuts):
                lane = cut * LANES
                parts = []
                for phase in range(radix):
                    at = pl.ds(pl.multiple_of(phase * group + s * rows + sub, ROWS16), ROWS16)
                    yr = prod[at, lane : lane + LANES]
                    yi = prod[at, inner + lane : inner + lane + LANES]
                    cos_here = tw_ref[0, phase : phase + 1, lane : lane + LANES]
                    sin_here = tw_ref[1, phase : phase + 1, lane : lane + LANES]
                    if phase == 0:
                        parts.append((yr * cos_here, yi * cos_here))
                    else:
                        parts.append(
                            (yr * cos_here + yi * sin_here, yi * cos_here - yr * sin_here)
                        )
                for step, pair in enumerate(butterflies(parts)):
                    unit = step % halves * lane_cuts + cut
                    for part in range(2):
                        made[step // halves, unit, part, s, sub : sub + ROWS16, :] = pair[
                            part
                        ].astype(jnp.bfloat16)

    for shift in range(dests):
        for unit in range(units):
            out_refs[unit * dests + shift][...] = made[place_ref[shift], unit]


def transform_all(blocks, place, tables, radix, after):
    dests = len(blocks)
    _, rows, samples = blocks[0].shape
    spectra = dests
    inner = samples // radix
    units = samples // dests // LANES
    anywhere = pl.BlockSpec(memory_space=pl.ANY)
    vmem = pl.BlockSpec(memory_space=pltpu.VMEM)
    total = radix * spectra * rows
    made = pl.pallas_call(
        functools.partial(transform_kernel, radix, dests, units),
        grid_spec=pltpu.PrefetchScalarGridSpec(
            num_scalar_prefetch=1,
            grid=(),
            in_specs=[vmem] * (dests + 4) + [anywhere],
            out_specs=[vmem] * (units * dests),
            scratch_shapes=[
                pltpu.VMEM((spectra, 2, rows, samples), jnp.bfloat16),
                pltpu.VMEM((total, 4 * inner), jnp.bfloat16),
                pltpu.VMEM((total, 2 * inner), jnp.float32),
                pltpu.VMEM((dests, units, 2, spectra, rows, LANES), jnp.bfloat16),
            ],
        ),
        out_shape=[jax.ShapeDtypeStruct((2, spectra, rows, LANES), jnp.bfloat16)]
        * (units * dests),
        cost_estimate=pl.CostEstimate(
            flops=3 * 2 * total * 4 * inner * inner, bytes_accessed=6 << 20, transcendentals=0
        ),
        compiler_params=pltpu.CompilerParams(vmem_limit_bytes=VMEM_BYTES),
        name="filter_transform",
    )(
        place,
        *blocks,
        *tables,
        after,
    )
    return [made[unit * dests : (unit + 1) * dests] for unit in range(units)]


def join_kernel(count, where, place_ref, *rest):
    for shift in range(count):
        rest[-1][place_ref[where + shift]] = rest[shift][...]


def join(pieces, place, where, after):
    vmem = pl.BlockSpec(memory_space=pltpu.VMEM)
    return pl.pallas_call(
        functools.partial(join_kernel, len(pieces), where),
        grid_spec=pltpu.PrefetchScalarGridSpec(
            num_scalar_prefetch=1,
            grid=(),
            in_specs=[vmem] * len(pieces) + [pl.BlockSpec(memory_space=pl.ANY)],
            out_specs=vmem,
        ),
        out_shape=jax.ShapeDtypeStruct((len(pieces), *pieces[0].shape), pieces[0].dtype),
        compiler_params=pltpu.CompilerParams(vmem_limit_bytes=VMEM_BYTES // 4),
        name="join_pieces",
    )(place, *pieces, after)


def correlate_kernel(chunks, scale, table_ref, *rest):
    o_ref, token_ref, left = rest[-3:]
    half, senders, _, spectra, rows, lanes = rest[0].shape
    order = block_order(2 * half)
    blocks = len(order)
    slots = o_ref.shape[2]
    coarse = lanes // AVG
    side = senders * rows
    run = rows // chunks
    step = pl.program_id(0)

    @pl.when(step == 0)
    def _():
        token_ref[...] = jnp.zeros_like(token_ref)
        for at, block in enumerate(order):

            @pl.loop(0, senders)
            def _(sender, block=block, source=rest[at // half].at[at % half]):
                for part in range(2):
                    for chunk in range(chunks):
                        row = pl.multiple_of((chunk * senders + sender) * run, run)
                        pieces = [
                            source[sender, part, s, chunk * run : (chunk + 1) * run]
                            for s in range(spectra)
                        ]
                        for c in range(coarse):
                            line = jnp.concatenate(
                                [piece[:, c * AVG : (c + 1) * AVG] for piece in pieces], axis=1
                            )
                            width = line.shape[1]
                            left[
                                c, block, pl.ds(row, run), part * width : (part + 1) * width
                            ] = line
                            left[
                                c,
                                block,
                                pl.ds(pl.multiple_of(side + row, run), run),
                                (1 - part) * width : (2 - part) * width,
                            ] = -line if part == 0 else line

    count = table_ref[2 * slots]
    for slot in range(slots):

        @pl.when(slot < count)
        def _(slot=slot):
            rows_of = left[step, table_ref[slot]]
            cols_of = left[step, table_ref[slots + slot], pl.ds(0, side), :]
            tile = (
                lax.dot_general(
                    rows_of,
                    cols_of,
                    (((1,), (1,)), ((), ())),
                    preferred_element_type=jnp.float32,
                )
                * scale
            )
            o_ref[0, 0, slot] = tile[:side]
            o_ref[1, 0, slot] = tile[side:]

        @pl.when(slot >= count)
        def _(slot=slot):
            o_ref[:, 0, slot] = jnp.zeros((2, side, side), jnp.float32)


def correlate(table, gathered, unit, units, chunks, slots, vis):
    half, senders, _, spectra, rows, lanes = gathered[0].shape
    blocks = 2 * half
    coarse = lanes // AVG
    side = senders * rows
    scale = 1.0 / (AVG * spectra)
    in_specs = [
        pl.BlockSpec(
            part.shape, lambda c, t, n=part.ndim: (0,) * n, pipeline_mode=pl.Buffered(1)
        )
        for part in gathered
    ]
    args = [table, *gathered]
    aliases = {}
    if vis is not None:
        in_specs.append(pl.BlockSpec(memory_space=pl.ANY))
        args.append(vis)
        aliases = {len(args) - 1: 0}
    return pl.pallas_call(
        functools.partial(correlate_kernel, chunks, scale),
        grid_spec=pltpu.PrefetchScalarGridSpec(
            num_scalar_prefetch=1,
            grid=(coarse,),
            in_specs=in_specs,
            out_specs=[
                pl.BlockSpec(
                    (2, 1, slots, side, side), lambda c, t: (0, unit * coarse + c, 0, 0, 0)
                ),
                pl.BlockSpec((8, LANES), lambda c, t: (0, 0)),
            ],
            scratch_shapes=[
                pltpu.VMEM((coarse, blocks, 2 * side, 2 * spectra * AVG), jnp.bfloat16)
            ],
        ),
        out_shape=[
            jax.ShapeDtypeStruct((2, units * coarse, slots, side, side), jnp.float32),
            jax.ShapeDtypeStruct((8, LANES), jnp.float32),
        ],
        input_output_aliases=aliases,
        cost_estimate=pl.CostEstimate(
            flops=coarse * slots * 2 * 4 * side * side * spectra * AVG,
            bytes_accessed=8 << 20,
            transcendentals=0,
        ),
        compiler_params=pltpu.CompilerParams(vmem_limit_bytes=VMEM_BYTES),
        name="correlate_tiles",
    )(*args)


def places(count):
    steps = np.arange(count, dtype=np.int32)
    index = lax.axis_index("ft").astype(jnp.int32)
    return jnp.concatenate([(index + steps) % count, (index + count - steps) % count])


def spread(pieces):
    count = len(pieces)
    return [pieces[0]] + [
        lax.ppermute(pieces[d], "ft", [(i, (i + d) % count) for i in range(count)])
        for d in range(1, count)
    ]


def exchange(own, bit):
    count = lax.axis_size("bl")
    return lax.ppermute(own, "bl", [(i, i ^ bit) for i in range(count)])


def gather_blocks(own, partner, after):
    bit = lax.axis_size("bl") // 2
    held, other = own[None], partner[None]
    while bit > 1:
        both = join([held, other], np.arange(2, dtype=np.int32), 0, after)
        held = both.reshape(-1, *own.shape)
        bit //= 2
        other = exchange(held, bit)
    return held, other


def block_order(count):
    order, bit = [0], count // 2
    while bit:
        order += [r ^ bit for r in order]
        bit //= 2
    return order


def tile_tables(block_ids, tile_owner):
    block_count = lax.axis_size("bl")
    tile_count = block_count * (block_count + 1) // 2
    slot_cap = 2 * tile_count // block_count
    pairs = [(i, j) for i in range(block_count) for j in range(i, block_count)]
    row_table = np.array([i for i, _ in pairs], np.int32)
    col_table = np.array([j for _, j in pairs], np.int32)
    mine = (tile_owner == lax.axis_index("bl")).astype(jnp.int32)
    earlier = np.tril(np.ones((tile_count, tile_count), np.int32), -1)
    rank = jnp.sum(earlier * mine[None, :], axis=1)
    labels = np.arange(block_count, dtype=np.int32)
    shard_of = jnp.sum(jnp.where(block_ids[None, :] == labels[:, None], labels[None, :], 0), axis=1)
    row_shard = jnp.sum(
        jnp.where(row_table[:, None] == labels[None, :], shard_of[None, :], 0), axis=1
    )
    col_shard = jnp.sum(
        jnp.where(col_table[:, None] == labels[None, :], shard_of[None, :], 0), axis=1
    )
    here = (mine[None, :] == 1) & (rank[None, :] == np.arange(slot_cap, dtype=np.int32)[:, None])
    rows = jnp.sum(jnp.where(here, row_shard[None, :], 0), axis=1)
    cols = jnp.sum(jnp.where(here, col_shard[None, :], 0), axis=1)
    index = lax.axis_index("bl")
    table = jnp.concatenate(
        [rows ^ index, cols ^ index, jnp.sum(mine, keepdims=True)]
    ).astype(jnp.int32)
    return table, slot_cap


def takes_kernels(mesh, voltages, coefs):
    dests = mesh.shape["ft"]
    blocks = mesh.shape["bl"]
    inputs = voltages.shape[2] // mesh.shape["bl"]
    per_dev = voltages.shape[1] // (mesh.shape["grp"] * dests)
    chan_count = coefs.shape[1]
    radix = chan_count // MXU
    return (
        per_dev == chan_count
        and chan_count % MXU == 0
        and radix & (radix - 1) == 0
        and radix % dests == 0
        and radix <= 8
        and blocks & (blocks - 1) == 0
        and blocks > 1
        and inputs % LANES == 0
        and LANES % dests == 0
        and (LANES // dests) % ROWS16 == 0
        and (dests * AVG) % LANES == 0
    )


def per_device_kernels(voltages, coefs, block_ids, tile_owner):
    dests = lax.axis_size("ft")
    taps, chan_count = coefs.shape
    radix = chan_count // MXU
    chunks = voltages.shape[2] // LANES
    coef_table = coefs.reshape(taps, MXU, radix).transpose(0, 2, 1)
    place = places(dests)
    table, slot_cap = tile_tables(block_ids, tile_owner)
    tables = stage(coef_table, twiddle_tables(radix, MXU), *matrix_tables(MXU))
    arrived = spread(pack(voltages, place, dests, radix))
    made = transform_all(arrived, place, tables, radix, table)
    half = lax.axis_size("bl") // 2
    partners, tokens, vis = [], [], None
    for unit in range(len(made) + 1):
        if unit < len(made):
            parts = made[unit]
            if unit > 1:
                first = (partners[unit - 2][1], arrived)
                parts, _ = lax.optimization_barrier((parts, first))
            arrived = spread(parts)
            own = join(arrived, place, dests, tokens[unit - 2] if unit > 1 else table)
            partners.append((own, exchange(own, half)))
        if unit > 0:
            gathered = gather_blocks(
                *partners[unit - 1], partners[unit][0] if unit < len(made) else table
            )
            vis, token = correlate(
                table, gathered, unit - 1, len(made), chunks, slot_cap, vis
            )
            tokens.append(token)
    return vis


def tile_product(row_part, col_part, norm_scale):
    products = jnp.einsum(
        "pscax,qscay->cpqxy", row_part, col_part, preferred_element_type=jnp.float32
    )
    real_part = products[:, 0, 0] + products[:, 1, 1]
    imag_part = products[:, 1, 0] - products[:, 0, 1]
    return jnp.stack([real_part, imag_part]) * norm_scale


def dft_tables(order_len):
    steps_one = jnp.arange(order_len, dtype=jnp.int32)
    phase_grid = steps_one[:, None] * steps_one[None, :] % order_len
    angles = phase_grid.astype(jnp.float32) * (2.0 * math.pi / order_len)
    return (jnp.cos(angles), jnp.sin(angles))


def transform(filtered):
    per_dev = filtered.shape[1]
    chan_count = filtered.shape[2]
    rows_here = filtered.shape[3]
    outer_len = math.isqrt(chan_count)
    while chan_count % outer_len != 0:
        outer_len = outer_len - 1
    inner_len = chan_count // outer_len
    highest = lax.Precision.HIGHEST
    reshaped = filtered.reshape(2, per_dev, outer_len, inner_len, rows_here)
    real_in = reshaped[0]
    imag_in = reshaped[1]
    cos_outer, sin_outer = dft_tables(outer_len)
    section_re = jnp.einsum("snkb,nm->smkb", real_in, cos_outer, precision=highest) + jnp.einsum(
        "snkb,nm->smkb", imag_in, sin_outer, precision=highest
    )
    section_im = jnp.einsum("snkb,nm->smkb", imag_in, cos_outer, precision=highest) - jnp.einsum(
        "snkb,nm->smkb", real_in, sin_outer, precision=highest
    )
    twiddle_grid = (
        jnp.arange(outer_len, dtype=jnp.int32)[:, None]
        * jnp.arange(inner_len, dtype=jnp.int32)[None, :]
        % chan_count
    )
    twiddle_angles = twiddle_grid.astype(jnp.float32) * (2.0 * math.pi / chan_count)
    cos_twiddle = jnp.cos(twiddle_angles)[None, :, :, None]
    sin_twiddle = jnp.sin(twiddle_angles)[None, :, :, None]
    rot_re = section_re * cos_twiddle + section_im * sin_twiddle
    rot_im = section_im * cos_twiddle - section_re * sin_twiddle
    cos_inner, sin_inner = dft_tables(inner_len)
    final_re = jnp.einsum("smkb,kq->sqmb", rot_re, cos_inner, precision=highest) + jnp.einsum(
        "smkb,kq->sqmb", rot_im, sin_inner, precision=highest
    )
    final_im = jnp.einsum("smkb,kq->sqmb", rot_im, cos_inner, precision=highest) - jnp.einsum(
        "smkb,kq->sqmb", rot_re, sin_inner, precision=highest
    )
    stacked = jnp.stack([final_re, final_im]).reshape(2, per_dev, chan_count, rows_here)
    return (stacked * (1.0 / math.sqrt(chan_count))).astype(jnp.bfloat16)


def apply_taps(window, coef_part, taps_count, out_len):
    filtered = jnp.zeros((2, out_len, window.shape[2], window.shape[3]), jnp.float32)
    for tap_index in range(taps_count):
        filtered = filtered + coef_part[tap_index][None, None, :, None] * window[
            :, tap_index : tap_index + out_len
        ].astype(jnp.float32)
    return filtered


def per_device(voltages, coefs, block_ids, tile_owner):
    taps_count = coefs.shape[0]
    chan_count = coefs.shape[1]
    rows_here = voltages.shape[2]
    per_dev = voltages.shape[1] // chan_count
    volt_blocks = voltages.reshape(2, per_dev, chan_count, rows_here)
    phase_block = lax.all_to_all(volt_blocks, "ft", split_axis=2, concat_axis=1, tiled=True)
    spectra_count = phase_block.shape[1]
    phase_here = phase_block.shape[2]
    coef_part = lax.dynamic_slice_in_dim(coefs, lax.axis_index("ft") * phase_here, phase_here, 1)
    zero_front = jnp.zeros((2, taps_count - 1, phase_here, rows_here), phase_block.dtype)
    long_window = jnp.concatenate([zero_front, phase_block], axis=1)
    phase_filtered = apply_taps(long_window, coef_part, taps_count, spectra_count)
    filtered = lax.all_to_all(phase_filtered, "ft", split_axis=1, concat_axis=2, tiled=True)
    spectra = transform(filtered)
    turned = lax.all_to_all(spectra, "ft", split_axis=2, concat_axis=1, tiled=True)
    spectra_all = turned.shape[1]
    chan_here = turned.shape[2]
    coarse_here = chan_here // AVG
    coarse_view = turned.reshape(2, spectra_all, coarse_here, AVG, rows_here)
    norm_scale = 1.0 / (AVG * spectra_all)
    block_count = lax.axis_size("bl")
    my_index = lax.axis_index("bl")
    tile_count = block_count * (block_count + 1) // 2
    slot_cap = 2 * tile_count // block_count
    row_table = jnp.asarray(
        np.array(
            [
                first_id
                for first_id in range(block_count)
                for second_id in range(first_id, block_count)
            ],
            dtype=np.int32,
        )
    )
    col_table = jnp.asarray(
        np.array(
            [
                second_id
                for first_id in range(block_count)
                for second_id in range(first_id, block_count)
            ],
            dtype=np.int32,
        )
    )
    tile_pos = jnp.arange(tile_count, dtype=jnp.int32)
    same_owner = tile_owner[None, :] == tile_owner[:, None]
    before_mask = tile_pos[None, :] < tile_pos[:, None]
    slot_rank = jnp.sum((same_owner & before_mask).astype(jnp.int32), axis=1)
    labels = jnp.arange(block_count, dtype=jnp.int32)
    shard_of = jnp.sum(jnp.where(block_ids[None, :] == labels[:, None], labels[None, :], 0), axis=1)
    gathered = lax.all_gather(coarse_view[None], "bl", axis=0, tiled=True)
    mine_mask = tile_owner == my_index
    own_count = jnp.sum(mine_mask.astype(jnp.int32))
    slot_steps = jnp.arange(slot_cap, dtype=jnp.int32)
    slot_tile = jnp.sum(
        jnp.where(
            mine_mask[None, :] & (slot_rank[None, :] == slot_steps[:, None]), tile_pos[None, :], 0
        ),
        axis=1,
    )

    def one_tile(slot_pos, result_tiles):
        tile_id = slot_tile[slot_pos]
        row_block = gathered[shard_of[row_table[tile_id]]]
        col_block = gathered[shard_of[col_table[tile_id]]]
        tile = tile_product(row_block, col_block, norm_scale)
        return lax.dynamic_update_slice(result_tiles, tile[:, :, None], (0, 0, slot_pos, 0, 0))

    empty_tiles = jnp.zeros((2, coarse_here, slot_cap, rows_here, rows_here), jnp.float32)
    return lax.fori_loop(0, own_count, one_tile, empty_tiles)


def solution(mesh):
    def correlator(voltages, coefs, block_ids, tile_owner):
        fits = takes_kernels(mesh, voltages, coefs)
        return jax.shard_map(
            per_device_kernels if fits else per_device,
            mesh=mesh,
            in_specs=(P(None, ("grp", "ft"), "bl"), P(), P(), P("grp")),
            out_specs=P(None, ("grp", "ft"), "bl", None, None),
            check_vma=False,
        )(voltages, coefs, block_ids, tile_owner)

    return correlator
```

```python
import functools
import math

import jax
import jax.numpy as jnp
import ml_dtypes
import numpy as np
from jax import lax
from jax.experimental import pallas as pl
from jax.experimental.pallas import tpu as pltpu
from jax.sharding import PartitionSpec as P

AVG = 64
MXU = 256
LANES = 128
ROWS16 = 16
VMEM_BYTES = 48 * 1024 * 1024
VMEM_MOST = 60 * 1024 * 1024


def split_bf16(table):
    high = table.astype(ml_dtypes.bfloat16)
    low = (table - high.astype(np.float64)).astype(ml_dtypes.bfloat16)
    return high, low


def matrix_tables(inner_len):
    steps = np.arange(inner_len)
    angles = 2.0 * np.pi * (np.outer(steps, steps) % inner_len) / inner_len
    cos_part, sin_part = np.cos(angles), np.sin(angles)
    return split_bf16(np.block([[cos_part, -sin_part], [sin_part, cos_part]]))


def twiddle_tables(radix, inner_len):
    chan_count = radix * inner_len
    angles = 2.0 * np.pi * np.outer(np.arange(radix), np.arange(inner_len)) / chan_count
    scale = 1.0 / math.sqrt(chan_count)
    return np.stack([np.cos(angles) * scale, np.sin(angles) * scale]).astype(np.float32)


def rotate(real, imag, step, count):
    step = step % count
    if step == 0:
        return real, imag
    if 4 * step == count:
        return imag, -real
    if 2 * step == count:
        return -real, -imag
    if 4 * step == 3 * count:
        return -imag, real
    cos_step = math.cos(2.0 * math.pi * step / count)
    sin_step = math.sin(2.0 * math.pi * step / count)
    if 8 * step == count:
        return cos_step * (real + imag), cos_step * (imag - real)
    return cos_step * real + sin_step * imag, cos_step * imag - sin_step * real


def butterflies(parts):
    count = len(parts)
    if count == 1:
        return parts
    half = count // 2
    sums, diffs = [], []
    for k in range(half):
        (ar, ai), (br, bi) = parts[k], parts[k + half]
        sums.append((ar + br, ai + bi))
        diffs.append(rotate(ar - br, ai - bi, k, count))
    even, odd = butterflies(sums), butterflies(diffs)
    out = []
    for k in range(half):
        out += [even[k], odd[k]]
    return out


def pack_kernel(radix, place_ref, v_ref, *rest):
    o_refs, (wide, turned) = rest[:-2], rest[-2:]
    dests, rows, samples = turned.shape
    inner = samples // radix
    wide[...] = v_ref[0].astype(jnp.float32)
    for phase in range(radix):
        part = wide[pl.ds(phase, inner, stride=radix), :].T.astype(jnp.bfloat16)
        for dest in range(dests):
            turned[dest, :, phase * inner : (phase + 1) * inner] = part[
                dest * rows : (dest + 1) * rows
            ]
    for shift in range(dests):
        o_refs[shift][0] = turned[place_ref[shift]]


def pack(voltages, place, dests, radix):
    _, samples, inputs = voltages.shape
    chunks = inputs // LANES
    rows = LANES // dests
    return pl.pallas_call(
        functools.partial(pack_kernel, radix),
        grid_spec=pltpu.PrefetchScalarGridSpec(
            num_scalar_prefetch=1,
            grid=(2, chunks),
            in_specs=[pl.BlockSpec((1, samples, LANES), lambda p, h, t: (p, 0, h))],
            out_specs=[pl.BlockSpec((1, rows, samples), lambda p, h, t: (p, h, 0))] * dests,
            scratch_shapes=[
                pltpu.VMEM((samples, LANES), jnp.float32),
                pltpu.VMEM((dests, rows, samples), jnp.bfloat16),
            ],
        ),
        out_shape=[jax.ShapeDtypeStruct((2, chunks * rows, samples), jnp.bfloat16)] * dests,
        compiler_params=pltpu.CompilerParams(vmem_limit_bytes=VMEM_MOST),
        name="pack_inputs",
    )(place, voltages)


def stage_kernel(*refs):
    half = len(refs) // 2
    for source, target in zip(refs[:half], refs[half:]):
        target[...] = source[...]


def stage(*tables):
    vmem = pl.BlockSpec(memory_space=pltpu.VMEM)
    return pl.pallas_call(
        stage_kernel,
        in_specs=[vmem] * len(tables),
        out_specs=[vmem] * len(tables),
        out_shape=[jax.ShapeDtypeStruct(table.shape, table.dtype) for table in tables],
        compiler_params=pltpu.CompilerParams(vmem_limit_bytes=VMEM_BYTES // 4),
        name="stage_tables",
    )(*tables)


def transform_kernel(radix, dests, units, place_ref, *rest):
    v_refs = rest[:dests]
    c_ref, tw_ref, gh_ref, gl_ref = rest[dests : dests + 4]
    out_refs = rest[dests + 5 : -4]
    held, split, prod, made = rest[-4:]
    spectra, _, rows, samples = held.shape
    taps = c_ref.shape[0]
    inner = samples // radix
    group = spectra * rows
    for shift in range(dests):
        held[place_ref[dests + shift]] = v_refs[shift][...]

    @pl.loop(0, radix)
    def _(phase):
        lane0 = pl.multiple_of(phase * inner, inner)
        row0 = pl.multiple_of(phase * group, group)
        for part in range(2):
            for sub in range(0, rows, ROWS16):
                blocks = [
                    held[b, part, pl.ds(sub, ROWS16), pl.ds(lane0, inner)].astype(jnp.float32)
                    for b in range(spectra)
                ]
                for s in range(spectra):
                    total = None
                    for b in range(max(0, s - taps + 1), s + 1):
                        term = c_ref[taps - 1 - s + b, pl.ds(phase, 1), :] * blocks[b]
                        total = term if total is None else total + term
                    high = total.astype(jnp.bfloat16)
                    low = (total - high.astype(jnp.float32)).astype(jnp.bfloat16)
                    at = pl.ds(pl.multiple_of(row0 + s * rows + sub, ROWS16), ROWS16)
                    split[at, part * inner : (part + 1) * inner] = high
                    split[at, (2 + part) * inner : (3 + part) * inner] = low

    @pl.loop(0, radix // 2)
    def _(pair):
        at = pl.ds(pl.multiple_of(pair * 2 * group, 2 * group), 2 * group)
        high = split[at, : 2 * inner]
        low = split[at, 2 * inner :]
        prod[at, :] = (
            jnp.dot(high, gh_ref[...], preferred_element_type=jnp.float32)
            + jnp.dot(high, gl_ref[...], preferred_element_type=jnp.float32)
            + jnp.dot(low, gh_ref[...], preferred_element_type=jnp.float32)
        )

    halves = radix // dests
    lane_cuts = inner // LANES

    @pl.loop(0, spectra)
    def _(s):
        for sub in range(0, rows, ROWS16):
            for cut in range(lane_cuts):
                lane = cut * LANES
                parts = []
                for phase in range(radix):
                    at = pl.ds(pl.multiple_of(phase * group + s * rows + sub, ROWS16), ROWS16)
                    yr = prod[at, lane : lane + LANES]
                    yi = prod[at, inner + lane : inner + lane + LANES]
                    cos_here = tw_ref[0, phase : phase + 1, lane : lane + LANES]
                    sin_here = tw_ref[1, phase : phase + 1, lane : lane + LANES]
                    if phase == 0:
                        parts.append((yr * cos_here, yi * cos_here))
                    else:
                        parts.append(
                            (yr * cos_here + yi * sin_here, yi * cos_here - yr * sin_here)
                        )
                for step, pair in enumerate(butterflies(parts)):
                    unit = step % halves * lane_cuts + cut
                    for part in range(2):
                        made[step // halves, unit, part, s, sub : sub + ROWS16, :] = pair[
                            part
                        ].astype(jnp.bfloat16)

    for shift in range(dests):
        for unit in range(units):
            out_refs[unit * dests + shift][...] = made[place_ref[shift], unit]


def transform_all(blocks, place, tables, radix, after):
    dests = len(blocks)
    _, rows, samples = blocks[0].shape
    spectra = dests
    inner = samples // radix
    units = samples // dests // LANES
    anywhere = pl.BlockSpec(memory_space=pl.ANY)
    vmem = pl.BlockSpec(memory_space=pltpu.VMEM)
    total = radix * spectra * rows
    made = pl.pallas_call(
        functools.partial(transform_kernel, radix, dests, units),
        grid_spec=pltpu.PrefetchScalarGridSpec(
            num_scalar_prefetch=1,
            grid=(),
            in_specs=[vmem] * (dests + 4) + [anywhere],
            out_specs=[vmem] * (units * dests),
            scratch_shapes=[
                pltpu.VMEM((spectra, 2, rows, samples), jnp.bfloat16),
                pltpu.VMEM((total, 4 * inner), jnp.bfloat16),
                pltpu.VMEM((total, 2 * inner), jnp.float32),
                pltpu.VMEM((dests, units, 2, spectra, rows, LANES), jnp.bfloat16),
            ],
        ),
        out_shape=[jax.ShapeDtypeStruct((2, spectra, rows, LANES), jnp.bfloat16)]
        * (units * dests),
        cost_estimate=pl.CostEstimate(
            flops=3 * 2 * total * 4 * inner * inner, bytes_accessed=6 << 20, transcendentals=0
        ),
        compiler_params=pltpu.CompilerParams(vmem_limit_bytes=VMEM_BYTES),
        name="filter_transform",
    )(
        place,
        *blocks,
        *tables,
        after,
    )
    return [made[unit * dests : (unit + 1) * dests] for unit in range(units)]


def join_kernel(count, where, place_ref, *rest):
    for shift in range(count):
        rest[-1][place_ref[where + shift]] = rest[shift][...]


def join(pieces, place, where, after):
    vmem = pl.BlockSpec(memory_space=pltpu.VMEM)
    return pl.pallas_call(
        functools.partial(join_kernel, len(pieces), where),
        grid_spec=pltpu.PrefetchScalarGridSpec(
            num_scalar_prefetch=1,
            grid=(),
            in_specs=[vmem] * len(pieces) + [pl.BlockSpec(memory_space=pl.ANY)],
            out_specs=vmem,
        ),
        out_shape=jax.ShapeDtypeStruct((len(pieces), *pieces[0].shape), pieces[0].dtype),
        compiler_params=pltpu.CompilerParams(vmem_limit_bytes=VMEM_BYTES // 4),
        name="join_pieces",
    )(place, *pieces, after)


def correlate_kernel(chunks, scale, table_ref, *rest):
    o_ref, token_ref, left = rest[-3:]
    half, senders, _, spectra, rows, lanes = rest[0].shape
    order = block_order(2 * half)
    blocks = len(order)
    slots = o_ref.shape[2]
    coarse = lanes // AVG
    side = senders * rows
    run = rows // chunks
    step = pl.program_id(0)

    @pl.when(step == 0)
    def _():
        token_ref[...] = jnp.zeros_like(token_ref)

    for c in range(coarse):

        @pl.when(step == c)
        def _(c=c):
            for at, block in enumerate(order):

                @pl.loop(0, senders)
                def _(sender, block=block, source=rest[at // half].at[at % half]):
                    for part in range(2):
                        for chunk in range(chunks):
                            row = pl.multiple_of(
                                part * side + (chunk * senders + sender) * run, run
                            )
                            left[block, pl.ds(row, run), :] = jnp.concatenate(
                                [
                                    source[
                                        sender,
                                        part,
                                        s,
                                        chunk * run : (chunk + 1) * run,
                                        c * AVG : (c + 1) * AVG,
                                    ]
                                    for s in range(spectra)
                                ],
                                axis=1,
                            )

    count = table_ref[2 * slots]
    for slot in range(slots):

        @pl.when(slot < count)
        def _(slot=slot):
            rows_of = left[table_ref[slot]]
            with_real, with_imag = [
                lax.dot_general(
                    rows_of,
                    left[table_ref[slots + slot], pl.ds(part * side, side), :],
                    (((1,), (1,)), ((), ())),
                    preferred_element_type=jnp.float32,
                )
                for part in range(2)
            ]
            o_ref[0, 0, slot] = (with_real[:side] + with_imag[side:]) * scale
            o_ref[1, 0, slot] = (with_real[side:] - with_imag[:side]) * scale

        @pl.when(slot >= count)
        def _(slot=slot):
            o_ref[:, 0, slot] = jnp.zeros((2, side, side), jnp.float32)


def correlate(table, gathered, unit, units, chunks, slots, vis):
    half, senders, _, spectra, rows, lanes = gathered[0].shape
    blocks = 2 * half
    coarse = lanes // AVG
    side = senders * rows
    scale = 1.0 / (AVG * spectra)
    in_specs = [
        pl.BlockSpec(
            part.shape, lambda c, t, n=part.ndim: (0,) * n, pipeline_mode=pl.Buffered(1)
        )
        for part in gathered
    ]
    args = [table, *gathered]
    aliases = {}
    if vis is not None:
        in_specs.append(pl.BlockSpec(memory_space=pl.ANY))
        args.append(vis)
        aliases = {len(args) - 1: 0}
    return pl.pallas_call(
        functools.partial(correlate_kernel, chunks, scale),
        grid_spec=pltpu.PrefetchScalarGridSpec(
            num_scalar_prefetch=1,
            grid=(coarse,),
            in_specs=in_specs,
            out_specs=[
                pl.BlockSpec(
                    (2, 1, slots, side, side), lambda c, t: (0, unit * coarse + c, 0, 0, 0)
                ),
                pl.BlockSpec((8, LANES), lambda c, t: (0, 0)),
            ],
            scratch_shapes=[
                pltpu.VMEM((blocks, 2 * side, spectra * AVG), jnp.bfloat16)
            ],
        ),
        out_shape=[
            jax.ShapeDtypeStruct((2, units * coarse, slots, side, side), jnp.float32),
            jax.ShapeDtypeStruct((8, LANES), jnp.float32),
        ],
        input_output_aliases=aliases,
        cost_estimate=pl.CostEstimate(flops=0, bytes_accessed=0, transcendentals=0),
        compiler_params=pltpu.CompilerParams(vmem_limit_bytes=VMEM_BYTES),
        name="correlate_tiles",
    )(*args)


def places(count):
    steps = np.arange(count, dtype=np.int32)
    index = lax.axis_index("ft").astype(jnp.int32)
    return jnp.concatenate([(index + steps) % count, (index + count - steps) % count])


def spread(pieces):
    count = len(pieces)
    return [pieces[0]] + [
        lax.ppermute(pieces[d], "ft", [(i, (i + d) % count) for i in range(count)])
        for d in range(1, count)
    ]


def exchange(own, bit):
    count = lax.axis_size("bl")
    return lax.ppermute(own, "bl", [(i, i ^ bit) for i in range(count)])


def gather_blocks(own, partner, after):
    bit = lax.axis_size("bl") // 2
    held, other = own[None], partner[None]
    while bit > 1:
        both = join([held, other], np.arange(2, dtype=np.int32), 0, after)
        held = both.reshape(-1, *own.shape)
        bit //= 2
        other = exchange(held, bit)
    return held, other


def block_order(count):
    order, bit = [0], count // 2
    while bit:
        order += [r ^ bit for r in order]
        bit //= 2
    return order


def tile_tables(block_ids, tile_owner):
    block_count = lax.axis_size("bl")
    tile_count = block_count * (block_count + 1) // 2
    slot_cap = 2 * tile_count // block_count
    pairs = [(i, j) for i in range(block_count) for j in range(i, block_count)]
    row_table = np.array([i for i, _ in pairs], np.int32)
    col_table = np.array([j for _, j in pairs], np.int32)
    mine = (tile_owner == lax.axis_index("bl")).astype(jnp.int32)
    earlier = np.tril(np.ones((tile_count, tile_count), np.int32), -1)
    rank = jnp.sum(earlier * mine[None, :], axis=1)
    labels = np.arange(block_count, dtype=np.int32)
    shard_of = jnp.sum(jnp.where(block_ids[None, :] == labels[:, None], labels[None, :], 0), axis=1)
    row_shard = jnp.sum(
        jnp.where(row_table[:, None] == labels[None, :], shard_of[None, :], 0), axis=1
    )
    col_shard = jnp.sum(
        jnp.where(col_table[:, None] == labels[None, :], shard_of[None, :], 0), axis=1
    )
    here = (mine[None, :] == 1) & (rank[None, :] == np.arange(slot_cap, dtype=np.int32)[:, None])
    rows = jnp.sum(jnp.where(here, row_shard[None, :], 0), axis=1)
    cols = jnp.sum(jnp.where(here, col_shard[None, :], 0), axis=1)
    index = lax.axis_index("bl")
    table = jnp.concatenate(
        [rows ^ index, cols ^ index, jnp.sum(mine, keepdims=True)]
    ).astype(jnp.int32)
    return table, slot_cap


def takes_kernels(mesh, voltages, coefs):
    dests = mesh.shape["ft"]
    blocks = mesh.shape["bl"]
    inputs = voltages.shape[2] // mesh.shape["bl"]
    per_dev = voltages.shape[1] // (mesh.shape["grp"] * dests)
    chan_count = coefs.shape[1]
    radix = chan_count // MXU
    return (
        per_dev == chan_count
        and chan_count % MXU == 0
        and radix & (radix - 1) == 0
        and radix % dests == 0
        and radix <= 8
        and blocks & (blocks - 1) == 0
        and blocks > 1
        and inputs % LANES == 0
        and LANES % dests == 0
        and (LANES // dests) % ROWS16 == 0
        and (dests * AVG) % LANES == 0
    )


def per_device_kernels(voltages, coefs, block_ids, tile_owner):
    dests = lax.axis_size("ft")
    taps, chan_count = coefs.shape
    radix = chan_count // MXU
    chunks = voltages.shape[2] // LANES
    coef_table = coefs.reshape(taps, MXU, radix).transpose(0, 2, 1)
    place = places(dests)
    table, slot_cap = tile_tables(block_ids, tile_owner)
    tables = stage(coef_table, twiddle_tables(radix, MXU), *matrix_tables(MXU))
    arrived = spread(pack(voltages, place, dests, radix))
    made = transform_all(arrived, place, tables, radix, table)
    half = lax.axis_size("bl") // 2
    partners, tokens, vis = [], [], None
    for unit in range(len(made) + 1):
        if unit < len(made):
            parts = made[unit]
            if unit > 1:
                first = (partners[unit - 2][1], arrived)
                parts, _ = lax.optimization_barrier((parts, first))
            arrived = spread(parts)
            own = join(arrived, place, dests, tokens[unit - 2] if unit > 1 else table)
            partners.append((own, exchange(own, half)))
        if unit > 0:
            gathered = gather_blocks(
                *partners[unit - 1], partners[unit][0] if unit < len(made) else tokens[-1]
            )
            vis, token = correlate(
                table, gathered, unit - 1, len(made), chunks, slot_cap, vis
            )
            tokens.append(token)
    return vis


def tile_product(row_part, col_part, norm_scale):
    products = jnp.einsum(
        "pscax,qscay->cpqxy", row_part, col_part, preferred_element_type=jnp.float32
    )
    real_part = products[:, 0, 0] + products[:, 1, 1]
    imag_part = products[:, 1, 0] - products[:, 0, 1]
    return jnp.stack([real_part, imag_part]) * norm_scale


def dft_tables(order_len):
    steps_one = jnp.arange(order_len, dtype=jnp.int32)
    phase_grid = steps_one[:, None] * steps_one[None, :] % order_len
    angles = phase_grid.astype(jnp.float32) * (2.0 * math.pi / order_len)
    return (jnp.cos(angles), jnp.sin(angles))


def transform(filtered):
    per_dev = filtered.shape[1]
    chan_count = filtered.shape[2]
    rows_here = filtered.shape[3]
    outer_len = math.isqrt(chan_count)
    while chan_count % outer_len != 0:
        outer_len = outer_len - 1
    inner_len = chan_count // outer_len
    highest = lax.Precision.HIGHEST
    reshaped = filtered.reshape(2, per_dev, outer_len, inner_len, rows_here)
    real_in = reshaped[0]
    imag_in = reshaped[1]
    cos_outer, sin_outer = dft_tables(outer_len)
    section_re = jnp.einsum("snkb,nm->smkb", real_in, cos_outer, precision=highest) + jnp.einsum(
        "snkb,nm->smkb", imag_in, sin_outer, precision=highest
    )
    section_im = jnp.einsum("snkb,nm->smkb", imag_in, cos_outer, precision=highest) - jnp.einsum(
        "snkb,nm->smkb", real_in, sin_outer, precision=highest
    )
    twiddle_grid = (
        jnp.arange(outer_len, dtype=jnp.int32)[:, None]
        * jnp.arange(inner_len, dtype=jnp.int32)[None, :]
        % chan_count
    )
    twiddle_angles = twiddle_grid.astype(jnp.float32) * (2.0 * math.pi / chan_count)
    cos_twiddle = jnp.cos(twiddle_angles)[None, :, :, None]
    sin_twiddle = jnp.sin(twiddle_angles)[None, :, :, None]
    rot_re = section_re * cos_twiddle + section_im * sin_twiddle
    rot_im = section_im * cos_twiddle - section_re * sin_twiddle
    cos_inner, sin_inner = dft_tables(inner_len)
    final_re = jnp.einsum("smkb,kq->sqmb", rot_re, cos_inner, precision=highest) + jnp.einsum(
        "smkb,kq->sqmb", rot_im, sin_inner, precision=highest
    )
    final_im = jnp.einsum("smkb,kq->sqmb", rot_im, cos_inner, precision=highest) - jnp.einsum(
        "smkb,kq->sqmb", rot_re, sin_inner, precision=highest
    )
    stacked = jnp.stack([final_re, final_im]).reshape(2, per_dev, chan_count, rows_here)
    return (stacked * (1.0 / math.sqrt(chan_count))).astype(jnp.bfloat16)


def apply_taps(window, coef_part, taps_count, out_len):
    filtered = jnp.zeros((2, out_len, window.shape[2], window.shape[3]), jnp.float32)
    for tap_index in range(taps_count):
        filtered = filtered + coef_part[tap_index][None, None, :, None] * window[
            :, tap_index : tap_index + out_len
        ].astype(jnp.float32)
    return filtered


def per_device(voltages, coefs, block_ids, tile_owner):
    taps_count = coefs.shape[0]
    chan_count = coefs.shape[1]
    rows_here = voltages.shape[2]
    per_dev = voltages.shape[1] // chan_count
    volt_blocks = voltages.reshape(2, per_dev, chan_count, rows_here)
    phase_block = lax.all_to_all(volt_blocks, "ft", split_axis=2, concat_axis=1, tiled=True)
    spectra_count = phase_block.shape[1]
    phase_here = phase_block.shape[2]
    coef_part = lax.dynamic_slice_in_dim(coefs, lax.axis_index("ft") * phase_here, phase_here, 1)
    zero_front = jnp.zeros((2, taps_count - 1, phase_here, rows_here), phase_block.dtype)
    long_window = jnp.concatenate([zero_front, phase_block], axis=1)
    phase_filtered = apply_taps(long_window, coef_part, taps_count, spectra_count)
    filtered = lax.all_to_all(phase_filtered, "ft", split_axis=1, concat_axis=2, tiled=True)
    spectra = transform(filtered)
    turned = lax.all_to_all(spectra, "ft", split_axis=2, concat_axis=1, tiled=True)
    spectra_all = turned.shape[1]
    chan_here = turned.shape[2]
    coarse_here = chan_here // AVG
    coarse_view = turned.reshape(2, spectra_all, coarse_here, AVG, rows_here)
    norm_scale = 1.0 / (AVG * spectra_all)
    block_count = lax.axis_size("bl")
    my_index = lax.axis_index("bl")
    tile_count = block_count * (block_count + 1) // 2
    slot_cap = 2 * tile_count // block_count
    row_table = jnp.asarray(
        np.array(
            [
                first_id
                for first_id in range(block_count)
                for second_id in range(first_id, block_count)
            ],
            dtype=np.int32,
        )
    )
    col_table = jnp.asarray(
        np.array(
            [
                second_id
                for first_id in range(block_count)
                for second_id in range(first_id, block_count)
            ],
            dtype=np.int32,
        )
    )
    tile_pos = jnp.arange(tile_count, dtype=jnp.int32)
    same_owner = tile_owner[None, :] == tile_owner[:, None]
    before_mask = tile_pos[None, :] < tile_pos[:, None]
    slot_rank = jnp.sum((same_owner & before_mask).astype(jnp.int32), axis=1)
    labels = jnp.arange(block_count, dtype=jnp.int32)
    shard_of = jnp.sum(jnp.where(block_ids[None, :] == labels[:, None], labels[None, :], 0), axis=1)
    gathered = lax.all_gather(coarse_view[None], "bl", axis=0, tiled=True)
    mine_mask = tile_owner == my_index
    own_count = jnp.sum(mine_mask.astype(jnp.int32))
    slot_steps = jnp.arange(slot_cap, dtype=jnp.int32)
    slot_tile = jnp.sum(
        jnp.where(
            mine_mask[None, :] & (slot_rank[None, :] == slot_steps[:, None]), tile_pos[None, :], 0
        ),
        axis=1,
    )

    def one_tile(slot_pos, result_tiles):
        tile_id = slot_tile[slot_pos]
        row_block = gathered[shard_of[row_table[tile_id]]]
        col_block = gathered[shard_of[col_table[tile_id]]]
        tile = tile_product(row_block, col_block, norm_scale)
        return lax.dynamic_update_slice(result_tiles, tile[:, :, None], (0, 0, slot_pos, 0, 0))

    empty_tiles = jnp.zeros((2, coarse_here, slot_cap, rows_here, rows_here), jnp.float32)
    return lax.fori_loop(0, own_count, one_tile, empty_tiles)


def solution(mesh):
    def correlator(voltages, coefs, block_ids, tile_owner):
        fits = takes_kernels(mesh, voltages, coefs)
        return jax.shard_map(
            per_device_kernels if fits else per_device,
            mesh=mesh,
            in_specs=(P(None, ("grp", "ft"), "bl"), P(), P(), P("grp")),
            out_specs=P(None, ("grp", "ft"), "bl", None, None),
            check_vma=False,
        )(voltages, coefs, block_ids, tile_owner)

    return correlator
```

```python
import functools
import math

import jax
import jax.numpy as jnp
import ml_dtypes
import numpy as np
from jax import lax
from jax.experimental import pallas as pl
from jax.experimental.pallas import tpu as pltpu
from jax.sharding import PartitionSpec as P

AVG = 64
MXU = 256
LANES = 128
ROWS16 = 16
VMEM_BYTES = 48 * 1024 * 1024


def split_bf16(table):
    high = table.astype(ml_dtypes.bfloat16)
    low = (table - high.astype(np.float64)).astype(ml_dtypes.bfloat16)
    return high, low


def matrix_tables(inner_len):
    steps = np.arange(inner_len)
    angles = 2.0 * np.pi * (np.outer(steps, steps) % inner_len) / inner_len
    cos_part, sin_part = np.cos(angles), np.sin(angles)
    high, low = split_bf16(np.block([[cos_part, -sin_part], [sin_part, cos_part]]))
    return np.concatenate([high, high, low])


def twiddle_tables(radix, inner_len):
    chan_count = radix * inner_len
    angles = 2.0 * np.pi * np.outer(np.arange(radix), np.arange(inner_len)) / chan_count
    scale = 1.0 / math.sqrt(chan_count)
    return np.stack([np.cos(angles) * scale, np.sin(angles) * scale]).astype(np.float32)


def rotate(real, imag, step, count):
    step = step % count
    if step == 0:
        return real, imag
    if 4 * step == count:
        return imag, -real
    if 2 * step == count:
        return -real, -imag
    if 4 * step == 3 * count:
        return -imag, real
    cos_step = math.cos(2.0 * math.pi * step / count)
    sin_step = math.sin(2.0 * math.pi * step / count)
    if 8 * step == count:
        return cos_step * (real + imag), cos_step * (imag - real)
    return cos_step * real + sin_step * imag, cos_step * imag - sin_step * real


def butterflies(parts):
    count = len(parts)
    if count == 1:
        return parts
    half = count // 2
    sums, diffs = [], []
    for k in range(half):
        (ar, ai), (br, bi) = parts[k], parts[k + half]
        sums.append((ar + br, ai + bi))
        diffs.append(rotate(ar - br, ai - bi, k, count))
    even, odd = butterflies(sums), butterflies(diffs)
    out = []
    for k in range(half):
        out += [even[k], odd[k]]
    return out


def pack_kernel(radix, place_ref, v_ref, *rest):
    o_refs, (wide, turned) = rest[:-2], rest[-2:]
    dests, rows, samples = turned.shape
    inner = samples // radix
    wide[...] = v_ref[0].astype(jnp.float32)
    for phase in range(radix):
        part = wide[pl.ds(phase, inner, stride=radix), :].T.astype(jnp.bfloat16)
        for dest in range(dests):
            turned[dest, :, phase * inner : (phase + 1) * inner] = part[
                dest * rows : (dest + 1) * rows
            ]
    for shift in range(dests):
        o_refs[shift][0] = turned[place_ref[shift]]


def pack(voltages, place, dests, radix):
    _, samples, inputs = voltages.shape
    chunks = inputs // LANES
    rows = LANES // dests
    return pl.pallas_call(
        functools.partial(pack_kernel, radix),
        grid_spec=pltpu.PrefetchScalarGridSpec(
            num_scalar_prefetch=1,
            grid=(2, chunks),
            in_specs=[pl.BlockSpec((1, samples, LANES), lambda p, h, t: (p, 0, h))],
            out_specs=[pl.BlockSpec((1, rows, samples), lambda p, h, t: (p, h, 0))] * dests,
            scratch_shapes=[
                pltpu.VMEM((samples, LANES), jnp.float32),
                pltpu.VMEM((dests, rows, samples), jnp.bfloat16),
            ],
        ),
        out_shape=[jax.ShapeDtypeStruct((2, chunks * rows, samples), jnp.bfloat16)] * dests,
        compiler_params=pltpu.CompilerParams(vmem_limit_bytes=VMEM_BYTES),
        name="pack_inputs",
    )(place, voltages)


def stage_kernel(*refs):
    half = len(refs) // 2
    for source, target in zip(refs[:half], refs[half:]):
        target[...] = source[...]


def stage(*tables):
    vmem = pl.BlockSpec(memory_space=pltpu.VMEM)
    return pl.pallas_call(
        stage_kernel,
        in_specs=[vmem] * len(tables),
        out_specs=[vmem] * len(tables),
        out_shape=[jax.ShapeDtypeStruct(table.shape, table.dtype) for table in tables],
        compiler_params=pltpu.CompilerParams(vmem_limit_bytes=VMEM_BYTES // 4),
        name="stage_tables",
    )(*tables)


def transform_kernel(radix, dests, units, place_ref, *rest):
    v_refs = rest[:dests]
    c_ref, tw_ref, g_ref = rest[dests : dests + 3]
    out_refs = rest[dests + 4 : -4]
    held, split, prod, made = rest[-4:]
    spectra, _, rows, samples = held.shape
    taps = c_ref.shape[0]
    inner = samples // radix
    group = spectra * rows
    for shift in range(dests):
        held[place_ref[dests + shift]] = v_refs[shift][...]

    @pl.loop(0, radix)
    def _(phase):
        lane0 = pl.multiple_of(phase * inner, inner)
        row0 = pl.multiple_of(phase * group, group)
        for part in range(2):
            for sub in range(0, rows, ROWS16):
                blocks = [
                    held[b, part, pl.ds(sub, ROWS16), pl.ds(lane0, inner)].astype(jnp.float32)
                    for b in range(spectra)
                ]
                for s in range(spectra):
                    total = None
                    for b in range(max(0, s - taps + 1), s + 1):
                        term = c_ref[taps - 1 - s + b, pl.ds(phase, 1), :] * blocks[b]
                        total = term if total is None else total + term
                    high = total.astype(jnp.bfloat16)
                    low = (total - high.astype(jnp.float32)).astype(jnp.bfloat16)
                    at = pl.ds(pl.multiple_of(row0 + s * rows + sub, ROWS16), ROWS16)
                    split[at, part * inner : (part + 1) * inner] = high
                    split[at, (2 + part) * inner : (3 + part) * inner] = low

    @pl.loop(0, radix // 2)
    def _(pair):
        at = pl.ds(pl.multiple_of(pair * 2 * group, 2 * group), 2 * group)
        high = split[at, : 2 * inner]
        line = jnp.concatenate([high, split[at, 2 * inner :], high], axis=1)
        prod[at, :] = jnp.dot(line, g_ref[...], preferred_element_type=jnp.float32)

    halves = radix // dests
    lane_cuts = inner // LANES

    @pl.loop(0, spectra)
    def _(s):
        for sub in range(0, rows, ROWS16):
            for cut in range(lane_cuts):
                lane = cut * LANES
                parts = []
                for phase in range(radix):
                    at = pl.ds(pl.multiple_of(phase * group + s * rows + sub, ROWS16), ROWS16)
                    yr = prod[at, lane : lane + LANES]
                    yi = prod[at, inner + lane : inner + lane + LANES]
                    cos_here = tw_ref[0, phase : phase + 1, lane : lane + LANES]
                    sin_here = tw_ref[1, phase : phase + 1, lane : lane + LANES]
                    if phase == 0:
                        parts.append((yr * cos_here, yi * cos_here))
                    else:
                        parts.append(
                            (yr * cos_here + yi * sin_here, yi * cos_here - yr * sin_here)
                        )
                for step, pair in enumerate(butterflies(parts)):
                    unit = step % halves * lane_cuts + cut
                    for part in range(2):
                        made[step // halves, unit, part, s, sub : sub + ROWS16, :] = pair[
                            part
                        ].astype(jnp.bfloat16)

    for shift in range(dests):
        for unit in range(units):
            out_refs[unit * dests + shift][...] = made[place_ref[shift], unit]


def transform_all(blocks, place, tables, radix, after):
    dests = len(blocks)
    _, rows, samples = blocks[0].shape
    spectra = dests
    inner = samples // radix
    units = samples // dests // LANES
    anywhere = pl.BlockSpec(memory_space=pl.ANY)
    vmem = pl.BlockSpec(memory_space=pltpu.VMEM)
    total = radix * spectra * rows
    made = pl.pallas_call(
        functools.partial(transform_kernel, radix, dests, units),
        grid_spec=pltpu.PrefetchScalarGridSpec(
            num_scalar_prefetch=1,
            grid=(),
            in_specs=[vmem] * (dests + 3) + [anywhere],
            out_specs=[vmem] * (units * dests),
            scratch_shapes=[
                pltpu.VMEM((spectra, 2, rows, samples), jnp.bfloat16),
                pltpu.VMEM((total, 4 * inner), jnp.bfloat16),
                pltpu.VMEM((total, 2 * inner), jnp.float32),
                pltpu.VMEM((dests, units, 2, spectra, rows, LANES), jnp.bfloat16),
            ],
        ),
        out_shape=[jax.ShapeDtypeStruct((2, spectra, rows, LANES), jnp.bfloat16)]
        * (units * dests),
        cost_estimate=pl.CostEstimate(
            flops=3 * 2 * total * 4 * inner * inner, bytes_accessed=6 << 20, transcendentals=0
        ),
        compiler_params=pltpu.CompilerParams(vmem_limit_bytes=VMEM_BYTES),
        name="filter_transform",
    )(
        place,
        *blocks,
        *tables,
        after,
    )
    return [made[unit * dests : (unit + 1) * dests] for unit in range(units)]


def join(pieces, place, before, after):
    count = len(pieces)
    vmem = pl.BlockSpec(memory_space=pltpu.VMEM)
    shapes = [jax.ShapeDtypeStruct((count, *pieces[0].shape), pieces[0].dtype)]
    if before:
        shapes.append(jax.ShapeDtypeStruct((2, *before[0].shape), before[0].dtype))

    def kernel(place_ref, *rest):
        ins, outs = rest[: count + len(before)], rest[count + len(before) + 1 :]
        for shift in range(count):
            outs[0][place_ref[count + shift]] = ins[shift][...]
        for at in range(len(before)):
            outs[1][at] = ins[count + at][...]

    return pl.pallas_call(
        kernel,
        grid_spec=pltpu.PrefetchScalarGridSpec(
            num_scalar_prefetch=1,
            grid=(),
            in_specs=[vmem] * (count + len(before)) + [pl.BlockSpec(memory_space=pl.ANY)],
            out_specs=[vmem] * len(shapes),
        ),
        out_shape=shapes,
        compiler_params=pltpu.CompilerParams(vmem_limit_bytes=VMEM_BYTES // 4),
        name="join_pieces",
    )(place, *pieces, *before, after)


def pair(own, other, after):
    def kernel(own_ref, other_ref, _, out_ref):
        out_ref[0] = own_ref[...]
        out_ref[1] = other_ref[...]

    vmem = pl.BlockSpec(memory_space=pltpu.VMEM)
    return pl.pallas_call(
        kernel,
        in_specs=[vmem, vmem, pl.BlockSpec(memory_space=pl.ANY)],
        out_specs=vmem,
        out_shape=jax.ShapeDtypeStruct((2, *own.shape), own.dtype),
        compiler_params=pltpu.CompilerParams(vmem_limit_bytes=VMEM_BYTES // 4),
        name="pair_blocks",
    )(own, other, after)


def correlate_kernel(chunks, scale, first, table_ref, low_ref, high_ref, *rest):
    o_ref, token_ref, left, tiles, empty, sems = rest[-6:]
    half, senders, _, spectra, rows, lanes = low_ref.shape
    order = block_order(2 * half)
    slots = o_ref.shape[2]
    coarse = lanes // AVG
    side = senders * rows
    run = rows // chunks
    count = table_ref[2 * slots]
    token_ref[...] = jnp.zeros_like(token_ref)
    empty[...] = jnp.zeros_like(empty)

    def copy_out(source, c, slot):
        return pltpu.make_async_copy(source, o_ref.at[:, first + c, slot], sems.at[c, slot])

    for slot in range(slots):

        @pl.when(slot >= count)
        def _(slot=slot):
            for c in range(coarse):
                copy_out(empty, c, slot).start()

    for at, block in enumerate(order):
        source = (low_ref, high_ref)[at // half].at[at % half]

        @pl.loop(0, senders)
        def _(sender, block=block, source=source):
            for part in range(2):
                for chunk in range(chunks):
                    row = pl.multiple_of(part * side + (chunk * senders + sender) * run, run)
                    pieces = [
                        source[sender, part, s, chunk * run : (chunk + 1) * run]
                        for s in range(spectra)
                    ]
                    for c in range(coarse):
                        left[c, block, pl.ds(row, run), :] = jnp.concatenate(
                            [piece[:, c * AVG : (c + 1) * AVG] for piece in pieces], axis=1
                        )

    for slot in range(slots):

        @pl.when(slot < count)
        def _(slot=slot):
            for c in range(coarse):
                rows_of = left[c, table_ref[slot]]
                with_real, with_imag = [
                    lax.dot_general(
                        rows_of,
                        left[c, table_ref[slots + slot], pl.ds(part * side, side), :],
                        (((1,), (1,)), ((), ())),
                        preferred_element_type=jnp.float32,
                    )
                    for part in range(2)
                ]
                tiles[c, slot, 0] = (with_real[:side] + with_imag[side:]) * scale
                tiles[c, slot, 1] = (with_real[side:] - with_imag[:side]) * scale
                copy_out(tiles.at[c, slot], c, slot).start()

    for slot in range(slots):
        for c in range(coarse):
            copy_out(empty, c, slot).wait()


def correlate(table, gathered, unit, units, chunks, slots, vis):
    half, senders, _, spectra, rows, lanes = gathered[0].shape
    coarse = lanes // AVG
    side = senders * rows
    vmem = pl.BlockSpec(memory_space=pltpu.VMEM)
    anywhere = pl.BlockSpec(memory_space=pl.ANY)
    args = [table, *gathered]
    aliases = {}
    if vis is not None:
        args.append(vis)
        aliases = {len(args) - 1: 0}
    return pl.pallas_call(
        functools.partial(correlate_kernel, chunks, 1.0 / (AVG * spectra), unit * coarse),
        grid_spec=pltpu.PrefetchScalarGridSpec(
            num_scalar_prefetch=1,
            grid=(),
            in_specs=[vmem, vmem] + [anywhere] * (len(args) - 3),
            out_specs=[anywhere, vmem],
            scratch_shapes=[
                pltpu.VMEM((coarse, 2 * half, 2 * side, spectra * AVG), jnp.bfloat16),
                pltpu.VMEM((coarse, slots, 2, side, side), jnp.float32),
                pltpu.VMEM((2, side, side), jnp.float32),
                pltpu.SemaphoreType.DMA((coarse, slots)),
            ],
        ),
        out_shape=[
            jax.ShapeDtypeStruct((2, units * coarse, slots, side, side), jnp.float32),
            jax.ShapeDtypeStruct((8, LANES), jnp.float32),
        ],
        input_output_aliases=aliases,
        cost_estimate=pl.CostEstimate(flops=0, bytes_accessed=0, transcendentals=0),
        compiler_params=pltpu.CompilerParams(vmem_limit_bytes=VMEM_BYTES),
        name="correlate_tiles",
    )(*args)


def places(count):
    steps = np.arange(count, dtype=np.int32)
    index = lax.axis_index("ft").astype(jnp.int32)
    return jnp.concatenate([(index + steps) % count, (index + count - steps) % count])


def spread(pieces):
    count = len(pieces)
    return [pieces[0]] + [
        lax.ppermute(pieces[d], "ft", [(i, (i + d) % count) for i in range(count)])
        for d in range(1, count)
    ]


def exchange(own, bit):
    count = lax.axis_size("bl")
    return lax.ppermute(own, "bl", [(i, i ^ bit) for i in range(count)])


def gather_blocks(held, after):
    bit = lax.axis_size("bl") // 4
    other = exchange(held, bit)
    while bit > 1:
        bit //= 2
        held = pair(held, other, after).reshape(-1, *held.shape[1:])
        other = exchange(held, bit)
    return held, other


def block_order(count):
    order, bit = [0], count // 2
    while bit:
        order += [r ^ bit for r in order]
        bit //= 2
    return order


def tile_tables(block_ids, tile_owner):
    block_count = lax.axis_size("bl")
    tile_count = block_count * (block_count + 1) // 2
    slot_cap = 2 * tile_count // block_count
    pairs = [(i, j) for i in range(block_count) for j in range(i, block_count)]
    row_table = np.array([i for i, _ in pairs], np.int32)
    col_table = np.array([j for _, j in pairs], np.int32)
    mine = (tile_owner == lax.axis_index("bl")).astype(jnp.int32)
    earlier = np.tril(np.ones((tile_count, tile_count), np.int32), -1)
    rank = jnp.sum(earlier * mine[None, :], axis=1)
    labels = np.arange(block_count, dtype=np.int32)
    shard_of = jnp.sum(jnp.where(block_ids[None, :] == labels[:, None], labels[None, :], 0), axis=1)
    row_shard = jnp.sum(
        jnp.where(row_table[:, None] == labels[None, :], shard_of[None, :], 0), axis=1
    )
    col_shard = jnp.sum(
        jnp.where(col_table[:, None] == labels[None, :], shard_of[None, :], 0), axis=1
    )
    here = (mine[None, :] == 1) & (rank[None, :] == np.arange(slot_cap, dtype=np.int32)[:, None])
    rows = jnp.sum(jnp.where(here, row_shard[None, :], 0), axis=1)
    cols = jnp.sum(jnp.where(here, col_shard[None, :], 0), axis=1)
    index = lax.axis_index("bl")
    table = jnp.concatenate(
        [rows ^ index, cols ^ index, jnp.sum(mine, keepdims=True)]
    ).astype(jnp.int32)
    return table, slot_cap


def takes_kernels(mesh, voltages, coefs):
    dests = mesh.shape["ft"]
    blocks = mesh.shape["bl"]
    inputs = voltages.shape[2] // mesh.shape["bl"]
    per_dev = voltages.shape[1] // (mesh.shape["grp"] * dests)
    chan_count = coefs.shape[1]
    radix = chan_count // MXU
    return (
        per_dev == chan_count
        and chan_count % MXU == 0
        and radix & (radix - 1) == 0
        and radix % dests == 0
        and radix <= 8
        and blocks & (blocks - 1) == 0
        and blocks > 2
        and inputs % LANES == 0
        and LANES % dests == 0
        and (LANES // dests) % ROWS16 == 0
        and (dests * AVG) % LANES == 0
    )


def per_device_kernels(voltages, coefs, block_ids, tile_owner):
    dests = lax.axis_size("ft")
    taps, chan_count = coefs.shape
    radix = chan_count // MXU
    chunks = voltages.shape[2] // LANES
    coef_table = coefs.reshape(taps, MXU, radix).transpose(0, 2, 1)
    place = places(dests)
    table, slot_cap = tile_tables(block_ids, tile_owner)
    tables = stage(coef_table, twiddle_tables(radix, MXU), matrix_tables(MXU))
    arrived = spread(pack(voltages, place, dests, radix))
    made = transform_all(arrived, place, tables, radix, table)
    half = lax.axis_size("bl") // 2
    units = len(made)
    own, other, arrived, tokens, vis = None, None, None, [], None
    for unit in range(units + 1):
        held = None
        if unit < units:
            parts = made[unit]
            if unit > 1:
                parts, _ = lax.optimization_barrier((parts, arrived))
            arrived = spread(parts)
            after = tokens[-1] if tokens else table
            if unit > 0:
                own, held = join(arrived, place, (own, other), after)
            else:
                (own,) = join(arrived, place, (), after)
            other = exchange(own, half)
        else:
            held = pair(own, other, tokens[-1])
        if unit > 0:
            gathered = gather_blocks(held, table)
            vis, token = correlate(table, gathered, unit - 1, units, chunks, slot_cap, vis)
            tokens.append(token)
    return vis


def tile_product(row_part, col_part, norm_scale):
    products = jnp.einsum(
        "pscax,qscay->cpqxy", row_part, col_part, preferred_element_type=jnp.float32
    )
    real_part = products[:, 0, 0] + products[:, 1, 1]
    imag_part = products[:, 1, 0] - products[:, 0, 1]
    return jnp.stack([real_part, imag_part]) * norm_scale


def dft_tables(order_len):
    steps_one = jnp.arange(order_len, dtype=jnp.int32)
    phase_grid = steps_one[:, None] * steps_one[None, :] % order_len
    angles = phase_grid.astype(jnp.float32) * (2.0 * math.pi / order_len)
    return (jnp.cos(angles), jnp.sin(angles))


def transform(filtered):
    per_dev = filtered.shape[1]
    chan_count = filtered.shape[2]
    rows_here = filtered.shape[3]
    outer_len = math.isqrt(chan_count)
    while chan_count % outer_len != 0:
        outer_len = outer_len - 1
    inner_len = chan_count // outer_len
    highest = lax.Precision.HIGHEST
    reshaped = filtered.reshape(2, per_dev, outer_len, inner_len, rows_here)
    real_in = reshaped[0]
    imag_in = reshaped[1]
    cos_outer, sin_outer = dft_tables(outer_len)
    section_re = jnp.einsum("snkb,nm->smkb", real_in, cos_outer, precision=highest) + jnp.einsum(
        "snkb,nm->smkb", imag_in, sin_outer, precision=highest
    )
    section_im = jnp.einsum("snkb,nm->smkb", imag_in, cos_outer, precision=highest) - jnp.einsum(
        "snkb,nm->smkb", real_in, sin_outer, precision=highest
    )
    twiddle_grid = (
        jnp.arange(outer_len, dtype=jnp.int32)[:, None]
        * jnp.arange(inner_len, dtype=jnp.int32)[None, :]
        % chan_count
    )
    twiddle_angles = twiddle_grid.astype(jnp.float32) * (2.0 * math.pi / chan_count)
    cos_twiddle = jnp.cos(twiddle_angles)[None, :, :, None]
    sin_twiddle = jnp.sin(twiddle_angles)[None, :, :, None]
    rot_re = section_re * cos_twiddle + section_im * sin_twiddle
    rot_im = section_im * cos_twiddle - section_re * sin_twiddle
    cos_inner, sin_inner = dft_tables(inner_len)
    final_re = jnp.einsum("smkb,kq->sqmb", rot_re, cos_inner, precision=highest) + jnp.einsum(
        "smkb,kq->sqmb", rot_im, sin_inner, precision=highest
    )
    final_im = jnp.einsum("smkb,kq->sqmb", rot_im, cos_inner, precision=highest) - jnp.einsum(
        "smkb,kq->sqmb", rot_re, sin_inner, precision=highest
    )
    stacked = jnp.stack([final_re, final_im]).reshape(2, per_dev, chan_count, rows_here)
    return (stacked * (1.0 / math.sqrt(chan_count))).astype(jnp.bfloat16)


def apply_taps(window, coef_part, taps_count, out_len):
    filtered = jnp.zeros((2, out_len, window.shape[2], window.shape[3]), jnp.float32)
    for tap_index in range(taps_count):
        filtered = filtered + coef_part[tap_index][None, None, :, None] * window[
            :, tap_index : tap_index + out_len
        ].astype(jnp.float32)
    return filtered


def per_device(voltages, coefs, block_ids, tile_owner):
    taps_count = coefs.shape[0]
    chan_count = coefs.shape[1]
    rows_here = voltages.shape[2]
    per_dev = voltages.shape[1] // chan_count
    volt_blocks = voltages.reshape(2, per_dev, chan_count, rows_here)
    phase_block = lax.all_to_all(volt_blocks, "ft", split_axis=2, concat_axis=1, tiled=True)
    spectra_count = phase_block.shape[1]
    phase_here = phase_block.shape[2]
    coef_part = lax.dynamic_slice_in_dim(coefs, lax.axis_index("ft") * phase_here, phase_here, 1)
    zero_front = jnp.zeros((2, taps_count - 1, phase_here, rows_here), phase_block.dtype)
    long_window = jnp.concatenate([zero_front, phase_block], axis=1)
    phase_filtered = apply_taps(long_window, coef_part, taps_count, spectra_count)
    filtered = lax.all_to_all(phase_filtered, "ft", split_axis=1, concat_axis=2, tiled=True)
    spectra = transform(filtered)
    turned = lax.all_to_all(spectra, "ft", split_axis=2, concat_axis=1, tiled=True)
    spectra_all = turned.shape[1]
    chan_here = turned.shape[2]
    coarse_here = chan_here // AVG
    coarse_view = turned.reshape(2, spectra_all, coarse_here, AVG, rows_here)
    norm_scale = 1.0 / (AVG * spectra_all)
    block_count = lax.axis_size("bl")
    my_index = lax.axis_index("bl")
    tile_count = block_count * (block_count + 1) // 2
    slot_cap = 2 * tile_count // block_count
    row_table = jnp.asarray(
        np.array(
            [
                first_id
                for first_id in range(block_count)
                for second_id in range(first_id, block_count)
            ],
            dtype=np.int32,
        )
    )
    col_table = jnp.asarray(
        np.array(
            [
                second_id
                for first_id in range(block_count)
                for second_id in range(first_id, block_count)
            ],
            dtype=np.int32,
        )
    )
    tile_pos = jnp.arange(tile_count, dtype=jnp.int32)
    same_owner = tile_owner[None, :] == tile_owner[:, None]
    before_mask = tile_pos[None, :] < tile_pos[:, None]
    slot_rank = jnp.sum((same_owner & before_mask).astype(jnp.int32), axis=1)
    labels = jnp.arange(block_count, dtype=jnp.int32)
    shard_of = jnp.sum(jnp.where(block_ids[None, :] == labels[:, None], labels[None, :], 0), axis=1)
    gathered = lax.all_gather(coarse_view[None], "bl", axis=0, tiled=True)
    mine_mask = tile_owner == my_index
    own_count = jnp.sum(mine_mask.astype(jnp.int32))
    slot_steps = jnp.arange(slot_cap, dtype=jnp.int32)
    slot_tile = jnp.sum(
        jnp.where(
            mine_mask[None, :] & (slot_rank[None, :] == slot_steps[:, None]), tile_pos[None, :], 0
        ),
        axis=1,
    )

    def one_tile(slot_pos, result_tiles):
        tile_id = slot_tile[slot_pos]
        row_block = gathered[shard_of[row_table[tile_id]]]
        col_block = gathered[shard_of[col_table[tile_id]]]
        tile = tile_product(row_block, col_block, norm_scale)
        return lax.dynamic_update_slice(result_tiles, tile[:, :, None], (0, 0, slot_pos, 0, 0))

    empty_tiles = jnp.zeros((2, coarse_here, slot_cap, rows_here, rows_here), jnp.float32)
    return lax.fori_loop(0, own_count, one_tile, empty_tiles)


def solution(mesh):
    def correlator(voltages, coefs, block_ids, tile_owner):
        fits = takes_kernels(mesh, voltages, coefs)
        return jax.shard_map(
            per_device_kernels if fits else per_device,
            mesh=mesh,
            in_specs=(P(None, ("grp", "ft"), "bl"), P(), P(), P("grp")),
            out_specs=P(None, ("grp", "ft"), "bl", None, None),
            check_vma=False,
        )(voltages, coefs, block_ids, tile_owner)

    return correlator
```

```python
import functools
import math

import jax
import jax.numpy as jnp
import ml_dtypes
import numpy as np
from jax import lax
from jax.experimental import pallas as pl
from jax.experimental.pallas import tpu as pltpu
from jax.sharding import PartitionSpec as P

AVG = 64
MXU = 256
LANES = 128
ROWS16 = 16
VMEM_BYTES = 48 * 1024 * 1024


def split_bf16(table):
    high = table.astype(ml_dtypes.bfloat16)
    low = (table - high.astype(np.float64)).astype(ml_dtypes.bfloat16)
    return high, low


def matrix_tables(inner_len):
    steps = np.arange(inner_len)
    angles = 2.0 * np.pi * (np.outer(steps, steps) % inner_len) / inner_len
    cos_part, sin_part = np.cos(angles), np.sin(angles)
    high, low = split_bf16(np.block([[cos_part, -sin_part], [sin_part, cos_part]]))
    return np.concatenate([high, high, low])


def twiddle_tables(radix, inner_len):
    chan_count = radix * inner_len
    angles = 2.0 * np.pi * np.outer(np.arange(radix), np.arange(inner_len)) / chan_count
    scale = 1.0 / math.sqrt(chan_count)
    return np.stack([np.cos(angles) * scale, np.sin(angles) * scale]).astype(np.float32)


def rotate(real, imag, step, count):
    step = step % count
    if step == 0:
        return real, imag
    if 4 * step == count:
        return imag, -real
    if 2 * step == count:
        return -real, -imag
    if 4 * step == 3 * count:
        return -imag, real
    cos_step = math.cos(2.0 * math.pi * step / count)
    sin_step = math.sin(2.0 * math.pi * step / count)
    if 8 * step == count:
        return cos_step * (real + imag), cos_step * (imag - real)
    return cos_step * real + sin_step * imag, cos_step * imag - sin_step * real


def butterflies(parts):
    count = len(parts)
    if count == 1:
        return parts
    half = count // 2
    sums, diffs = [], []
    for k in range(half):
        (ar, ai), (br, bi) = parts[k], parts[k + half]
        sums.append((ar + br, ai + bi))
        diffs.append(rotate(ar - br, ai - bi, k, count))
    even, odd = butterflies(sums), butterflies(diffs)
    out = []
    for k in range(half):
        out += [even[k], odd[k]]
    return out


def pack_kernel(radix, place_ref, v_ref, *rest):
    o_refs, (wide, turned) = rest[:-2], rest[-2:]
    dests, rows, samples = turned.shape
    inner = samples // radix
    for part in range(2):
        for chunk in range(v_ref.shape[2] // LANES):
            wide[...] = v_ref[part, :, chunk * LANES : (chunk + 1) * LANES].astype(jnp.float32)
            for phase in range(radix):
                here = wide[pl.ds(phase, inner, stride=radix), :].T.astype(jnp.bfloat16)
                for dest in range(dests):
                    turned[dest, :, phase * inner : (phase + 1) * inner] = here[
                        dest * rows : (dest + 1) * rows
                    ]
            for shift in range(dests):
                o_refs[shift][part, chunk * rows : (chunk + 1) * rows] = turned[place_ref[shift]]


def pack(voltages, place, dests, radix):
    _, samples, inputs = voltages.shape
    chunks = inputs // LANES
    rows = LANES // dests
    vmem = pl.BlockSpec(memory_space=pltpu.VMEM)
    return pl.pallas_call(
        functools.partial(pack_kernel, radix),
        grid_spec=pltpu.PrefetchScalarGridSpec(
            num_scalar_prefetch=1,
            grid=(),
            in_specs=[vmem],
            out_specs=[vmem] * dests,
            scratch_shapes=[
                pltpu.VMEM((samples, LANES), jnp.float32),
                pltpu.VMEM((dests, rows, samples), jnp.bfloat16),
            ],
        ),
        out_shape=[jax.ShapeDtypeStruct((2, chunks * rows, samples), jnp.bfloat16)] * dests,
        compiler_params=pltpu.CompilerParams(vmem_limit_bytes=VMEM_BYTES // 2),
        name="pack_inputs",
    )(place, voltages)


def stage_kernel(*refs):
    half = len(refs) // 2
    for source, target in zip(refs[:half], refs[half:]):
        target[...] = source[...]


def stage(*tables):
    vmem = pl.BlockSpec(memory_space=pltpu.VMEM)
    return pl.pallas_call(
        stage_kernel,
        in_specs=[vmem] * len(tables),
        out_specs=[vmem] * len(tables),
        out_shape=[jax.ShapeDtypeStruct(table.shape, table.dtype) for table in tables],
        compiler_params=pltpu.CompilerParams(vmem_limit_bytes=VMEM_BYTES // 4),
        name="stage_tables",
    )(*tables)


def filter_blocks(place_ref, v_refs, c_ref, held, split):
    spectra, _, rows, samples = held.shape
    taps, radix, inner = c_ref.shape
    for shift in range(len(v_refs)):
        held[place_ref[len(v_refs) + shift]] = v_refs[shift][...]

    @pl.loop(0, radix)
    def _(phase):
        lane0 = pl.multiple_of(phase * inner, inner)
        row0 = pl.multiple_of(phase * spectra * rows, spectra * rows)
        for part in range(2):
            for sub in range(0, rows, ROWS16):
                blocks = [
                    held[b, part, pl.ds(sub, ROWS16), pl.ds(lane0, inner)].astype(jnp.float32)
                    for b in range(spectra)
                ]
                for s in range(spectra):
                    total = None
                    for b in range(max(0, s - taps + 1), s + 1):
                        term = c_ref[taps - 1 - s + b, pl.ds(phase, 1), :] * blocks[b]
                        total = term if total is None else total + term
                    high = total.astype(jnp.bfloat16)
                    low = (total - high.astype(jnp.float32)).astype(jnp.bfloat16)
                    at = pl.ds(pl.multiple_of(row0 + s * rows + sub, ROWS16), ROWS16)
                    split[at, part * inner : (part + 1) * inner] = high
                    split[at, (2 + part) * inner : (3 + part) * inner] = low


def transform_lanes(place_ref, split, tw_ref, g_ref, prod, made, out_refs):
    dests, halves, _, spectra, rows, _ = made.shape
    radix = tw_ref.shape[1]
    group = spectra * rows
    depth = split.shape[1] // 2

    @pl.loop(0, radix // 2)
    def _(pair):
        at = pl.ds(pl.multiple_of(pair * 2 * group, 2 * group), 2 * group)
        high = split[at, :depth]
        line = jnp.concatenate([high, split[at, depth:], high], axis=1)
        prod[at, :] = jnp.dot(line, g_ref[...], preferred_element_type=jnp.float32)

    @pl.loop(0, spectra)
    def _(s):
        for sub in range(0, rows, ROWS16):
            parts = []
            for phase in range(radix):
                at = pl.ds(pl.multiple_of(phase * group + s * rows + sub, ROWS16), ROWS16)
                yr, yi = prod[at, :LANES], prod[at, LANES:]
                cos_here = tw_ref[0, phase : phase + 1, :]
                sin_here = tw_ref[1, phase : phase + 1, :]
                if phase == 0:
                    parts.append((yr * cos_here, yi * cos_here))
                else:
                    parts.append((yr * cos_here + yi * sin_here, yi * cos_here - yr * sin_here))
            for step, pair in enumerate(butterflies(parts)):
                for part in range(2):
                    made[step // halves, step % halves, part, s, sub : sub + ROWS16, :] = pair[
                        part
                    ].astype(jnp.bfloat16)

    for shift in range(dests):
        for half in range(halves):
            out_refs[half * dests + shift][...] = made[place_ref[shift], half]


def transform_cut(source, place, coef_table, tables, cut, sizes, after):
    dests, spectra, rows, samples, radix = sizes
    inner = samples // radix
    halves = radix // dests
    total = radix * spectra * rows
    begins = coef_table is not None
    vmem = pl.BlockSpec(memory_space=pltpu.VMEM)

    def kernel(place_ref, *rest):
        if begins:
            v_refs, (c_ref, tw_ref, g_ref) = rest[:dests], rest[dests : dests + 3]
            out_refs, (split, held, prod, made) = rest[dests + 4 : -4], rest[-4:]
            filter_blocks(place_ref, v_refs, c_ref, held, split)
        else:
            split, tw_ref, g_ref = rest[:3]
            out_refs, (prod, made) = rest[4:-2], rest[-2:]
        transform_lanes(place_ref, split, tw_ref, g_ref, prod, made, out_refs)

    scratch = [
        pltpu.VMEM((total, 2 * LANES), jnp.float32),
        pltpu.VMEM((dests, halves, 2, spectra, rows, LANES), jnp.bfloat16),
    ]
    shapes = [jax.ShapeDtypeStruct((2, spectra, rows, LANES), jnp.bfloat16)] * (halves * dests)
    if begins:
        scratch = [pltpu.VMEM((spectra, 2, rows, samples), jnp.bfloat16)] + scratch
        shapes = shapes + [jax.ShapeDtypeStruct((total, 4 * inner), jnp.bfloat16)]
    args = [*source, coef_table] if begins else [source]
    args += [tables[2 * cut], tables[2 * cut + 1]]
    made = pl.pallas_call(
        kernel,
        grid_spec=pltpu.PrefetchScalarGridSpec(
            num_scalar_prefetch=1,
            grid=(),
            in_specs=[vmem] * len(args) + [pl.BlockSpec(memory_space=pl.ANY)],
            out_specs=[vmem] * len(shapes),
            scratch_shapes=scratch,
        ),
        out_shape=shapes,
        cost_estimate=pl.CostEstimate(
            flops=3 * 2 * total * 4 * inner * LANES, bytes_accessed=6 << 20, transcendentals=0
        ),
        compiler_params=pltpu.CompilerParams(vmem_limit_bytes=VMEM_BYTES // 2),
        name="filter_transform" if begins else "transform_rest",
    )(place, *args, after)
    units = [made[half * dests : (half + 1) * dests] for half in range(halves)]
    return units, made[-1]


def join(pieces, place, before, after):
    count = len(pieces)
    vmem = pl.BlockSpec(memory_space=pltpu.VMEM)
    shapes = [jax.ShapeDtypeStruct((count, *pieces[0].shape), pieces[0].dtype)]
    if before:
        shapes.append(jax.ShapeDtypeStruct((2, *before[0].shape), before[0].dtype))

    def kernel(place_ref, *rest):
        ins, outs = rest[: count + len(before)], rest[count + len(before) + 1 :]
        for shift in range(count):
            outs[0][place_ref[count + shift]] = ins[shift][...]
        for at in range(len(before)):
            outs[1][at] = ins[count + at][...]

    return pl.pallas_call(
        kernel,
        grid_spec=pltpu.PrefetchScalarGridSpec(
            num_scalar_prefetch=1,
            grid=(),
            in_specs=[vmem] * (count + len(before)) + [pl.BlockSpec(memory_space=pl.ANY)],
            out_specs=[vmem] * len(shapes),
        ),
        out_shape=shapes,
        compiler_params=pltpu.CompilerParams(vmem_limit_bytes=VMEM_BYTES // 4),
        name="join_pieces",
    )(place, *pieces, *before, after)


def pair(own, other, after):
    def kernel(own_ref, other_ref, _, out_ref):
        out_ref[0] = own_ref[...]
        out_ref[1] = other_ref[...]

    vmem = pl.BlockSpec(memory_space=pltpu.VMEM)
    return pl.pallas_call(
        kernel,
        in_specs=[vmem, vmem, pl.BlockSpec(memory_space=pl.ANY)],
        out_specs=vmem,
        out_shape=jax.ShapeDtypeStruct((2, *own.shape), own.dtype),
        compiler_params=pltpu.CompilerParams(vmem_limit_bytes=VMEM_BYTES // 4),
        name="pair_blocks",
    )(own, other, after)


def correlate_kernel(chunks, scale, first, table_ref, low_ref, high_ref, *rest):
    o_ref, token_ref, left, tiles, empty, sems = rest[-6:]
    half, senders, _, spectra, rows, lanes = low_ref.shape
    order = block_order(2 * half)
    slots = o_ref.shape[2]
    coarse = lanes // AVG
    side = senders * rows
    run = rows // chunks
    count = table_ref[2 * slots]
    token_ref[...] = jnp.zeros_like(token_ref)
    empty[...] = jnp.zeros_like(empty)

    def copy_out(source, c, slot):
        return pltpu.make_async_copy(source, o_ref.at[:, first + c, slot], sems.at[c, slot])

    for slot in range(slots):

        @pl.when(slot >= count)
        def _(slot=slot):
            for c in range(coarse):
                copy_out(empty, c, slot).start()

    for at, block in enumerate(order):
        source = (low_ref, high_ref)[at // half].at[at % half]

        @pl.loop(0, senders)
        def _(sender, block=block, source=source):
            for part in range(2):
                for chunk in range(chunks):
                    row = pl.multiple_of(part * side + (chunk * senders + sender) * run, run)
                    pieces = [
                        source[sender, part, s, chunk * run : (chunk + 1) * run]
                        for s in range(spectra)
                    ]
                    for c in range(coarse):
                        left[c, block, pl.ds(row, run), :] = jnp.concatenate(
                            [piece[:, c * AVG : (c + 1) * AVG] for piece in pieces], axis=1
                        )

    for slot in range(slots):

        @pl.when(slot < count)
        def _(slot=slot):
            for c in range(coarse):
                rows_of = left[c, table_ref[slot]]
                with_real, with_imag = [
                    lax.dot_general(
                        rows_of,
                        left[c, table_ref[slots + slot], pl.ds(part * side, side), :],
                        (((1,), (1,)), ((), ())),
                        preferred_element_type=jnp.float32,
                    )
                    for part in range(2)
                ]
                tiles[c, slot, 0] = (with_real[:side] + with_imag[side:]) * scale
                tiles[c, slot, 1] = (with_real[side:] - with_imag[:side]) * scale
                copy_out(tiles.at[c, slot], c, slot).start()

    for slot in range(slots):
        for c in range(coarse):
            copy_out(empty, c, slot).wait()


def correlate(table, gathered, first, channels, chunks, slots, vis):
    half, senders, _, spectra, rows, lanes = gathered[0].shape
    coarse = lanes // AVG
    side = senders * rows
    vmem = pl.BlockSpec(memory_space=pltpu.VMEM)
    anywhere = pl.BlockSpec(memory_space=pl.ANY)
    args = [table, *gathered]
    aliases = {}
    if vis is not None:
        args.append(vis)
        aliases = {len(args) - 1: 0}
    return pl.pallas_call(
        functools.partial(correlate_kernel, chunks, 1.0 / (AVG * spectra), first),
        grid_spec=pltpu.PrefetchScalarGridSpec(
            num_scalar_prefetch=1,
            grid=(),
            in_specs=[vmem, vmem] + [anywhere] * (len(args) - 3),
            out_specs=[anywhere, vmem],
            scratch_shapes=[
                pltpu.VMEM((coarse, 2 * half, 2 * side, spectra * AVG), jnp.bfloat16),
                pltpu.VMEM((coarse, slots, 2, side, side), jnp.float32),
                pltpu.VMEM((2, side, side), jnp.float32),
                pltpu.SemaphoreType.DMA((coarse, slots)),
            ],
        ),
        out_shape=[
            jax.ShapeDtypeStruct((2, channels, slots, side, side), jnp.float32),
            jax.ShapeDtypeStruct((8, LANES), jnp.float32),
        ],
        input_output_aliases=aliases,
        cost_estimate=pl.CostEstimate(flops=0, bytes_accessed=0, transcendentals=0),
        compiler_params=pltpu.CompilerParams(vmem_limit_bytes=VMEM_BYTES),
        name="correlate_tiles",
    )(*args)


def places(count):
    steps = np.arange(count, dtype=np.int32)
    index = lax.axis_index("ft").astype(jnp.int32)
    return jnp.concatenate([(index + steps) % count, (index + count - steps) % count])


def spread(pieces):
    count = len(pieces)
    return [pieces[0]] + [
        lax.ppermute(pieces[d], "ft", [(i, (i + d) % count) for i in range(count)])
        for d in range(1, count)
    ]


def exchange(own, bit):
    count = lax.axis_size("bl")
    return lax.ppermute(own, "bl", [(i, i ^ bit) for i in range(count)])


def gather_blocks(held, after):
    bit = lax.axis_size("bl") // 4
    other = exchange(held, bit)
    while bit > 1:
        bit //= 2
        held = pair(held, other, after).reshape(-1, *held.shape[1:])
        other = exchange(held, bit)
    return held, other


def block_order(count):
    order, bit = [0], count // 2
    while bit:
        order += [r ^ bit for r in order]
        bit //= 2
    return order


def tile_tables(block_ids, tile_owner):
    block_count = lax.axis_size("bl")
    tile_count = block_count * (block_count + 1) // 2
    slot_cap = 2 * tile_count // block_count
    pairs = [(i, j) for i in range(block_count) for j in range(i, block_count)]
    row_table = np.array([i for i, _ in pairs], np.int32)
    col_table = np.array([j for _, j in pairs], np.int32)
    mine = (tile_owner == lax.axis_index("bl")).astype(jnp.int32)
    earlier = np.tril(np.ones((tile_count, tile_count), np.int32), -1)
    rank = jnp.sum(earlier * mine[None, :], axis=1)
    labels = np.arange(block_count, dtype=np.int32)
    shard_of = jnp.sum(jnp.where(block_ids[None, :] == labels[:, None], labels[None, :], 0), axis=1)
    row_shard = jnp.sum(
        jnp.where(row_table[:, None] == labels[None, :], shard_of[None, :], 0), axis=1
    )
    col_shard = jnp.sum(
        jnp.where(col_table[:, None] == labels[None, :], shard_of[None, :], 0), axis=1
    )
    here = (mine[None, :] == 1) & (rank[None, :] == np.arange(slot_cap, dtype=np.int32)[:, None])
    rows = jnp.sum(jnp.where(here, row_shard[None, :], 0), axis=1)
    cols = jnp.sum(jnp.where(here, col_shard[None, :], 0), axis=1)
    index = lax.axis_index("bl")
    table = jnp.concatenate(
        [rows ^ index, cols ^ index, jnp.sum(mine, keepdims=True)]
    ).astype(jnp.int32)
    return table, slot_cap


def takes_kernels(mesh, voltages, coefs):
    dests = mesh.shape["ft"]
    blocks = mesh.shape["bl"]
    inputs = voltages.shape[2] // mesh.shape["bl"]
    per_dev = voltages.shape[1] // (mesh.shape["grp"] * dests)
    chan_count = coefs.shape[1]
    radix = chan_count // MXU
    return (
        per_dev == chan_count
        and chan_count % MXU == 0
        and radix & (radix - 1) == 0
        and radix % dests == 0
        and radix <= 8
        and blocks & (blocks - 1) == 0
        and blocks > 2
        and inputs % LANES == 0
        and LANES % dests == 0
        and (LANES // dests) % ROWS16 == 0
        and (dests * AVG) % LANES == 0
    )


def per_device_kernels(voltages, coefs, block_ids, tile_owner):
    dests = lax.axis_size("ft")
    taps, chan_count = coefs.shape
    radix = chan_count // MXU
    chunks = voltages.shape[2] // LANES
    coef_table = coefs.reshape(taps, MXU, radix).transpose(0, 2, 1)
    place = places(dests)
    table, slot_cap = tile_tables(block_ids, tile_owner)
    matrix, twiddle = matrix_tables(MXU), twiddle_tables(radix, MXU)
    cuts = MXU // LANES
    tables = []
    for cut in range(cuts):
        at = slice(cut * LANES, (cut + 1) * LANES)
        tables.append(np.ascontiguousarray(twiddle[:, :, at]))
        tables.append(np.concatenate([matrix[:, :MXU][:, at], matrix[:, MXU:][:, at]], axis=1))
    coef_table, *tables = stage(coef_table, *tables)
    arrived = spread(pack(voltages, place, dests, radix))
    _, rows, samples = arrived[0].shape
    sizes = (dests, dests, rows, samples, radix)
    made, split = transform_cut(arrived, place, coef_table, tables, 0, sizes, table)
    firsts = [table]
    for cut in range(1, cuts):
        more, _ = transform_cut(split, place, None, tables, cut, sizes, table)
        made = made + more
        firsts.append(more[0][0])
    half = lax.axis_size("bl") // 2
    units = len(made)
    own, other, arrived, tokens, vis = None, None, None, [], None
    for unit in range(units + 1):
        held = None
        if unit < units:
            parts = made[unit]
            if unit > 1:
                parts, _ = lax.optimization_barrier((parts, arrived))
            arrived = spread(parts)
            after = tokens[-1] if tokens else table
            if unit > 0:
                own, held = join(arrived, place, (own, other), after)
            else:
                (own,) = join(arrived, place, (), firsts[-1])
            other = exchange(own, half)
        else:
            held = pair(own, other, tokens[-1])
        if unit > 0:
            gathered = gather_blocks(held, table)
            cut, part = divmod(unit - 1, radix // dests)
            first = (part * MXU + cut * LANES) // AVG
            vis, token = correlate(
                table, gathered, first, units * LANES // AVG, chunks, slot_cap, vis
            )
            tokens.append(token)
    return vis


def tile_product(row_part, col_part, norm_scale):
    products = jnp.einsum(
        "pscax,qscay->cpqxy", row_part, col_part, preferred_element_type=jnp.float32
    )
    real_part = products[:, 0, 0] + products[:, 1, 1]
    imag_part = products[:, 1, 0] - products[:, 0, 1]
    return jnp.stack([real_part, imag_part]) * norm_scale


def dft_tables(order_len):
    steps_one = jnp.arange(order_len, dtype=jnp.int32)
    phase_grid = steps_one[:, None] * steps_one[None, :] % order_len
    angles = phase_grid.astype(jnp.float32) * (2.0 * math.pi / order_len)
    return (jnp.cos(angles), jnp.sin(angles))


def transform(filtered):
    per_dev = filtered.shape[1]
    chan_count = filtered.shape[2]
    rows_here = filtered.shape[3]
    outer_len = math.isqrt(chan_count)
    while chan_count % outer_len != 0:
        outer_len = outer_len - 1
    inner_len = chan_count // outer_len
    highest = lax.Precision.HIGHEST
    reshaped = filtered.reshape(2, per_dev, outer_len, inner_len, rows_here)
    real_in = reshaped[0]
    imag_in = reshaped[1]
    cos_outer, sin_outer = dft_tables(outer_len)
    section_re = jnp.einsum("snkb,nm->smkb", real_in, cos_outer, precision=highest) + jnp.einsum(
        "snkb,nm->smkb", imag_in, sin_outer, precision=highest
    )
    section_im = jnp.einsum("snkb,nm->smkb", imag_in, cos_outer, precision=highest) - jnp.einsum(
        "snkb,nm->smkb", real_in, sin_outer, precision=highest
    )
    twiddle_grid = (
        jnp.arange(outer_len, dtype=jnp.int32)[:, None]
        * jnp.arange(inner_len, dtype=jnp.int32)[None, :]
        % chan_count
    )
    twiddle_angles = twiddle_grid.astype(jnp.float32) * (2.0 * math.pi / chan_count)
    cos_twiddle = jnp.cos(twiddle_angles)[None, :, :, None]
    sin_twiddle = jnp.sin(twiddle_angles)[None, :, :, None]
    rot_re = section_re * cos_twiddle + section_im * sin_twiddle
    rot_im = section_im * cos_twiddle - section_re * sin_twiddle
    cos_inner, sin_inner = dft_tables(inner_len)
    final_re = jnp.einsum("smkb,kq->sqmb", rot_re, cos_inner, precision=highest) + jnp.einsum(
        "smkb,kq->sqmb", rot_im, sin_inner, precision=highest
    )
    final_im = jnp.einsum("smkb,kq->sqmb", rot_im, cos_inner, precision=highest) - jnp.einsum(
        "smkb,kq->sqmb", rot_re, sin_inner, precision=highest
    )
    stacked = jnp.stack([final_re, final_im]).reshape(2, per_dev, chan_count, rows_here)
    return (stacked * (1.0 / math.sqrt(chan_count))).astype(jnp.bfloat16)


def apply_taps(window, coef_part, taps_count, out_len):
    filtered = jnp.zeros((2, out_len, window.shape[2], window.shape[3]), jnp.float32)
    for tap_index in range(taps_count):
        filtered = filtered + coef_part[tap_index][None, None, :, None] * window[
            :, tap_index : tap_index + out_len
        ].astype(jnp.float32)
    return filtered


def per_device(voltages, coefs, block_ids, tile_owner):
    taps_count = coefs.shape[0]
    chan_count = coefs.shape[1]
    rows_here = voltages.shape[2]
    per_dev = voltages.shape[1] // chan_count
    volt_blocks = voltages.reshape(2, per_dev, chan_count, rows_here)
    phase_block = lax.all_to_all(volt_blocks, "ft", split_axis=2, concat_axis=1, tiled=True)
    spectra_count = phase_block.shape[1]
    phase_here = phase_block.shape[2]
    coef_part = lax.dynamic_slice_in_dim(coefs, lax.axis_index("ft") * phase_here, phase_here, 1)
    zero_front = jnp.zeros((2, taps_count - 1, phase_here, rows_here), phase_block.dtype)
    long_window = jnp.concatenate([zero_front, phase_block], axis=1)
    phase_filtered = apply_taps(long_window, coef_part, taps_count, spectra_count)
    filtered = lax.all_to_all(phase_filtered, "ft", split_axis=1, concat_axis=2, tiled=True)
    spectra = transform(filtered)
    turned = lax.all_to_all(spectra, "ft", split_axis=2, concat_axis=1, tiled=True)
    spectra_all = turned.shape[1]
    chan_here = turned.shape[2]
    coarse_here = chan_here // AVG
    coarse_view = turned.reshape(2, spectra_all, coarse_here, AVG, rows_here)
    norm_scale = 1.0 / (AVG * spectra_all)
    block_count = lax.axis_size("bl")
    my_index = lax.axis_index("bl")
    tile_count = block_count * (block_count + 1) // 2
    slot_cap = 2 * tile_count // block_count
    row_table = jnp.asarray(
        np.array(
            [
                first_id
                for first_id in range(block_count)
                for second_id in range(first_id, block_count)
            ],
            dtype=np.int32,
        )
    )
    col_table = jnp.asarray(
        np.array(
            [
                second_id
                for first_id in range(block_count)
                for second_id in range(first_id, block_count)
            ],
            dtype=np.int32,
        )
    )
    tile_pos = jnp.arange(tile_count, dtype=jnp.int32)
    same_owner = tile_owner[None, :] == tile_owner[:, None]
    before_mask = tile_pos[None, :] < tile_pos[:, None]
    slot_rank = jnp.sum((same_owner & before_mask).astype(jnp.int32), axis=1)
    labels = jnp.arange(block_count, dtype=jnp.int32)
    shard_of = jnp.sum(jnp.where(block_ids[None, :] == labels[:, None], labels[None, :], 0), axis=1)
    gathered = lax.all_gather(coarse_view[None], "bl", axis=0, tiled=True)
    mine_mask = tile_owner == my_index
    own_count = jnp.sum(mine_mask.astype(jnp.int32))
    slot_steps = jnp.arange(slot_cap, dtype=jnp.int32)
    slot_tile = jnp.sum(
        jnp.where(
            mine_mask[None, :] & (slot_rank[None, :] == slot_steps[:, None]), tile_pos[None, :], 0
        ),
        axis=1,
    )

    def one_tile(slot_pos, result_tiles):
        tile_id = slot_tile[slot_pos]
        row_block = gathered[shard_of[row_table[tile_id]]]
        col_block = gathered[shard_of[col_table[tile_id]]]
        tile = tile_product(row_block, col_block, norm_scale)
        return lax.dynamic_update_slice(result_tiles, tile[:, :, None], (0, 0, slot_pos, 0, 0))

    empty_tiles = jnp.zeros((2, coarse_here, slot_cap, rows_here, rows_here), jnp.float32)
    return lax.fori_loop(0, own_count, one_tile, empty_tiles)


def solution(mesh):
    def correlator(voltages, coefs, block_ids, tile_owner):
        fits = takes_kernels(mesh, voltages, coefs)
        return jax.shard_map(
            per_device_kernels if fits else per_device,
            mesh=mesh,
            in_specs=(P(None, ("grp", "ft"), "bl"), P(), P(), P("grp")),
            out_specs=P(None, ("grp", "ft"), "bl", None, None),
            check_vma=False,
        )(voltages, coefs, block_ids, tile_owner)

    return correlator
```

```python
import functools
import math

import jax
import jax.numpy as jnp
import ml_dtypes
import numpy as np
from jax import lax
from jax.experimental import pallas as pl
from jax.experimental.pallas import tpu as pltpu
from jax.sharding import PartitionSpec as P

AVG = 64
MXU = 256
LANES = 128
ROWS16 = 16
VMEM_BYTES = 48 * 1024 * 1024


def split_bf16(table):
    high = table.astype(ml_dtypes.bfloat16)
    low = (table - high.astype(np.float64)).astype(ml_dtypes.bfloat16)
    return high, low


def matrix_tables(inner_len):
    steps = np.arange(inner_len)
    angles = 2.0 * np.pi * (np.outer(steps, steps) % inner_len) / inner_len
    cos_part, sin_part = np.cos(angles), np.sin(angles)
    high, low = split_bf16(np.block([[cos_part, -sin_part], [sin_part, cos_part]]))
    return np.concatenate([high, high, low])


def twiddle_tables(radix, inner_len):
    chan_count = radix * inner_len
    angles = 2.0 * np.pi * np.outer(np.arange(radix), np.arange(inner_len)) / chan_count
    scale = 1.0 / math.sqrt(chan_count)
    return np.stack([np.cos(angles) * scale, np.sin(angles) * scale]).astype(np.float32)


def rotate(real, imag, step, count):
    step = step % count
    if step == 0:
        return real, imag
    if 4 * step == count:
        return imag, -real
    if 2 * step == count:
        return -real, -imag
    if 4 * step == 3 * count:
        return -imag, real
    cos_step = math.cos(2.0 * math.pi * step / count)
    sin_step = math.sin(2.0 * math.pi * step / count)
    if 8 * step == count:
        return cos_step * (real + imag), cos_step * (imag - real)
    return cos_step * real + sin_step * imag, cos_step * imag - sin_step * real


def butterflies(parts):
    count = len(parts)
    if count == 1:
        return parts
    half = count // 2
    sums, diffs = [], []
    for k in range(half):
        (ar, ai), (br, bi) = parts[k], parts[k + half]
        sums.append((ar + br, ai + bi))
        diffs.append(rotate(ar - br, ai - bi, k, count))
    even, odd = butterflies(sums), butterflies(diffs)
    out = []
    for k in range(half):
        out += [even[k], odd[k]]
    return out


def pack_kernel(radix, place_ref, v_ref, *rest):
    o_refs, (wide, turned) = rest[:-2], rest[-2:]
    dests, rows, samples = turned.shape
    inner = samples // radix
    for part in range(2):
        for chunk in range(v_ref.shape[2] // LANES):
            wide[...] = v_ref[part, :, chunk * LANES : (chunk + 1) * LANES].astype(jnp.float32)
            for phase in range(radix):
                here = wide[pl.ds(phase, inner, stride=radix), :].T.astype(jnp.bfloat16)
                for dest in range(dests):
                    turned[dest, :, phase * inner : (phase + 1) * inner] = here[
                        dest * rows : (dest + 1) * rows
                    ]
            for shift in range(dests):
                o_refs[shift][part, chunk * rows : (chunk + 1) * rows] = turned[place_ref[shift]]


def pack(voltages, place, dests, radix):
    _, samples, inputs = voltages.shape
    chunks = inputs // LANES
    rows = LANES // dests
    vmem = pl.BlockSpec(memory_space=pltpu.VMEM)
    return pl.pallas_call(
        functools.partial(pack_kernel, radix),
        grid_spec=pltpu.PrefetchScalarGridSpec(
            num_scalar_prefetch=1,
            grid=(),
            in_specs=[vmem],
            out_specs=[vmem] * dests,
            scratch_shapes=[
                pltpu.VMEM((samples, LANES), jnp.float32),
                pltpu.VMEM((dests, rows, samples), jnp.bfloat16),
            ],
        ),
        out_shape=[jax.ShapeDtypeStruct((2, chunks * rows, samples), jnp.bfloat16)] * dests,
        compiler_params=pltpu.CompilerParams(vmem_limit_bytes=VMEM_BYTES // 2),
        name="pack_inputs",
    )(place, voltages)


def stage_kernel(*refs):
    half = len(refs) // 2
    for source, target in zip(refs[:half], refs[half:]):
        target[...] = source[...]


def stage(*tables):
    vmem = pl.BlockSpec(memory_space=pltpu.VMEM)
    return pl.pallas_call(
        stage_kernel,
        in_specs=[vmem] * len(tables),
        out_specs=[vmem] * len(tables),
        out_shape=[jax.ShapeDtypeStruct(table.shape, table.dtype) for table in tables],
        compiler_params=pltpu.CompilerParams(vmem_limit_bytes=VMEM_BYTES // 4),
        name="stage_tables",
    )(*tables)


def filter_blocks(place_ref, v_refs, c_ref, held, split):
    spectra, _, rows, samples = held.shape
    taps, radix, inner = c_ref.shape
    for shift in range(len(v_refs)):
        held[place_ref[len(v_refs) + shift]] = v_refs[shift][...]

    @pl.loop(0, radix)
    def _(phase):
        lane0 = pl.multiple_of(phase * inner, inner)
        row0 = pl.multiple_of(phase * spectra * rows, spectra * rows)
        for part in range(2):
            for sub in range(0, rows, ROWS16):
                blocks = [
                    held[b, part, pl.ds(sub, ROWS16), pl.ds(lane0, inner)].astype(jnp.float32)
                    for b in range(spectra)
                ]
                for s in range(spectra):
                    total = None
                    for b in range(max(0, s - taps + 1), s + 1):
                        term = c_ref[taps - 1 - s + b, pl.ds(phase, 1), :] * blocks[b]
                        total = term if total is None else total + term
                    high = total.astype(jnp.bfloat16)
                    low = (total - high.astype(jnp.float32)).astype(jnp.bfloat16)
                    at = pl.ds(pl.multiple_of(row0 + s * rows + sub, ROWS16), ROWS16)
                    split[at, part * inner : (part + 1) * inner] = high
                    split[at, (2 + part) * inner : (3 + part) * inner] = low


def transform_lanes(place_ref, split, tw_ref, g_ref, prod, made, out_refs):
    dests, halves, _, spectra, rows, _ = made.shape
    radix = tw_ref.shape[1]
    group = spectra * rows
    depth = split.shape[1] // 2

    @pl.loop(0, radix // 2)
    def _(pair):
        at = pl.ds(pl.multiple_of(pair * 2 * group, 2 * group), 2 * group)
        high = split[at, :depth]
        line = jnp.concatenate([high, split[at, depth:], high], axis=1)
        prod[at, :] = jnp.dot(line, g_ref[...], preferred_element_type=jnp.float32)

    @pl.loop(0, spectra)
    def _(s):
        for sub in range(0, rows, ROWS16):
            parts = []
            for phase in range(radix):
                at = pl.ds(pl.multiple_of(phase * group + s * rows + sub, ROWS16), ROWS16)
                yr, yi = prod[at, :LANES], prod[at, LANES:]
                cos_here = tw_ref[0, phase : phase + 1, :]
                sin_here = tw_ref[1, phase : phase + 1, :]
                if phase == 0:
                    parts.append((yr * cos_here, yi * cos_here))
                else:
                    parts.append((yr * cos_here + yi * sin_here, yi * cos_here - yr * sin_here))
            for step, pair in enumerate(butterflies(parts)):
                for part in range(2):
                    made[step // halves, step % halves, part, s, sub : sub + ROWS16, :] = pair[
                        part
                    ].astype(jnp.bfloat16)

    whole = halves if len(out_refs) == halves * dests else halves - 1
    for shift in range(dests):
        for half in range(whole):
            out_refs[half * dests + shift][...] = made[place_ref[shift], half]
        if whole < halves:
            run = rows // 2
            for part in range(2):
                for s in range(spectra):
                    both = made[place_ref[shift], whole, part, s]
                    for c in range(2):
                        at = slice(c * AVG, (c + 1) * AVG)
                        out_refs[(whole + c) * dests + shift][part, s] = jnp.concatenate(
                            [both[:run, at], both[run:, at]], axis=1
                        )


def transform_cut(source, place, coef_table, tables, cut, sizes, after):
    dests, spectra, rows, samples, radix = sizes
    inner = samples // radix
    halves = radix // dests
    total = radix * spectra * rows
    begins = coef_table is not None
    vmem = pl.BlockSpec(memory_space=pltpu.VMEM)

    def kernel(place_ref, *rest):
        if begins:
            v_refs, (c_ref, tw_ref, g_ref) = rest[:dests], rest[dests : dests + 3]
            out_refs, (split, held, prod, made) = rest[dests + 4 : -4], rest[-4:]
            filter_blocks(place_ref, v_refs, c_ref, held, split)
        else:
            split, tw_ref, g_ref = rest[:3]
            out_refs, (prod, made) = rest[4:-2], rest[-2:]
        transform_lanes(place_ref, split, tw_ref, g_ref, prod, made, out_refs)

    scratch = [
        pltpu.VMEM((total, 2 * LANES), jnp.float32),
        pltpu.VMEM((dests, halves, 2, spectra, rows, LANES), jnp.bfloat16),
    ]
    shapes = [jax.ShapeDtypeStruct((2, spectra, rows, LANES), jnp.bfloat16)] * (halves * dests)
    if not begins:
        shapes[-dests:] = [
            jax.ShapeDtypeStruct((2, spectra, rows // 2, LANES), jnp.bfloat16)
        ] * (2 * dests)
    outs = len(shapes) // dests
    if begins:
        scratch = [pltpu.VMEM((spectra, 2, rows, samples), jnp.bfloat16)] + scratch
        shapes = shapes + [jax.ShapeDtypeStruct((total, 4 * inner), jnp.bfloat16)]
    args = [*source, coef_table] if begins else [source]
    args += [tables[2 * cut], tables[2 * cut + 1]]
    made = pl.pallas_call(
        kernel,
        grid_spec=pltpu.PrefetchScalarGridSpec(
            num_scalar_prefetch=1,
            grid=(),
            in_specs=[vmem] * len(args) + [pl.BlockSpec(memory_space=pl.ANY)],
            out_specs=[vmem] * len(shapes),
            scratch_shapes=scratch,
        ),
        out_shape=shapes,
        cost_estimate=pl.CostEstimate(
            flops=3 * 2 * total * 4 * inner * LANES, bytes_accessed=6 << 20, transcendentals=0
        ),
        compiler_params=pltpu.CompilerParams(vmem_limit_bytes=VMEM_BYTES // 2),
        name="filter_transform" if begins else "transform_rest",
    )(place, *args, after)
    units = [made[unit * dests : (unit + 1) * dests] for unit in range(outs)]
    return units, made[-1]


def join(pieces, place, before, after):
    count = len(pieces)
    vmem = pl.BlockSpec(memory_space=pltpu.VMEM)
    shapes = [jax.ShapeDtypeStruct((count, *pieces[0].shape), pieces[0].dtype)]
    if before:
        shapes.append(jax.ShapeDtypeStruct((2, *before[0].shape), before[0].dtype))

    def kernel(place_ref, *rest):
        ins, outs = rest[: count + len(before)], rest[count + len(before) + 1 :]
        for shift in range(count):
            outs[0][place_ref[count + shift]] = ins[shift][...]
        for at in range(len(before)):
            outs[1][at] = ins[count + at][...]

    return pl.pallas_call(
        kernel,
        grid_spec=pltpu.PrefetchScalarGridSpec(
            num_scalar_prefetch=1,
            grid=(),
            in_specs=[vmem] * (count + len(before)) + [pl.BlockSpec(memory_space=pl.ANY)],
            out_specs=[vmem] * len(shapes),
        ),
        out_shape=shapes,
        compiler_params=pltpu.CompilerParams(vmem_limit_bytes=VMEM_BYTES // 4),
        name="join_pieces",
    )(place, *pieces, *before, after)


def pair(own, other, after):
    def kernel(own_ref, other_ref, _, out_ref):
        out_ref[0] = own_ref[...]
        out_ref[1] = other_ref[...]

    vmem = pl.BlockSpec(memory_space=pltpu.VMEM)
    return pl.pallas_call(
        kernel,
        in_specs=[vmem, vmem, pl.BlockSpec(memory_space=pl.ANY)],
        out_specs=vmem,
        out_shape=jax.ShapeDtypeStruct((2, *own.shape), own.dtype),
        compiler_params=pltpu.CompilerParams(vmem_limit_bytes=VMEM_BYTES // 4),
        name="pair_blocks",
    )(own, other, after)


def correlate_kernel(chunks, single, scale, first, table_ref, low_ref, high_ref, *rest):
    o_ref, token_ref, left, tiles, empty, sems = rest[-6:]
    half, senders, _, spectra, rows, lanes = low_ref.shape
    order = block_order(2 * half)
    slots = o_ref.shape[2]
    coarse = 1 if single else lanes // AVG
    run = rows if single else rows // chunks
    side = senders * chunks * run
    count = table_ref[2 * slots]
    token_ref[...] = jnp.zeros_like(token_ref)
    empty[...] = jnp.zeros_like(empty)

    def copy_out(source, c, slot):
        return pltpu.make_async_copy(source, o_ref.at[:, first + c, slot], sems.at[c, slot])

    for slot in range(slots):

        @pl.when(slot >= count)
        def _(slot=slot):
            for c in range(coarse):
                copy_out(empty, c, slot).start()

    for at, block in enumerate(order):
        source = (low_ref, high_ref)[at // half].at[at % half]

        @pl.loop(0, senders)
        def _(sender, block=block, source=source):
            for part in range(2):
                for chunk in range(chunks):
                    row = pl.multiple_of(part * side + (chunk * senders + sender) * run, run)
                    top = 0 if single else chunk * run
                    pieces = [
                        source[sender, part, s, top : top + run] for s in range(spectra)
                    ]
                    for c in range(coarse):
                        lane = (chunk if single else c) * AVG
                        left[c, block, pl.ds(row, run), :] = jnp.concatenate(
                            [piece[:, lane : lane + AVG] for piece in pieces], axis=1
                        )

    for slot in range(slots):

        @pl.when(slot < count)
        def _(slot=slot):
            for c in range(coarse):
                rows_of = left[c, table_ref[slot]]
                with_real, with_imag = [
                    lax.dot_general(
                        rows_of,
                        left[c, table_ref[slots + slot], pl.ds(part * side, side), :],
                        (((1,), (1,)), ((), ())),
                        preferred_element_type=jnp.float32,
                    )
                    for part in range(2)
                ]
                tiles[c, slot, 0] = (with_real[:side] + with_imag[side:]) * scale
                tiles[c, slot, 1] = (with_real[side:] - with_imag[:side]) * scale
                copy_out(tiles.at[c, slot], c, slot).start()

    for slot in range(slots):
        for c in range(coarse):
            copy_out(empty, c, slot).wait()


def correlate(table, gathered, first, channels, chunks, single, slots, vis):
    half, senders, _, spectra, rows, lanes = gathered[0].shape
    coarse = 1 if single else lanes // AVG
    side = senders * rows * (chunks if single else 1)
    vmem = pl.BlockSpec(memory_space=pltpu.VMEM)
    anywhere = pl.BlockSpec(memory_space=pl.ANY)
    args = [table, *gathered]
    aliases = {}
    if vis is not None:
        args.append(vis)
        aliases = {len(args) - 1: 0}
    return pl.pallas_call(
        functools.partial(correlate_kernel, chunks, single, 1.0 / (AVG * spectra), first),
        grid_spec=pltpu.PrefetchScalarGridSpec(
            num_scalar_prefetch=1,
            grid=(),
            in_specs=[vmem, vmem] + [anywhere] * (len(args) - 3),
            out_specs=[anywhere, vmem],
            scratch_shapes=[
                pltpu.VMEM((coarse, 2 * half, 2 * side, spectra * AVG), jnp.bfloat16),
                pltpu.VMEM((coarse, slots, 2, side, side), jnp.float32),
                pltpu.VMEM((2, side, side), jnp.float32),
                pltpu.SemaphoreType.DMA((coarse, slots)),
            ],
        ),
        out_shape=[
            jax.ShapeDtypeStruct((2, channels, slots, side, side), jnp.float32),
            jax.ShapeDtypeStruct((8, LANES), jnp.float32),
        ],
        input_output_aliases=aliases,
        cost_estimate=pl.CostEstimate(flops=0, bytes_accessed=0, transcendentals=0),
        compiler_params=pltpu.CompilerParams(vmem_limit_bytes=VMEM_BYTES),
        name="correlate_tiles",
    )(*args)


def places(count):
    steps = np.arange(count, dtype=np.int32)
    index = lax.axis_index("ft").astype(jnp.int32)
    return jnp.concatenate([(index + steps) % count, (index + count - steps) % count])


def spread(pieces):
    count = len(pieces)
    return [pieces[0]] + [
        lax.ppermute(pieces[d], "ft", [(i, (i + d) % count) for i in range(count)])
        for d in range(1, count)
    ]


def exchange(own, bit):
    count = lax.axis_size("bl")
    return lax.ppermute(own, "bl", [(i, i ^ bit) for i in range(count)])


def gather_blocks(held, after):
    bit = lax.axis_size("bl") // 4
    other = exchange(held, bit)
    while bit > 1:
        bit //= 2
        held = pair(held, other, after).reshape(-1, *held.shape[1:])
        other = exchange(held, bit)
    return held, other


def block_order(count):
    order, bit = [0], count // 2
    while bit:
        order += [r ^ bit for r in order]
        bit //= 2
    return order


def tile_tables(block_ids, tile_owner):
    block_count = lax.axis_size("bl")
    tile_count = block_count * (block_count + 1) // 2
    slot_cap = 2 * tile_count // block_count
    pairs = [(i, j) for i in range(block_count) for j in range(i, block_count)]
    row_table = np.array([i for i, _ in pairs], np.int32)
    col_table = np.array([j for _, j in pairs], np.int32)
    mine = (tile_owner == lax.axis_index("bl")).astype(jnp.int32)
    earlier = np.tril(np.ones((tile_count, tile_count), np.int32), -1)
    rank = jnp.sum(earlier * mine[None, :], axis=1)
    labels = np.arange(block_count, dtype=np.int32)
    shard_of = jnp.sum(jnp.where(block_ids[None, :] == labels[:, None], labels[None, :], 0), axis=1)
    row_shard = jnp.sum(
        jnp.where(row_table[:, None] == labels[None, :], shard_of[None, :], 0), axis=1
    )
    col_shard = jnp.sum(
        jnp.where(col_table[:, None] == labels[None, :], shard_of[None, :], 0), axis=1
    )
    here = (mine[None, :] == 1) & (rank[None, :] == np.arange(slot_cap, dtype=np.int32)[:, None])
    rows = jnp.sum(jnp.where(here, row_shard[None, :], 0), axis=1)
    cols = jnp.sum(jnp.where(here, col_shard[None, :], 0), axis=1)
    index = lax.axis_index("bl")
    table = jnp.concatenate(
        [rows ^ index, cols ^ index, jnp.sum(mine, keepdims=True)]
    ).astype(jnp.int32)
    return table, slot_cap


def takes_kernels(mesh, voltages, coefs):
    dests = mesh.shape["ft"]
    blocks = mesh.shape["bl"]
    inputs = voltages.shape[2] // mesh.shape["bl"]
    per_dev = voltages.shape[1] // (mesh.shape["grp"] * dests)
    chan_count = coefs.shape[1]
    radix = chan_count // MXU
    return (
        per_dev == chan_count
        and chan_count % MXU == 0
        and radix & (radix - 1) == 0
        and radix % dests == 0
        and radix <= 8
        and blocks & (blocks - 1) == 0
        and blocks > 2
        and inputs == 2 * LANES
        and LANES == 2 * AVG
        and radix // dests * MXU // LANES > 1
        and MXU > LANES
        and LANES % dests == 0
        and (LANES // dests) % ROWS16 == 0
        and (dests * AVG) % LANES == 0
    )


def per_device_kernels(voltages, coefs, block_ids, tile_owner):
    dests = lax.axis_size("ft")
    taps, chan_count = coefs.shape
    radix = chan_count // MXU
    chunks = voltages.shape[2] // LANES
    coef_table = coefs.reshape(taps, MXU, radix).transpose(0, 2, 1)
    place = places(dests)
    table, slot_cap = tile_tables(block_ids, tile_owner)
    matrix, twiddle = matrix_tables(MXU), twiddle_tables(radix, MXU)
    cuts = MXU // LANES
    tables = []
    for cut in range(cuts):
        at = slice(cut * LANES, (cut + 1) * LANES)
        tables.append(np.ascontiguousarray(twiddle[:, :, at]))
        tables.append(np.concatenate([matrix[:, :MXU][:, at], matrix[:, MXU:][:, at]], axis=1))
    coef_table, *tables = stage(coef_table, *tables)
    arrived = spread(pack(voltages, place, dests, radix))
    _, rows, samples = arrived[0].shape
    sizes = (dests, dests, rows, samples, radix)
    made, split = transform_cut(arrived, place, coef_table, tables, 0, sizes, table)
    firsts = [table]
    for cut in range(1, cuts):
        more, _ = transform_cut(split, place, None, tables, cut, sizes, table)
        made = made + more
        firsts.append(more[0][0])
    half = lax.axis_size("bl") // 2
    units = len(made)
    own, other, arrived, tokens, vis = None, None, None, [], None
    for unit in range(units + 1):
        held = None
        if unit < units:
            parts = made[unit]
            if unit > 1:
                parts, _ = lax.optimization_barrier((parts, arrived))
            arrived = spread(parts)
            after = tokens[-1] if tokens else table
            if unit > 0:
                own, held = join(arrived, place, (own, other), after)
            else:
                (own,) = join(arrived, place, (), firsts[-1])
            other = exchange(own, half)
        else:
            held = pair(own, other, tokens[-1])
        if unit > 0:
            gathered = gather_blocks(held, table)
            single = unit > units - 2
            cut, part = divmod(min(unit, units - 1) - 1, radix // dests)
            first = (part * MXU + cut * LANES) // AVG + (1 if unit == units else 0)
            vis, token = correlate(
                table, gathered, first, samples // dests // AVG, chunks, single, slot_cap, vis
            )
            tokens.append(token)
    return vis


def tile_product(row_part, col_part, norm_scale):
    products = jnp.einsum(
        "pscax,qscay->cpqxy", row_part, col_part, preferred_element_type=jnp.float32
    )
    real_part = products[:, 0, 0] + products[:, 1, 1]
    imag_part = products[:, 1, 0] - products[:, 0, 1]
    return jnp.stack([real_part, imag_part]) * norm_scale


def dft_tables(order_len):
    steps_one = jnp.arange(order_len, dtype=jnp.int32)
    phase_grid = steps_one[:, None] * steps_one[None, :] % order_len
    angles = phase_grid.astype(jnp.float32) * (2.0 * math.pi / order_len)
    return (jnp.cos(angles), jnp.sin(angles))


def transform(filtered):
    per_dev = filtered.shape[1]
    chan_count = filtered.shape[2]
    rows_here = filtered.shape[3]
    outer_len = math.isqrt(chan_count)
    while chan_count % outer_len != 0:
        outer_len = outer_len - 1
    inner_len = chan_count // outer_len
    highest = lax.Precision.HIGHEST
    reshaped = filtered.reshape(2, per_dev, outer_len, inner_len, rows_here)
    real_in = reshaped[0]
    imag_in = reshaped[1]
    cos_outer, sin_outer = dft_tables(outer_len)
    section_re = jnp.einsum("snkb,nm->smkb", real_in, cos_outer, precision=highest) + jnp.einsum(
        "snkb,nm->smkb", imag_in, sin_outer, precision=highest
    )
    section_im = jnp.einsum("snkb,nm->smkb", imag_in, cos_outer, precision=highest) - jnp.einsum(
        "snkb,nm->smkb", real_in, sin_outer, precision=highest
    )
    twiddle_grid = (
        jnp.arange(outer_len, dtype=jnp.int32)[:, None]
        * jnp.arange(inner_len, dtype=jnp.int32)[None, :]
        % chan_count
    )
    twiddle_angles = twiddle_grid.astype(jnp.float32) * (2.0 * math.pi / chan_count)
    cos_twiddle = jnp.cos(twiddle_angles)[None, :, :, None]
    sin_twiddle = jnp.sin(twiddle_angles)[None, :, :, None]
    rot_re = section_re * cos_twiddle + section_im * sin_twiddle
    rot_im = section_im * cos_twiddle - section_re * sin_twiddle
    cos_inner, sin_inner = dft_tables(inner_len)
    final_re = jnp.einsum("smkb,kq->sqmb", rot_re, cos_inner, precision=highest) + jnp.einsum(
        "smkb,kq->sqmb", rot_im, sin_inner, precision=highest
    )
    final_im = jnp.einsum("smkb,kq->sqmb", rot_im, cos_inner, precision=highest) - jnp.einsum(
        "smkb,kq->sqmb", rot_re, sin_inner, precision=highest
    )
    stacked = jnp.stack([final_re, final_im]).reshape(2, per_dev, chan_count, rows_here)
    return (stacked * (1.0 / math.sqrt(chan_count))).astype(jnp.bfloat16)


def apply_taps(window, coef_part, taps_count, out_len):
    filtered = jnp.zeros((2, out_len, window.shape[2], window.shape[3]), jnp.float32)
    for tap_index in range(taps_count):
        filtered = filtered + coef_part[tap_index][None, None, :, None] * window[
            :, tap_index : tap_index + out_len
        ].astype(jnp.float32)
    return filtered


def per_device(voltages, coefs, block_ids, tile_owner):
    taps_count = coefs.shape[0]
    chan_count = coefs.shape[1]
    rows_here = voltages.shape[2]
    per_dev = voltages.shape[1] // chan_count
    volt_blocks = voltages.reshape(2, per_dev, chan_count, rows_here)
    phase_block = lax.all_to_all(volt_blocks, "ft", split_axis=2, concat_axis=1, tiled=True)
    spectra_count = phase_block.shape[1]
    phase_here = phase_block.shape[2]
    coef_part = lax.dynamic_slice_in_dim(coefs, lax.axis_index("ft") * phase_here, phase_here, 1)
    zero_front = jnp.zeros((2, taps_count - 1, phase_here, rows_here), phase_block.dtype)
    long_window = jnp.concatenate([zero_front, phase_block], axis=1)
    phase_filtered = apply_taps(long_window, coef_part, taps_count, spectra_count)
    filtered = lax.all_to_all(phase_filtered, "ft", split_axis=1, concat_axis=2, tiled=True)
    spectra = transform(filtered)
    turned = lax.all_to_all(spectra, "ft", split_axis=2, concat_axis=1, tiled=True)
    spectra_all = turned.shape[1]
    chan_here = turned.shape[2]
    coarse_here = chan_here // AVG
    coarse_view = turned.reshape(2, spectra_all, coarse_here, AVG, rows_here)
    norm_scale = 1.0 / (AVG * spectra_all)
    block_count = lax.axis_size("bl")
    my_index = lax.axis_index("bl")
    tile_count = block_count * (block_count + 1) // 2
    slot_cap = 2 * tile_count // block_count
    row_table = jnp.asarray(
        np.array(
            [
                first_id
                for first_id in range(block_count)
                for second_id in range(first_id, block_count)
            ],
            dtype=np.int32,
        )
    )
    col_table = jnp.asarray(
        np.array(
            [
                second_id
                for first_id in range(block_count)
                for second_id in range(first_id, block_count)
            ],
            dtype=np.int32,
        )
    )
    tile_pos = jnp.arange(tile_count, dtype=jnp.int32)
    same_owner = tile_owner[None, :] == tile_owner[:, None]
    before_mask = tile_pos[None, :] < tile_pos[:, None]
    slot_rank = jnp.sum((same_owner & before_mask).astype(jnp.int32), axis=1)
    labels = jnp.arange(block_count, dtype=jnp.int32)
    shard_of = jnp.sum(jnp.where(block_ids[None, :] == labels[:, None], labels[None, :], 0), axis=1)
    gathered = lax.all_gather(coarse_view[None], "bl", axis=0, tiled=True)
    mine_mask = tile_owner == my_index
    own_count = jnp.sum(mine_mask.astype(jnp.int32))
    slot_steps = jnp.arange(slot_cap, dtype=jnp.int32)
    slot_tile = jnp.sum(
        jnp.where(
            mine_mask[None, :] & (slot_rank[None, :] == slot_steps[:, None]), tile_pos[None, :], 0
        ),
        axis=1,
    )

    def one_tile(slot_pos, result_tiles):
        tile_id = slot_tile[slot_pos]
        row_block = gathered[shard_of[row_table[tile_id]]]
        col_block = gathered[shard_of[col_table[tile_id]]]
        tile = tile_product(row_block, col_block, norm_scale)
        return lax.dynamic_update_slice(result_tiles, tile[:, :, None], (0, 0, slot_pos, 0, 0))

    empty_tiles = jnp.zeros((2, coarse_here, slot_cap, rows_here, rows_here), jnp.float32)
    return lax.fori_loop(0, own_count, one_tile, empty_tiles)


def solution(mesh):
    def correlator(voltages, coefs, block_ids, tile_owner):
        fits = takes_kernels(mesh, voltages, coefs)
        return jax.shard_map(
            per_device_kernels if fits else per_device,
            mesh=mesh,
            in_specs=(P(None, ("grp", "ft"), "bl"), P(), P(), P("grp")),
            out_specs=P(None, ("grp", "ft"), "bl", None, None),
            check_vma=False,
        )(voltages, coefs, block_ids, tile_owner)

    return correlator
```

```python
import functools
import math

import jax
import jax.numpy as jnp
import ml_dtypes
import numpy as np
from jax import lax
from jax.experimental import pallas as pl
from jax.experimental.pallas import tpu as pltpu
from jax.sharding import PartitionSpec as P

AVG = 64
MXU = 256
LANES = 128
ROWS16 = 16
VMEM_BYTES = 48 * 1024 * 1024


def split_bf16(table):
    high = table.astype(ml_dtypes.bfloat16)
    low = (table - high.astype(np.float64)).astype(ml_dtypes.bfloat16)
    return high, low


def matrix_tables(inner_len):
    steps = np.arange(inner_len)
    angles = 2.0 * np.pi * (np.outer(steps, steps) % inner_len) / inner_len
    cos_part, sin_part = np.cos(angles), np.sin(angles)
    high, low = split_bf16(np.block([[cos_part, -sin_part], [sin_part, cos_part]]))
    return np.concatenate([high, high, low])


def twiddle_tables(radix, inner_len):
    chan_count = radix * inner_len
    angles = 2.0 * np.pi * np.outer(np.arange(radix), np.arange(inner_len)) / chan_count
    scale = 1.0 / math.sqrt(chan_count)
    return np.stack([np.cos(angles) * scale, np.sin(angles) * scale]).astype(np.float32)


def rotate(real, imag, step, count):
    step = step % count
    if step == 0:
        return real, imag
    if 4 * step == count:
        return imag, -real
    if 2 * step == count:
        return -real, -imag
    if 4 * step == 3 * count:
        return -imag, real
    cos_step = math.cos(2.0 * math.pi * step / count)
    sin_step = math.sin(2.0 * math.pi * step / count)
    if 8 * step == count:
        return cos_step * (real + imag), cos_step * (imag - real)
    return cos_step * real + sin_step * imag, cos_step * imag - sin_step * real


def butterflies(parts):
    count = len(parts)
    if count == 1:
        return parts
    half = count // 2
    sums, diffs = [], []
    for k in range(half):
        (ar, ai), (br, bi) = parts[k], parts[k + half]
        sums.append((ar + br, ai + bi))
        diffs.append(rotate(ar - br, ai - bi, k, count))
    even, odd = butterflies(sums), butterflies(diffs)
    out = []
    for k in range(half):
        out += [even[k], odd[k]]
    return out


def pack_kernel(radix, place_ref, v_ref, *rest):
    o_refs, (wide, turned) = rest[:-2], rest[-2:]
    dests, rows, samples = turned.shape
    inner = samples // radix
    for part in range(2):
        for chunk in range(v_ref.shape[2] // LANES):
            wide[...] = v_ref[part, :, chunk * LANES : (chunk + 1) * LANES].astype(jnp.float32)
            for phase in range(radix):
                here = wide[pl.ds(phase, inner, stride=radix), :].T.astype(jnp.bfloat16)
                for dest in range(dests):
                    turned[dest, :, phase * inner : (phase + 1) * inner] = here[
                        dest * rows : (dest + 1) * rows
                    ]
            for shift in range(dests):
                o_refs[shift][part, chunk * rows : (chunk + 1) * rows] = turned[place_ref[shift]]


def pack(voltages, place, dests, radix):
    _, samples, inputs = voltages.shape
    chunks = inputs // LANES
    rows = LANES // dests
    vmem = pl.BlockSpec(memory_space=pltpu.VMEM)
    return pl.pallas_call(
        functools.partial(pack_kernel, radix),
        grid_spec=pltpu.PrefetchScalarGridSpec(
            num_scalar_prefetch=1,
            grid=(),
            in_specs=[vmem],
            out_specs=[vmem] * dests,
            scratch_shapes=[
                pltpu.VMEM((samples, LANES), jnp.float32),
                pltpu.VMEM((dests, rows, samples), jnp.bfloat16),
            ],
        ),
        out_shape=[jax.ShapeDtypeStruct((2, chunks * rows, samples), jnp.bfloat16)] * dests,
        compiler_params=pltpu.CompilerParams(vmem_limit_bytes=VMEM_BYTES // 2),
        name="pack_inputs",
    )(place, voltages)


def stage_kernel(*refs):
    half = len(refs) // 2
    for source, target in zip(refs[:half], refs[half:]):
        target[...] = source[...]


def stage(*tables):
    vmem = pl.BlockSpec(memory_space=pltpu.VMEM)
    return pl.pallas_call(
        stage_kernel,
        in_specs=[vmem] * len(tables),
        out_specs=[vmem] * len(tables),
        out_shape=[jax.ShapeDtypeStruct(table.shape, table.dtype) for table in tables],
        compiler_params=pltpu.CompilerParams(vmem_limit_bytes=VMEM_BYTES // 4),
        name="stage_tables",
    )(*tables)


def filter_blocks(place_ref, v_refs, c_ref, held, split):
    spectra, _, rows, samples = held.shape
    taps, radix, inner = c_ref.shape
    for shift in range(len(v_refs)):
        held[place_ref[len(v_refs) + shift]] = v_refs[shift][...]

    @pl.loop(0, radix)
    def _(phase):
        lane0 = pl.multiple_of(phase * inner, inner)
        row0 = pl.multiple_of(phase * spectra * rows, spectra * rows)
        for part in range(2):
            for sub in range(0, rows, ROWS16):
                blocks = [
                    held[b, part, pl.ds(sub, ROWS16), pl.ds(lane0, inner)].astype(jnp.float32)
                    for b in range(spectra)
                ]
                for s in range(spectra):
                    total = None
                    for b in range(max(0, s - taps + 1), s + 1):
                        term = c_ref[taps - 1 - s + b, pl.ds(phase, 1), :] * blocks[b]
                        total = term if total is None else total + term
                    high = total.astype(jnp.bfloat16)
                    low = (total - high.astype(jnp.float32)).astype(jnp.bfloat16)
                    at = pl.ds(pl.multiple_of(row0 + s * rows + sub, ROWS16), ROWS16)
                    split[at, part * inner : (part + 1) * inner] = high
                    split[at, (2 + part) * inner : (3 + part) * inner] = low


def transform_lanes(place_ref, split, tw_ref, g_ref, prod, made, out_refs):
    dests, halves, _, spectra, rows, _ = made.shape
    radix = tw_ref.shape[1]
    group = spectra * rows
    depth = split.shape[1] // 2

    @pl.loop(0, radix // 2)
    def _(pair):
        at = pl.ds(pl.multiple_of(pair * 2 * group, 2 * group), 2 * group)
        high = split[at, :depth]
        line = jnp.concatenate([high, split[at, depth:], high], axis=1)
        prod[at, :] = jnp.dot(line, g_ref[...], preferred_element_type=jnp.float32)

    @pl.loop(0, spectra)
    def _(s):
        for sub in range(0, rows, ROWS16):
            parts = []
            for phase in range(radix):
                at = pl.ds(pl.multiple_of(phase * group + s * rows + sub, ROWS16), ROWS16)
                yr, yi = prod[at, :LANES], prod[at, LANES:]
                cos_here = tw_ref[0, phase : phase + 1, :]
                sin_here = tw_ref[1, phase : phase + 1, :]
                if phase == 0:
                    parts.append((yr * cos_here, yi * cos_here))
                else:
                    parts.append((yr * cos_here + yi * sin_here, yi * cos_here - yr * sin_here))
            for step, pair in enumerate(butterflies(parts)):
                for part in range(2):
                    made[step // halves, step % halves, part, s, sub : sub + ROWS16, :] = pair[
                        part
                    ].astype(jnp.bfloat16)

    for shift in range(dests):
        for half in range(halves):
            out_refs[half * dests + shift][...] = made[place_ref[shift], half]


def transform_cut(source, place, coef_table, tables, cut, sizes, after):
    dests, spectra, rows, samples, radix = sizes
    inner = samples // radix
    halves = radix // dests
    total = radix * spectra * rows
    begins = coef_table is not None
    vmem = pl.BlockSpec(memory_space=pltpu.VMEM)

    def kernel(place_ref, *rest):
        if begins:
            v_refs, (c_ref, tw_ref, g_ref) = rest[:dests], rest[dests : dests + 3]
            out_refs, (split, held, prod, made) = rest[dests + 4 : -4], rest[-4:]
            filter_blocks(place_ref, v_refs, c_ref, held, split)
        else:
            split, tw_ref, g_ref = rest[:3]
            out_refs, (prod, made) = rest[4:-2], rest[-2:]
        transform_lanes(place_ref, split, tw_ref, g_ref, prod, made, out_refs)

    scratch = [
        pltpu.VMEM((total, 2 * LANES), jnp.float32),
        pltpu.VMEM((dests, halves, 2, spectra, rows, LANES), jnp.bfloat16),
    ]
    shapes = [jax.ShapeDtypeStruct((2, spectra, rows, LANES), jnp.bfloat16)] * (halves * dests)
    if begins:
        scratch = [pltpu.VMEM((spectra, 2, rows, samples), jnp.bfloat16)] + scratch
        shapes = shapes + [jax.ShapeDtypeStruct((total, 4 * inner), jnp.bfloat16)]
    args = [*source, coef_table] if begins else [source]
    args += [tables[2 * cut], tables[2 * cut + 1]]
    made = pl.pallas_call(
        kernel,
        grid_spec=pltpu.PrefetchScalarGridSpec(
            num_scalar_prefetch=1,
            grid=(),
            in_specs=[vmem] * len(args) + [pl.BlockSpec(memory_space=pl.ANY)],
            out_specs=[vmem] * len(shapes),
            scratch_shapes=scratch,
        ),
        out_shape=shapes,
        cost_estimate=pl.CostEstimate(
            flops=3 * 2 * total * 4 * inner * LANES, bytes_accessed=6 << 20, transcendentals=0
        ),
        compiler_params=pltpu.CompilerParams(vmem_limit_bytes=VMEM_BYTES // 2),
        name="filter_transform" if begins else "transform_rest",
    )(place, *args, after)
    units = [made[half * dests : (half + 1) * dests] for half in range(halves)]
    return units, made[-1]


def join(pieces, place, before, after):
    count = len(pieces)
    vmem = pl.BlockSpec(memory_space=pltpu.VMEM)
    shapes = [jax.ShapeDtypeStruct((count, *pieces[0].shape), pieces[0].dtype)]
    if before:
        shapes.append(jax.ShapeDtypeStruct((2, *before[0].shape), before[0].dtype))

    def kernel(place_ref, *rest):
        ins, outs = rest[: count + len(before)], rest[count + len(before) + 1 :]
        for shift in range(count):
            outs[0][place_ref[count + shift]] = ins[shift][...]
        for at in range(len(before)):
            outs[1][at] = ins[count + at][...]

    return pl.pallas_call(
        kernel,
        grid_spec=pltpu.PrefetchScalarGridSpec(
            num_scalar_prefetch=1,
            grid=(),
            in_specs=[vmem] * (count + len(before)) + [pl.BlockSpec(memory_space=pl.ANY)],
            out_specs=[vmem] * len(shapes),
        ),
        out_shape=shapes,
        compiler_params=pltpu.CompilerParams(vmem_limit_bytes=VMEM_BYTES // 4),
        name="join_pieces",
    )(place, *pieces, *before, after)


def pair(own, other, after):
    def kernel(own_ref, other_ref, _, out_ref):
        out_ref[0] = own_ref[...]
        out_ref[1] = other_ref[...]

    vmem = pl.BlockSpec(memory_space=pltpu.VMEM)
    return pl.pallas_call(
        kernel,
        in_specs=[vmem, vmem, pl.BlockSpec(memory_space=pl.ANY)],
        out_specs=vmem,
        out_shape=jax.ShapeDtypeStruct((2, *own.shape), own.dtype),
        compiler_params=pltpu.CompilerParams(vmem_limit_bytes=VMEM_BYTES // 4),
        name="pair_blocks",
    )(own, other, after)


def correlate_kernel(chunks, scale, first, table_ref, low_ref, high_ref, *rest):
    o_ref, token_ref, left, tiles, empty, sems = rest[-6:]
    half, senders, _, spectra, rows, lanes = low_ref.shape
    order = block_order(2 * half)
    slots = o_ref.shape[2]
    coarse = lanes // AVG
    side = senders * rows
    run = rows // chunks
    count = table_ref[2 * slots]
    token_ref[...] = jnp.zeros_like(token_ref)
    empty[...] = jnp.zeros_like(empty)

    def copy_out(source, c, slot):
        return pltpu.make_async_copy(source, o_ref.at[:, first + c, slot], sems.at[c, slot])

    for slot in range(slots):

        @pl.when(slot >= count)
        def _(slot=slot):
            for c in range(coarse):
                copy_out(empty, c, slot).start()

    for at, block in enumerate(order):
        source = (low_ref, high_ref)[at // half].at[at % half]
        for sender in range(senders):
            for part in range(2):
                for chunk in range(chunks):
                    row = part * side + (chunk * senders + sender) * run
                    pieces = [
                        source[sender, part, s, chunk * run : (chunk + 1) * run]
                        for s in range(spectra)
                    ]
                    for c in range(coarse):
                        left[c, block, row : row + run, :] = jnp.concatenate(
                            [piece[:, c * AVG : (c + 1) * AVG] for piece in pieces], axis=1
                        )

    for slot in range(slots):

        @pl.when(slot < count)
        def _(slot=slot):
            for c in range(coarse):
                rows_of = left[c, table_ref[slot]]
                with_real, with_imag = [
                    lax.dot_general(
                        rows_of,
                        left[c, table_ref[slots + slot], pl.ds(part * side, side), :],
                        (((1,), (1,)), ((), ())),
                        preferred_element_type=jnp.float32,
                    )
                    for part in range(2)
                ]
                tiles[c, slot, 0] = (with_real[:side] + with_imag[side:]) * scale
                tiles[c, slot, 1] = (with_real[side:] - with_imag[:side]) * scale
                copy_out(tiles.at[c, slot], c, slot).start()

    for slot in range(slots):
        for c in range(coarse):
            copy_out(empty, c, slot).wait()


def correlate(table, gathered, first, channels, chunks, slots, vis):
    half, senders, _, spectra, rows, lanes = gathered[0].shape
    coarse = lanes // AVG
    side = senders * rows
    vmem = pl.BlockSpec(memory_space=pltpu.VMEM)
    anywhere = pl.BlockSpec(memory_space=pl.ANY)
    args = [table, *gathered]
    aliases = {}
    if vis is not None:
        args.append(vis)
        aliases = {len(args) - 1: 0}
    return pl.pallas_call(
        functools.partial(correlate_kernel, chunks, 1.0 / (AVG * spectra), first),
        grid_spec=pltpu.PrefetchScalarGridSpec(
            num_scalar_prefetch=1,
            grid=(),
            in_specs=[vmem, vmem] + [anywhere] * (len(args) - 3),
            out_specs=[anywhere, vmem],
            scratch_shapes=[
                pltpu.VMEM((coarse, 2 * half, 2 * side, spectra * AVG), jnp.bfloat16),
                pltpu.VMEM((coarse, slots, 2, side, side), jnp.float32),
                pltpu.VMEM((2, side, side), jnp.float32),
                pltpu.SemaphoreType.DMA((coarse, slots)),
            ],
        ),
        out_shape=[
            jax.ShapeDtypeStruct((2, channels, slots, side, side), jnp.float32),
            jax.ShapeDtypeStruct((8, LANES), jnp.float32),
        ],
        input_output_aliases=aliases,
        cost_estimate=pl.CostEstimate(flops=0, bytes_accessed=0, transcendentals=0),
        compiler_params=pltpu.CompilerParams(vmem_limit_bytes=VMEM_BYTES),
        name="correlate_tiles",
    )(*args)


def places(count):
    steps = np.arange(count, dtype=np.int32)
    index = lax.axis_index("ft").astype(jnp.int32)
    return jnp.concatenate([(index + steps) % count, (index + count - steps) % count])


def spread(pieces):
    count = len(pieces)
    return [pieces[0]] + [
        lax.ppermute(pieces[d], "ft", [(i, (i + d) % count) for i in range(count)])
        for d in range(1, count)
    ]


def exchange(own, bit):
    count = lax.axis_size("bl")
    return lax.ppermute(own, "bl", [(i, i ^ bit) for i in range(count)])


def gather_blocks(held, after):
    bit = lax.axis_size("bl") // 4
    other = exchange(held, bit)
    while bit > 1:
        bit //= 2
        held = pair(held, other, after).reshape(-1, *held.shape[1:])
        other = exchange(held, bit)
    return held, other


def block_order(count):
    order, bit = [0], count // 2
    while bit:
        order += [r ^ bit for r in order]
        bit //= 2
    return order


def tile_tables(block_ids, tile_owner):
    block_count = lax.axis_size("bl")
    tile_count = block_count * (block_count + 1) // 2
    slot_cap = 2 * tile_count // block_count
    pairs = [(i, j) for i in range(block_count) for j in range(i, block_count)]
    row_table = np.array([i for i, _ in pairs], np.int32)
    col_table = np.array([j for _, j in pairs], np.int32)
    mine = (tile_owner == lax.axis_index("bl")).astype(jnp.int32)
    earlier = np.tril(np.ones((tile_count, tile_count), np.int32), -1)
    rank = jnp.sum(earlier * mine[None, :], axis=1)
    labels = np.arange(block_count, dtype=np.int32)
    shard_of = jnp.sum(jnp.where(block_ids[None, :] == labels[:, None], labels[None, :], 0), axis=1)
    row_shard = jnp.sum(
        jnp.where(row_table[:, None] == labels[None, :], shard_of[None, :], 0), axis=1
    )
    col_shard = jnp.sum(
        jnp.where(col_table[:, None] == labels[None, :], shard_of[None, :], 0), axis=1
    )
    here = (mine[None, :] == 1) & (rank[None, :] == np.arange(slot_cap, dtype=np.int32)[:, None])
    rows = jnp.sum(jnp.where(here, row_shard[None, :], 0), axis=1)
    cols = jnp.sum(jnp.where(here, col_shard[None, :], 0), axis=1)
    index = lax.axis_index("bl")
    table = jnp.concatenate(
        [rows ^ index, cols ^ index, jnp.sum(mine, keepdims=True)]
    ).astype(jnp.int32)
    return table, slot_cap


def takes_kernels(mesh, voltages, coefs):
    dests = mesh.shape["ft"]
    blocks = mesh.shape["bl"]
    inputs = voltages.shape[2] // mesh.shape["bl"]
    per_dev = voltages.shape[1] // (mesh.shape["grp"] * dests)
    chan_count = coefs.shape[1]
    radix = chan_count // MXU
    return (
        per_dev == chan_count
        and chan_count % MXU == 0
        and radix & (radix - 1) == 0
        and radix % dests == 0
        and radix <= 8
        and blocks & (blocks - 1) == 0
        and blocks > 2
        and inputs % LANES == 0
        and LANES % dests == 0
        and (LANES // dests) % ROWS16 == 0
        and (dests * AVG) % LANES == 0
    )


def per_device_kernels(voltages, coefs, block_ids, tile_owner):
    dests = lax.axis_size("ft")
    taps, chan_count = coefs.shape
    radix = chan_count // MXU
    chunks = voltages.shape[2] // LANES
    coef_table = coefs.reshape(taps, MXU, radix).transpose(0, 2, 1)
    place = places(dests)
    table, slot_cap = tile_tables(block_ids, tile_owner)
    matrix, twiddle = matrix_tables(MXU), twiddle_tables(radix, MXU)
    cuts = MXU // LANES
    tables = []
    for cut in range(cuts):
        at = slice(cut * LANES, (cut + 1) * LANES)
        tables.append(np.ascontiguousarray(twiddle[:, :, at]))
        tables.append(np.concatenate([matrix[:, :MXU][:, at], matrix[:, MXU:][:, at]], axis=1))
    coef_table, *tables = stage(coef_table, *tables)
    arrived = spread(pack(voltages, place, dests, radix))
    _, rows, samples = arrived[0].shape
    sizes = (dests, dests, rows, samples, radix)
    made, split = transform_cut(arrived, place, coef_table, tables, 0, sizes, table)
    firsts = [table]
    for cut in range(1, cuts):
        more, _ = transform_cut(split, place, None, tables, cut, sizes, table)
        made = made + more
        firsts.append(more[0][0])
    half = lax.axis_size("bl") // 2
    units = len(made)
    own, other, arrived, tokens, vis = None, None, None, [], None
    for unit in range(units + 1):
        held = None
        if unit < units:
            parts = made[unit]
            if unit > 1:
                parts, _ = lax.optimization_barrier((parts, arrived))
            arrived = spread(parts)
            after = tokens[-1] if tokens else table
            if unit > 0:
                own, held = join(arrived, place, (own, other), after)
            else:
                (own,) = join(arrived, place, (), firsts[-1])
            other = exchange(own, half)
        else:
            held = pair(own, other, tokens[-1])
        if unit > 0:
            gathered = gather_blocks(held, table)
            cut, part = divmod(unit - 1, radix // dests)
            first = (part * MXU + cut * LANES) // AVG
            vis, token = correlate(
                table, gathered, first, units * LANES // AVG, chunks, slot_cap, vis
            )
            tokens.append(token)
    return vis


def tile_product(row_part, col_part, norm_scale):
    products = jnp.einsum(
        "pscax,qscay->cpqxy", row_part, col_part, preferred_element_type=jnp.float32
    )
    real_part = products[:, 0, 0] + products[:, 1, 1]
    imag_part = products[:, 1, 0] - products[:, 0, 1]
    return jnp.stack([real_part, imag_part]) * norm_scale


def dft_tables(order_len):
    steps_one = jnp.arange(order_len, dtype=jnp.int32)
    phase_grid = steps_one[:, None] * steps_one[None, :] % order_len
    angles = phase_grid.astype(jnp.float32) * (2.0 * math.pi / order_len)
    return (jnp.cos(angles), jnp.sin(angles))


def transform(filtered):
    per_dev = filtered.shape[1]
    chan_count = filtered.shape[2]
    rows_here = filtered.shape[3]
    outer_len = math.isqrt(chan_count)
    while chan_count % outer_len != 0:
        outer_len = outer_len - 1
    inner_len = chan_count // outer_len
    highest = lax.Precision.HIGHEST
    reshaped = filtered.reshape(2, per_dev, outer_len, inner_len, rows_here)
    real_in = reshaped[0]
    imag_in = reshaped[1]
    cos_outer, sin_outer = dft_tables(outer_len)
    section_re = jnp.einsum("snkb,nm->smkb", real_in, cos_outer, precision=highest) + jnp.einsum(
        "snkb,nm->smkb", imag_in, sin_outer, precision=highest
    )
    section_im = jnp.einsum("snkb,nm->smkb", imag_in, cos_outer, precision=highest) - jnp.einsum(
        "snkb,nm->smkb", real_in, sin_outer, precision=highest
    )
    twiddle_grid = (
        jnp.arange(outer_len, dtype=jnp.int32)[:, None]
        * jnp.arange(inner_len, dtype=jnp.int32)[None, :]
        % chan_count
    )
    twiddle_angles = twiddle_grid.astype(jnp.float32) * (2.0 * math.pi / chan_count)
    cos_twiddle = jnp.cos(twiddle_angles)[None, :, :, None]
    sin_twiddle = jnp.sin(twiddle_angles)[None, :, :, None]
    rot_re = section_re * cos_twiddle + section_im * sin_twiddle
    rot_im = section_im * cos_twiddle - section_re * sin_twiddle
    cos_inner, sin_inner = dft_tables(inner_len)
    final_re = jnp.einsum("smkb,kq->sqmb", rot_re, cos_inner, precision=highest) + jnp.einsum(
        "smkb,kq->sqmb", rot_im, sin_inner, precision=highest
    )
    final_im = jnp.einsum("smkb,kq->sqmb", rot_im, cos_inner, precision=highest) - jnp.einsum(
        "smkb,kq->sqmb", rot_re, sin_inner, precision=highest
    )
    stacked = jnp.stack([final_re, final_im]).reshape(2, per_dev, chan_count, rows_here)
    return (stacked * (1.0 / math.sqrt(chan_count))).astype(jnp.bfloat16)


def apply_taps(window, coef_part, taps_count, out_len):
    filtered = jnp.zeros((2, out_len, window.shape[2], window.shape[3]), jnp.float32)
    for tap_index in range(taps_count):
        filtered = filtered + coef_part[tap_index][None, None, :, None] * window[
            :, tap_index : tap_index + out_len
        ].astype(jnp.float32)
    return filtered


def per_device(voltages, coefs, block_ids, tile_owner):
    taps_count = coefs.shape[0]
    chan_count = coefs.shape[1]
    rows_here = voltages.shape[2]
    per_dev = voltages.shape[1] // chan_count
    volt_blocks = voltages.reshape(2, per_dev, chan_count, rows_here)
    phase_block = lax.all_to_all(volt_blocks, "ft", split_axis=2, concat_axis=1, tiled=True)
    spectra_count = phase_block.shape[1]
    phase_here = phase_block.shape[2]
    coef_part = lax.dynamic_slice_in_dim(coefs, lax.axis_index("ft") * phase_here, phase_here, 1)
    zero_front = jnp.zeros((2, taps_count - 1, phase_here, rows_here), phase_block.dtype)
    long_window = jnp.concatenate([zero_front, phase_block], axis=1)
    phase_filtered = apply_taps(long_window, coef_part, taps_count, spectra_count)
    filtered = lax.all_to_all(phase_filtered, "ft", split_axis=1, concat_axis=2, tiled=True)
    spectra = transform(filtered)
    turned = lax.all_to_all(spectra, "ft", split_axis=2, concat_axis=1, tiled=True)
    spectra_all = turned.shape[1]
    chan_here = turned.shape[2]
    coarse_here = chan_here // AVG
    coarse_view = turned.reshape(2, spectra_all, coarse_here, AVG, rows_here)
    norm_scale = 1.0 / (AVG * spectra_all)
    block_count = lax.axis_size("bl")
    my_index = lax.axis_index("bl")
    tile_count = block_count * (block_count + 1) // 2
    slot_cap = 2 * tile_count // block_count
    row_table = jnp.asarray(
        np.array(
            [
                first_id
                for first_id in range(block_count)
                for second_id in range(first_id, block_count)
            ],
            dtype=np.int32,
        )
    )
    col_table = jnp.asarray(
        np.array(
            [
                second_id
                for first_id in range(block_count)
                for second_id in range(first_id, block_count)
            ],
            dtype=np.int32,
        )
    )
    tile_pos = jnp.arange(tile_count, dtype=jnp.int32)
    same_owner = tile_owner[None, :] == tile_owner[:, None]
    before_mask = tile_pos[None, :] < tile_pos[:, None]
    slot_rank = jnp.sum((same_owner & before_mask).astype(jnp.int32), axis=1)
    labels = jnp.arange(block_count, dtype=jnp.int32)
    shard_of = jnp.sum(jnp.where(block_ids[None, :] == labels[:, None], labels[None, :], 0), axis=1)
    gathered = lax.all_gather(coarse_view[None], "bl", axis=0, tiled=True)
    mine_mask = tile_owner == my_index
    own_count = jnp.sum(mine_mask.astype(jnp.int32))
    slot_steps = jnp.arange(slot_cap, dtype=jnp.int32)
    slot_tile = jnp.sum(
        jnp.where(
            mine_mask[None, :] & (slot_rank[None, :] == slot_steps[:, None]), tile_pos[None, :], 0
        ),
        axis=1,
    )

    def one_tile(slot_pos, result_tiles):
        tile_id = slot_tile[slot_pos]
        row_block = gathered[shard_of[row_table[tile_id]]]
        col_block = gathered[shard_of[col_table[tile_id]]]
        tile = tile_product(row_block, col_block, norm_scale)
        return lax.dynamic_update_slice(result_tiles, tile[:, :, None], (0, 0, slot_pos, 0, 0))

    empty_tiles = jnp.zeros((2, coarse_here, slot_cap, rows_here, rows_here), jnp.float32)
    return lax.fori_loop(0, own_count, one_tile, empty_tiles)


def solution(mesh):
    def correlator(voltages, coefs, block_ids, tile_owner):
        fits = takes_kernels(mesh, voltages, coefs)
        return jax.shard_map(
            per_device_kernels if fits else per_device,
            mesh=mesh,
            in_specs=(P(None, ("grp", "ft"), "bl"), P(), P(), P("grp")),
            out_specs=P(None, ("grp", "ft"), "bl", None, None),
            check_vma=False,
        )(voltages, coefs, block_ids, tile_owner)

    return correlator
```

```python
import functools
import math

import jax
import jax.numpy as jnp
import ml_dtypes
import numpy as np
from jax import lax
from jax.experimental import pallas as pl
from jax.experimental.pallas import tpu as pltpu
from jax.sharding import PartitionSpec as P

AVG = 64
MXU = 256
LANES = 128
ROWS16 = 16
VMEM_BYTES = 48 * 1024 * 1024


def split_bf16(table):
    high = table.astype(ml_dtypes.bfloat16)
    low = (table - high.astype(np.float64)).astype(ml_dtypes.bfloat16)
    return high, low


def matrix_tables(inner_len):
    steps = np.arange(inner_len)
    angles = 2.0 * np.pi * (np.outer(steps, steps) % inner_len) / inner_len
    cos_part, sin_part = np.cos(angles), np.sin(angles)
    high, low = split_bf16(np.block([[cos_part, -sin_part], [sin_part, cos_part]]))
    return np.concatenate([high, high, low])


def twiddle_tables(radix, inner_len):
    chan_count = radix * inner_len
    angles = 2.0 * np.pi * np.outer(np.arange(radix), np.arange(inner_len)) / chan_count
    scale = 1.0 / math.sqrt(chan_count)
    return np.stack([np.cos(angles) * scale, np.sin(angles) * scale]).astype(np.float32)


def rotate(real, imag, step, count):
    step = step % count
    if step == 0:
        return real, imag
    if 4 * step == count:
        return imag, -real
    if 2 * step == count:
        return -real, -imag
    if 4 * step == 3 * count:
        return -imag, real
    cos_step = math.cos(2.0 * math.pi * step / count)
    sin_step = math.sin(2.0 * math.pi * step / count)
    if 8 * step == count:
        return cos_step * (real + imag), cos_step * (imag - real)
    return cos_step * real + sin_step * imag, cos_step * imag - sin_step * real


def butterflies(parts):
    count = len(parts)
    if count == 1:
        return parts
    half = count // 2
    sums, diffs = [], []
    for k in range(half):
        (ar, ai), (br, bi) = parts[k], parts[k + half]
        sums.append((ar + br, ai + bi))
        diffs.append(rotate(ar - br, ai - bi, k, count))
    even, odd = butterflies(sums), butterflies(diffs)
    out = []
    for k in range(half):
        out += [even[k], odd[k]]
    return out


def pack_kernel(radix, place_ref, v_ref, *rest):
    o_refs, (wide, turned) = rest[:-2], rest[-2:]
    dests, rows, samples = turned.shape
    inner = samples // radix
    for part in range(2):
        for chunk in range(v_ref.shape[2] // LANES):
            wide[...] = v_ref[part, :, chunk * LANES : (chunk + 1) * LANES].astype(jnp.float32)
            for phase in range(radix):
                here = wide[pl.ds(phase, inner, stride=radix), :].T.astype(jnp.bfloat16)
                for dest in range(dests):
                    turned[dest, :, phase * inner : (phase + 1) * inner] = here[
                        dest * rows : (dest + 1) * rows
                    ]
            for shift in range(dests):
                o_refs[shift][part, chunk * rows : (chunk + 1) * rows] = turned[place_ref[shift]]


def pack(voltages, place, dests, radix):
    _, samples, inputs = voltages.shape
    chunks = inputs // LANES
    rows = LANES // dests
    vmem = pl.BlockSpec(memory_space=pltpu.VMEM)
    return pl.pallas_call(
        functools.partial(pack_kernel, radix),
        grid_spec=pltpu.PrefetchScalarGridSpec(
            num_scalar_prefetch=1,
            grid=(),
            in_specs=[vmem],
            out_specs=[vmem] * dests,
            scratch_shapes=[
                pltpu.VMEM((samples, LANES), jnp.float32),
                pltpu.VMEM((dests, rows, samples), jnp.bfloat16),
            ],
        ),
        out_shape=[jax.ShapeDtypeStruct((2, chunks * rows, samples), jnp.bfloat16)] * dests,
        compiler_params=pltpu.CompilerParams(vmem_limit_bytes=VMEM_BYTES // 2),
        name="pack_inputs",
    )(place, voltages)


def stage_kernel(*refs):
    half = len(refs) // 2
    for source, target in zip(refs[:half], refs[half:]):
        target[...] = source[...]


def stage(*tables):
    vmem = pl.BlockSpec(memory_space=pltpu.VMEM)
    return pl.pallas_call(
        stage_kernel,
        in_specs=[vmem] * len(tables),
        out_specs=[vmem] * len(tables),
        out_shape=[jax.ShapeDtypeStruct(table.shape, table.dtype) for table in tables],
        compiler_params=pltpu.CompilerParams(vmem_limit_bytes=VMEM_BYTES // 4),
        name="stage_tables",
    )(*tables)


def filter_blocks(place_ref, v_refs, c_ref, held, split):
    spectra, _, rows, samples = held.shape
    taps, radix, inner = c_ref.shape
    for shift in range(len(v_refs)):
        held[place_ref[shift]] = v_refs[shift][...]

    @pl.loop(0, radix)
    def _(phase):
        lane0 = pl.multiple_of(phase * inner, inner)
        row0 = pl.multiple_of(phase * spectra * rows, spectra * rows)
        for part in range(2):
            for sub in range(0, rows, ROWS16):
                blocks = [
                    held[b, part, pl.ds(sub, ROWS16), pl.ds(lane0, inner)].astype(jnp.float32)
                    for b in range(spectra)
                ]
                for s in range(spectra):
                    total = None
                    for b in range(max(0, s - taps + 1), s + 1):
                        term = c_ref[taps - 1 - s + b, pl.ds(phase, 1), :] * blocks[b]
                        total = term if total is None else total + term
                    high = total.astype(jnp.bfloat16)
                    low = (total - high.astype(jnp.float32)).astype(jnp.bfloat16)
                    at = pl.ds(pl.multiple_of(row0 + s * rows + sub, ROWS16), ROWS16)
                    split[at, part * inner : (part + 1) * inner] = high
                    split[at, (2 + part) * inner : (3 + part) * inner] = low


def transform_lanes(place_ref, split, tw_ref, g_ref, prod, made, out_refs):
    dests, halves, _, spectra, rows, _ = made.shape
    radix = tw_ref.shape[1]
    group = spectra * rows
    depth = split.shape[1] // 2

    @pl.loop(0, radix // 2)
    def _(pair):
        at = pl.ds(pl.multiple_of(pair * 2 * group, 2 * group), 2 * group)
        high = split[at, :depth]
        line = jnp.concatenate([high, split[at, depth:], high], axis=1)
        prod[at, :] = jnp.dot(line, g_ref[...], preferred_element_type=jnp.float32)

    @pl.loop(0, spectra)
    def _(s):
        for sub in range(0, rows, ROWS16):
            parts = []
            for phase in range(radix):
                at = pl.ds(pl.multiple_of(phase * group + s * rows + sub, ROWS16), ROWS16)
                yr, yi = prod[at, :LANES], prod[at, LANES:]
                cos_here = tw_ref[0, phase : phase + 1, :]
                sin_here = tw_ref[1, phase : phase + 1, :]
                if phase == 0:
                    parts.append((yr * cos_here, yi * cos_here))
                else:
                    parts.append((yr * cos_here + yi * sin_here, yi * cos_here - yr * sin_here))
            for step, pair in enumerate(butterflies(parts)):
                for part in range(2):
                    made[step // halves, step % halves, part, s, sub : sub + ROWS16, :] = pair[
                        part
                    ].astype(jnp.bfloat16)

    for shift in range(dests):
        for half in range(halves):
            out_refs[half * dests + shift][...] = made[place_ref[shift], half]


def transform_cut(source, place, coef_table, tables, cut, sizes, after):
    dests, spectra, rows, samples, radix = sizes
    inner = samples // radix
    halves = radix // dests
    total = radix * spectra * rows
    begins = coef_table is not None
    vmem = pl.BlockSpec(memory_space=pltpu.VMEM)

    def kernel(place_ref, *rest):
        if begins:
            v_refs, (c_ref, tw_ref, g_ref) = rest[:dests], rest[dests : dests + 3]
            out_refs, (split, held, prod, made) = rest[dests + 4 : -4], rest[-4:]
            filter_blocks(place_ref, v_refs, c_ref, held, split)
        else:
            split, tw_ref, g_ref = rest[:3]
            out_refs, (prod, made) = rest[4:-2], rest[-2:]
        transform_lanes(place_ref, split, tw_ref, g_ref, prod, made, out_refs)

    scratch = [
        pltpu.VMEM((total, 2 * LANES), jnp.float32),
        pltpu.VMEM((dests, halves, 2, spectra, rows, LANES), jnp.bfloat16),
    ]
    shapes = [jax.ShapeDtypeStruct((2, spectra, rows, LANES), jnp.bfloat16)] * (halves * dests)
    if begins:
        scratch = [pltpu.VMEM((spectra, 2, rows, samples), jnp.bfloat16)] + scratch
        shapes = shapes + [jax.ShapeDtypeStruct((total, 4 * inner), jnp.bfloat16)]
    args = [*source, coef_table] if begins else [source]
    args += [tables[2 * cut], tables[2 * cut + 1]]
    made = pl.pallas_call(
        kernel,
        grid_spec=pltpu.PrefetchScalarGridSpec(
            num_scalar_prefetch=1,
            grid=(),
            in_specs=[vmem] * len(args) + [pl.BlockSpec(memory_space=pl.ANY)],
            out_specs=[vmem] * len(shapes),
            scratch_shapes=scratch,
        ),
        out_shape=shapes,
        cost_estimate=pl.CostEstimate(
            flops=3 * 2 * total * 4 * inner * LANES, bytes_accessed=6 << 20, transcendentals=0
        ),
        compiler_params=pltpu.CompilerParams(vmem_limit_bytes=VMEM_BYTES // 2),
        name="filter_transform" if begins else "transform_rest",
    )(place, *args, after)
    units = [made[half * dests : (half + 1) * dests] for half in range(halves)]
    return units, made[-1]


def join(pieces, place, before, after):
    count = len(pieces)
    vmem = pl.BlockSpec(memory_space=pltpu.VMEM)
    shapes = [jax.ShapeDtypeStruct((count, *pieces[0].shape), pieces[0].dtype)]
    if before:
        shapes.append(jax.ShapeDtypeStruct((2, *before[0].shape), before[0].dtype))

    def kernel(place_ref, *rest):
        ins, outs = rest[: count + len(before)], rest[count + len(before) + 1 :]
        for shift in range(count):
            outs[0][place_ref[shift]] = ins[shift][...]
        for at in range(len(before)):
            outs[1][at] = ins[count + at][...]

    return pl.pallas_call(
        kernel,
        grid_spec=pltpu.PrefetchScalarGridSpec(
            num_scalar_prefetch=1,
            grid=(),
            in_specs=[vmem] * (count + len(before)) + [pl.BlockSpec(memory_space=pl.ANY)],
            out_specs=[vmem] * len(shapes),
        ),
        out_shape=shapes,
        compiler_params=pltpu.CompilerParams(vmem_limit_bytes=VMEM_BYTES // 4),
        name="join_pieces",
    )(place, *pieces, *before, after)


def pair(own, other, after):
    def kernel(own_ref, other_ref, _, out_ref):
        out_ref[0] = own_ref[...]
        out_ref[1] = other_ref[...]

    vmem = pl.BlockSpec(memory_space=pltpu.VMEM)
    return pl.pallas_call(
        kernel,
        in_specs=[vmem, vmem, pl.BlockSpec(memory_space=pl.ANY)],
        out_specs=vmem,
        out_shape=jax.ShapeDtypeStruct((2, *own.shape), own.dtype),
        compiler_params=pltpu.CompilerParams(vmem_limit_bytes=VMEM_BYTES // 4),
        name="pair_blocks",
    )(own, other, after)


def correlate_kernel(chunks, scale, first, table_ref, low_ref, high_ref, *rest):
    o_ref, token_ref, left, tiles, empty, sems = rest[-6:]
    half, senders, _, spectra, rows, lanes = low_ref.shape
    order = block_order(2 * half)
    slots = o_ref.shape[2]
    coarse = lanes // AVG
    side = senders * rows
    run = rows // chunks
    count = table_ref[2 * slots]
    token_ref[...] = jnp.zeros_like(token_ref)
    empty[...] = jnp.zeros_like(empty)

    def copy_out(source, c, slot):
        return pltpu.make_async_copy(source, o_ref.at[:, first + c, slot], sems.at[c, slot])

    for slot in range(slots):

        @pl.when(slot >= count)
        def _(slot=slot):
            for c in range(coarse):
                copy_out(empty, c, slot).start()

    for at, block in enumerate(order):
        source = (low_ref, high_ref)[at // half].at[at % half]
        for sender in range(senders):
            for part in range(2):
                for chunk in range(chunks):
                    row = part * side + (chunk * senders + sender) * run
                    pieces = [
                        source[sender, part, s, chunk * run : (chunk + 1) * run]
                        for s in range(spectra)
                    ]
                    for c in range(coarse):
                        left[c, block, row : row + run, :] = jnp.concatenate(
                            [piece[:, c * AVG : (c + 1) * AVG] for piece in pieces], axis=1
                        )

    for slot in range(slots):

        @pl.when(slot < count)
        def _(slot=slot):
            for c in range(coarse):
                rows_of = left[c, table_ref[slot]]
                with_real, with_imag = [
                    lax.dot_general(
                        rows_of,
                        left[c, table_ref[slots + slot], pl.ds(part * side, side), :],
                        (((1,), (1,)), ((), ())),
                        preferred_element_type=jnp.float32,
                    )
                    for part in range(2)
                ]
                tiles[c, slot, 0] = (with_real[:side] + with_imag[side:]) * scale
                tiles[c, slot, 1] = (with_real[side:] - with_imag[:side]) * scale
                copy_out(tiles.at[c, slot], c, slot).start()

    for slot in range(slots):
        for c in range(coarse):
            copy_out(empty, c, slot).wait()


def correlate(table, gathered, first, channels, chunks, slots, vis):
    half, senders, _, spectra, rows, lanes = gathered[0].shape
    coarse = lanes // AVG
    side = senders * rows
    vmem = pl.BlockSpec(memory_space=pltpu.VMEM)
    anywhere = pl.BlockSpec(memory_space=pl.ANY)
    args = [table, *gathered]
    aliases = {}
    if vis is not None:
        args.append(vis)
        aliases = {len(args) - 1: 0}
    return pl.pallas_call(
        functools.partial(correlate_kernel, chunks, 1.0 / (AVG * spectra), first),
        grid_spec=pltpu.PrefetchScalarGridSpec(
            num_scalar_prefetch=1,
            grid=(),
            in_specs=[vmem, vmem] + [anywhere] * (len(args) - 3),
            out_specs=[anywhere, vmem],
            scratch_shapes=[
                pltpu.VMEM((coarse, 2 * half, 2 * side, spectra * AVG), jnp.bfloat16),
                pltpu.VMEM((coarse, slots, 2, side, side), jnp.float32),
                pltpu.VMEM((2, side, side), jnp.float32),
                pltpu.SemaphoreType.DMA((coarse, slots)),
            ],
        ),
        out_shape=[
            jax.ShapeDtypeStruct((2, channels, slots, side, side), jnp.float32),
            jax.ShapeDtypeStruct((8, LANES), jnp.float32),
        ],
        input_output_aliases=aliases,
        cost_estimate=pl.CostEstimate(flops=0, bytes_accessed=0, transcendentals=0),
        compiler_params=pltpu.CompilerParams(vmem_limit_bytes=VMEM_BYTES),
        name="correlate_tiles",
    )(*args)


def places(count):
    return lax.axis_index("ft").astype(jnp.int32) ^ np.arange(count, dtype=np.int32)


def spread(pieces):
    count = len(pieces)
    return [pieces[0]] + [
        lax.ppermute(pieces[r], "ft", [(i, i ^ r) for i in range(count)])
        for r in range(1, count)
    ]


def exchange(own, bit):
    count = lax.axis_size("bl")
    return lax.ppermute(own, "bl", [(i, i ^ bit) for i in range(count)])


def gather_blocks(held, after):
    bit = lax.axis_size("bl") // 4
    other = exchange(held, bit)
    while bit > 1:
        bit //= 2
        held = pair(held, other, after).reshape(-1, *held.shape[1:])
        other = exchange(held, bit)
    return held, other


def block_order(count):
    order, bit = [0], count // 2
    while bit:
        order += [r ^ bit for r in order]
        bit //= 2
    return order


def tile_tables(block_ids, tile_owner):
    block_count = lax.axis_size("bl")
    tile_count = block_count * (block_count + 1) // 2
    slot_cap = 2 * tile_count // block_count
    pairs = [(i, j) for i in range(block_count) for j in range(i, block_count)]
    row_table = np.array([i for i, _ in pairs], np.int32)
    col_table = np.array([j for _, j in pairs], np.int32)
    mine = (tile_owner == lax.axis_index("bl")).astype(jnp.int32)
    earlier = np.tril(np.ones((tile_count, tile_count), np.int32), -1)
    rank = jnp.sum(earlier * mine[None, :], axis=1)
    labels = np.arange(block_count, dtype=np.int32)
    shard_of = jnp.sum(jnp.where(block_ids[None, :] == labels[:, None], labels[None, :], 0), axis=1)
    row_shard = jnp.sum(
        jnp.where(row_table[:, None] == labels[None, :], shard_of[None, :], 0), axis=1
    )
    col_shard = jnp.sum(
        jnp.where(col_table[:, None] == labels[None, :], shard_of[None, :], 0), axis=1
    )
    here = (mine[None, :] == 1) & (rank[None, :] == np.arange(slot_cap, dtype=np.int32)[:, None])
    rows = jnp.sum(jnp.where(here, row_shard[None, :], 0), axis=1)
    cols = jnp.sum(jnp.where(here, col_shard[None, :], 0), axis=1)
    index = lax.axis_index("bl")
    table = jnp.concatenate(
        [rows ^ index, cols ^ index, jnp.sum(mine, keepdims=True)]
    ).astype(jnp.int32)
    return table, slot_cap


def takes_kernels(mesh, voltages, coefs):
    dests = mesh.shape["ft"]
    blocks = mesh.shape["bl"]
    inputs = voltages.shape[2] // mesh.shape["bl"]
    per_dev = voltages.shape[1] // (mesh.shape["grp"] * dests)
    chan_count = coefs.shape[1]
    radix = chan_count // MXU
    return (
        per_dev == chan_count
        and chan_count % MXU == 0
        and radix & (radix - 1) == 0
        and radix % dests == 0
        and dests & (dests - 1) == 0
        and radix <= 8
        and blocks & (blocks - 1) == 0
        and blocks > 2
        and inputs % LANES == 0
        and LANES % dests == 0
        and (LANES // dests) % ROWS16 == 0
        and (dests * AVG) % LANES == 0
    )


def per_device_kernels(voltages, coefs, block_ids, tile_owner):
    dests = lax.axis_size("ft")
    taps, chan_count = coefs.shape
    radix = chan_count // MXU
    chunks = voltages.shape[2] // LANES
    coef_table = coefs.reshape(taps, MXU, radix).transpose(0, 2, 1)
    place = places(dests)
    table, slot_cap = tile_tables(block_ids, tile_owner)
    matrix, twiddle = matrix_tables(MXU), twiddle_tables(radix, MXU)
    cuts = MXU // LANES
    tables = []
    for cut in range(cuts):
        at = slice(cut * LANES, (cut + 1) * LANES)
        tables.append(np.ascontiguousarray(twiddle[:, :, at]))
        tables.append(np.concatenate([matrix[:, :MXU][:, at], matrix[:, MXU:][:, at]], axis=1))
    coef_table, *tables = stage(coef_table, *tables)
    arrived = spread(pack(voltages, place, dests, radix))
    _, rows, samples = arrived[0].shape
    sizes = (dests, dests, rows, samples, radix)
    made, split = transform_cut(arrived, place, coef_table, tables, 0, sizes, table)
    firsts = [table]
    for cut in range(1, cuts):
        more, _ = transform_cut(split, place, None, tables, cut, sizes, table)
        made = made + more
        firsts.append(more[0][0])
    half = lax.axis_size("bl") // 2
    units = len(made)
    own, other, arrived, tokens, vis = None, None, None, [], None
    for unit in range(units + 1):
        held = None
        if unit < units:
            parts = made[unit]
            if unit > 1:
                parts, _ = lax.optimization_barrier((parts, arrived))
            arrived = spread(parts)
            after = tokens[-1] if tokens else table
            if unit > 0:
                own, held = join(arrived, place, (own, other), after)
            else:
                (own,) = join(arrived, place, (), firsts[-1])
            other = exchange(own, half)
        else:
            held = pair(own, other, tokens[-1])
        if unit > 0:
            gathered = gather_blocks(held, table)
            cut, part = divmod(unit - 1, radix // dests)
            first = (part * MXU + cut * LANES) // AVG
            vis, token = correlate(
                table, gathered, first, units * LANES // AVG, chunks, slot_cap, vis
            )
            tokens.append(token)
    return vis


def tile_product(row_part, col_part, norm_scale):
    products = jnp.einsum(
        "pscax,qscay->cpqxy", row_part, col_part, preferred_element_type=jnp.float32
    )
    real_part = products[:, 0, 0] + products[:, 1, 1]
    imag_part = products[:, 1, 0] - products[:, 0, 1]
    return jnp.stack([real_part, imag_part]) * norm_scale


def dft_tables(order_len):
    steps_one = jnp.arange(order_len, dtype=jnp.int32)
    phase_grid = steps_one[:, None] * steps_one[None, :] % order_len
    angles = phase_grid.astype(jnp.float32) * (2.0 * math.pi / order_len)
    return (jnp.cos(angles), jnp.sin(angles))


def transform(filtered):
    per_dev = filtered.shape[1]
    chan_count = filtered.shape[2]
    rows_here = filtered.shape[3]
    outer_len = math.isqrt(chan_count)
    while chan_count % outer_len != 0:
        outer_len = outer_len - 1
    inner_len = chan_count // outer_len
    highest = lax.Precision.HIGHEST
    reshaped = filtered.reshape(2, per_dev, outer_len, inner_len, rows_here)
    real_in = reshaped[0]
    imag_in = reshaped[1]
    cos_outer, sin_outer = dft_tables(outer_len)
    section_re = jnp.einsum("snkb,nm->smkb", real_in, cos_outer, precision=highest) + jnp.einsum(
        "snkb,nm->smkb", imag_in, sin_outer, precision=highest
    )
    section_im = jnp.einsum("snkb,nm->smkb", imag_in, cos_outer, precision=highest) - jnp.einsum(
        "snkb,nm->smkb", real_in, sin_outer, precision=highest
    )
    twiddle_grid = (
        jnp.arange(outer_len, dtype=jnp.int32)[:, None]
        * jnp.arange(inner_len, dtype=jnp.int32)[None, :]
        % chan_count
    )
    twiddle_angles = twiddle_grid.astype(jnp.float32) * (2.0 * math.pi / chan_count)
    cos_twiddle = jnp.cos(twiddle_angles)[None, :, :, None]
    sin_twiddle = jnp.sin(twiddle_angles)[None, :, :, None]
    rot_re = section_re * cos_twiddle + section_im * sin_twiddle
    rot_im = section_im * cos_twiddle - section_re * sin_twiddle
    cos_inner, sin_inner = dft_tables(inner_len)
    final_re = jnp.einsum("smkb,kq->sqmb", rot_re, cos_inner, precision=highest) + jnp.einsum(
        "smkb,kq->sqmb", rot_im, sin_inner, precision=highest
    )
    final_im = jnp.einsum("smkb,kq->sqmb", rot_im, cos_inner, precision=highest) - jnp.einsum(
        "smkb,kq->sqmb", rot_re, sin_inner, precision=highest
    )
    stacked = jnp.stack([final_re, final_im]).reshape(2, per_dev, chan_count, rows_here)
    return (stacked * (1.0 / math.sqrt(chan_count))).astype(jnp.bfloat16)


def apply_taps(window, coef_part, taps_count, out_len):
    filtered = jnp.zeros((2, out_len, window.shape[2], window.shape[3]), jnp.float32)
    for tap_index in range(taps_count):
        filtered = filtered + coef_part[tap_index][None, None, :, None] * window[
            :, tap_index : tap_index + out_len
        ].astype(jnp.float32)
    return filtered


def per_device(voltages, coefs, block_ids, tile_owner):
    taps_count = coefs.shape[0]
    chan_count = coefs.shape[1]
    rows_here = voltages.shape[2]
    per_dev = voltages.shape[1] // chan_count
    volt_blocks = voltages.reshape(2, per_dev, chan_count, rows_here)
    phase_block = lax.all_to_all(volt_blocks, "ft", split_axis=2, concat_axis=1, tiled=True)
    spectra_count = phase_block.shape[1]
    phase_here = phase_block.shape[2]
    coef_part = lax.dynamic_slice_in_dim(coefs, lax.axis_index("ft") * phase_here, phase_here, 1)
    zero_front = jnp.zeros((2, taps_count - 1, phase_here, rows_here), phase_block.dtype)
    long_window = jnp.concatenate([zero_front, phase_block], axis=1)
    phase_filtered = apply_taps(long_window, coef_part, taps_count, spectra_count)
    filtered = lax.all_to_all(phase_filtered, "ft", split_axis=1, concat_axis=2, tiled=True)
    spectra = transform(filtered)
    turned = lax.all_to_all(spectra, "ft", split_axis=2, concat_axis=1, tiled=True)
    spectra_all = turned.shape[1]
    chan_here = turned.shape[2]
    coarse_here = chan_here // AVG
    coarse_view = turned.reshape(2, spectra_all, coarse_here, AVG, rows_here)
    norm_scale = 1.0 / (AVG * spectra_all)
    block_count = lax.axis_size("bl")
    my_index = lax.axis_index("bl")
    tile_count = block_count * (block_count + 1) // 2
    slot_cap = 2 * tile_count // block_count
    row_table = jnp.asarray(
        np.array(
            [
                first_id
                for first_id in range(block_count)
                for second_id in range(first_id, block_count)
            ],
            dtype=np.int32,
        )
    )
    col_table = jnp.asarray(
        np.array(
            [
                second_id
                for first_id in range(block_count)
                for second_id in range(first_id, block_count)
            ],
            dtype=np.int32,
        )
    )
    tile_pos = jnp.arange(tile_count, dtype=jnp.int32)
    same_owner = tile_owner[None, :] == tile_owner[:, None]
    before_mask = tile_pos[None, :] < tile_pos[:, None]
    slot_rank = jnp.sum((same_owner & before_mask).astype(jnp.int32), axis=1)
    labels = jnp.arange(block_count, dtype=jnp.int32)
    shard_of = jnp.sum(jnp.where(block_ids[None, :] == labels[:, None], labels[None, :], 0), axis=1)
    gathered = lax.all_gather(coarse_view[None], "bl", axis=0, tiled=True)
    mine_mask = tile_owner == my_index
    own_count = jnp.sum(mine_mask.astype(jnp.int32))
    slot_steps = jnp.arange(slot_cap, dtype=jnp.int32)
    slot_tile = jnp.sum(
        jnp.where(
            mine_mask[None, :] & (slot_rank[None, :] == slot_steps[:, None]), tile_pos[None, :], 0
        ),
        axis=1,
    )

    def one_tile(slot_pos, result_tiles):
        tile_id = slot_tile[slot_pos]
        row_block = gathered[shard_of[row_table[tile_id]]]
        col_block = gathered[shard_of[col_table[tile_id]]]
        tile = tile_product(row_block, col_block, norm_scale)
        return lax.dynamic_update_slice(result_tiles, tile[:, :, None], (0, 0, slot_pos, 0, 0))

    empty_tiles = jnp.zeros((2, coarse_here, slot_cap, rows_here, rows_here), jnp.float32)
    return lax.fori_loop(0, own_count, one_tile, empty_tiles)


def solution(mesh):
    def correlator(voltages, coefs, block_ids, tile_owner):
        fits = takes_kernels(mesh, voltages, coefs)
        return jax.shard_map(
            per_device_kernels if fits else per_device,
            mesh=mesh,
            in_specs=(P(None, ("grp", "ft"), "bl"), P(), P(), P("grp")),
            out_specs=P(None, ("grp", "ft"), "bl", None, None),
            check_vma=False,
        )(voltages, coefs, block_ids, tile_owner)

    return correlator
```

```python
import functools
import math

import jax
import jax.numpy as jnp
import ml_dtypes
import numpy as np
from jax import lax
from jax.experimental import pallas as pl
from jax.experimental.pallas import tpu as pltpu
from jax.sharding import PartitionSpec as P

AVG = 64
MXU = 256
LANES = 128
ROWS16 = 16
VMEM_BYTES = 48 * 1024 * 1024


def split_bf16(table):
    high = table.astype(ml_dtypes.bfloat16)
    low = (table - high.astype(np.float64)).astype(ml_dtypes.bfloat16)
    return high, low


def matrix_tables(inner_len):
    steps = np.arange(inner_len)
    angles = 2.0 * np.pi * (np.outer(steps, steps) % inner_len) / inner_len
    cos_part, sin_part = np.cos(angles), np.sin(angles)
    high, low = split_bf16(np.block([[cos_part, -sin_part], [sin_part, cos_part]]))
    return np.concatenate([high, high, low])


def twiddle_tables(radix, inner_len):
    chan_count = radix * inner_len
    angles = 2.0 * np.pi * np.outer(np.arange(radix), np.arange(inner_len)) / chan_count
    scale = 1.0 / math.sqrt(chan_count)
    return np.stack([np.cos(angles) * scale, np.sin(angles) * scale]).astype(np.float32)


def rotate(real, imag, step, count):
    step = step % count
    if step == 0:
        return real, imag
    if 4 * step == count:
        return imag, -real
    if 2 * step == count:
        return -real, -imag
    if 4 * step == 3 * count:
        return -imag, real
    cos_step = math.cos(2.0 * math.pi * step / count)
    sin_step = math.sin(2.0 * math.pi * step / count)
    if 8 * step == count:
        return cos_step * (real + imag), cos_step * (imag - real)
    return cos_step * real + sin_step * imag, cos_step * imag - sin_step * real


def butterflies(parts):
    count = len(parts)
    if count == 1:
        return parts
    half = count // 2
    sums, diffs = [], []
    for k in range(half):
        (ar, ai), (br, bi) = parts[k], parts[k + half]
        sums.append((ar + br, ai + bi))
        diffs.append(rotate(ar - br, ai - bi, k, count))
    even, odd = butterflies(sums), butterflies(diffs)
    out = []
    for k in range(half):
        out += [even[k], odd[k]]
    return out


def pack_kernel(radix, place_ref, v_ref, *rest):
    o_refs, (wide, turned) = rest[:-2], rest[-2:]
    dests, rows, samples = turned.shape
    inner = samples // radix
    for part in range(2):
        for chunk in range(v_ref.shape[2] // LANES):
            wide[...] = v_ref[part, :, chunk * LANES : (chunk + 1) * LANES].astype(jnp.float32)
            for phase in range(radix):
                here = wide[pl.ds(phase, inner, stride=radix), :].T.astype(jnp.bfloat16)
                for dest in range(dests):
                    turned[dest, :, phase * inner : (phase + 1) * inner] = here[
                        dest * rows : (dest + 1) * rows
                    ]
            for shift in range(dests):
                o_refs[shift][part, chunk * rows : (chunk + 1) * rows] = turned[place_ref[shift]]


def pack(voltages, place, dests, radix):
    _, samples, inputs = voltages.shape
    chunks = inputs // LANES
    rows = LANES // dests
    vmem = pl.BlockSpec(memory_space=pltpu.VMEM)
    return pl.pallas_call(
        functools.partial(pack_kernel, radix),
        grid_spec=pltpu.PrefetchScalarGridSpec(
            num_scalar_prefetch=1,
            grid=(),
            in_specs=[vmem],
            out_specs=[vmem] * dests,
            scratch_shapes=[
                pltpu.VMEM((samples, LANES), jnp.float32),
                pltpu.VMEM((dests, rows, samples), jnp.bfloat16),
            ],
        ),
        out_shape=[jax.ShapeDtypeStruct((2, chunks * rows, samples), jnp.bfloat16)] * dests,
        compiler_params=pltpu.CompilerParams(vmem_limit_bytes=VMEM_BYTES // 2),
        name="pack_inputs",
    )(place, voltages)


def stage_kernel(*refs):
    half = len(refs) // 2
    for source, target in zip(refs[:half], refs[half:]):
        target[...] = source[...]


def stage(*tables):
    vmem = pl.BlockSpec(memory_space=pltpu.VMEM)
    return pl.pallas_call(
        stage_kernel,
        in_specs=[vmem] * len(tables),
        out_specs=[vmem] * len(tables),
        out_shape=[jax.ShapeDtypeStruct(table.shape, table.dtype) for table in tables],
        compiler_params=pltpu.CompilerParams(vmem_limit_bytes=VMEM_BYTES // 4),
        name="stage_tables",
    )(*tables)


def filter_blocks(place_ref, v_refs, c_ref, held, split):
    spectra, _, rows, samples = held.shape
    taps, radix, inner = c_ref.shape
    for shift in range(len(v_refs)):
        held[place_ref[len(v_refs) + shift]] = v_refs[shift][...]

    @pl.loop(0, radix)
    def _(phase):
        lane0 = pl.multiple_of(phase * inner, inner)
        row0 = pl.multiple_of(phase * spectra * rows, spectra * rows)
        for part in range(2):
            for sub in range(0, rows, ROWS16):
                blocks = [
                    held[b, part, pl.ds(sub, ROWS16), pl.ds(lane0, inner)].astype(jnp.float32)
                    for b in range(spectra)
                ]
                for s in range(spectra):
                    total = None
                    for b in range(max(0, s - taps + 1), s + 1):
                        term = c_ref[taps - 1 - s + b, pl.ds(phase, 1), :] * blocks[b]
                        total = term if total is None else total + term
                    high = total.astype(jnp.bfloat16)
                    low = (total - high.astype(jnp.float32)).astype(jnp.bfloat16)
                    at = pl.ds(pl.multiple_of(row0 + s * rows + sub, ROWS16), ROWS16)
                    split[at, part * inner : (part + 1) * inner] = high
                    split[at, (2 + part) * inner : (3 + part) * inner] = low


def transform_lanes(place_ref, split, tw_ref, g_ref, prod, made, out_refs):
    dests, halves, _, spectra, rows, _ = made.shape
    radix = tw_ref.shape[1]
    group = spectra * rows
    depth = split.shape[1] // 2

    @pl.loop(0, radix // 2)
    def _(pair):
        at = pl.ds(pl.multiple_of(pair * 2 * group, 2 * group), 2 * group)
        high = split[at, :depth]
        line = jnp.concatenate([high, split[at, depth:], high], axis=1)
        prod[at, :] = jnp.dot(line, g_ref[...], preferred_element_type=jnp.float32)

    @pl.loop(0, spectra)
    def _(s):
        for sub in range(0, rows, ROWS16):
            parts = []
            for phase in range(radix):
                at = pl.ds(pl.multiple_of(phase * group + s * rows + sub, ROWS16), ROWS16)
                yr, yi = prod[at, :LANES], prod[at, LANES:]
                cos_here = tw_ref[0, phase : phase + 1, :]
                sin_here = tw_ref[1, phase : phase + 1, :]
                if phase == 0:
                    parts.append((yr * cos_here, yi * cos_here))
                else:
                    parts.append((yr * cos_here + yi * sin_here, yi * cos_here - yr * sin_here))
            for step, pair in enumerate(butterflies(parts)):
                for part in range(2):
                    made[step // halves, step % halves, part, s, sub : sub + ROWS16, :] = pair[
                        part
                    ].astype(jnp.bfloat16)

    for shift in range(dests):
        for half in range(halves):
            out_refs[half * dests + shift][...] = made[place_ref[shift], half]


def transform_cut(source, place, coef_table, tables, cut, sizes, after):
    dests, spectra, rows, samples, radix = sizes
    inner = samples // radix
    halves = radix // dests
    total = radix * spectra * rows
    begins = coef_table is not None
    vmem = pl.BlockSpec(memory_space=pltpu.VMEM)

    def kernel(place_ref, *rest):
        if begins:
            v_refs, (c_ref, tw_ref, g_ref) = rest[:dests], rest[dests : dests + 3]
            out_refs, (split, held, prod, made) = rest[dests + 4 : -4], rest[-4:]
            filter_blocks(place_ref, v_refs, c_ref, held, split)
        else:
            split, tw_ref, g_ref = rest[:3]
            out_refs, (prod, made) = rest[4:-2], rest[-2:]
        transform_lanes(place_ref, split, tw_ref, g_ref, prod, made, out_refs)

    scratch = [
        pltpu.VMEM((total, 2 * LANES), jnp.float32),
        pltpu.VMEM((dests, halves, 2, spectra, rows, LANES), jnp.bfloat16),
    ]
    shapes = [jax.ShapeDtypeStruct((2, spectra, rows, LANES), jnp.bfloat16)] * (halves * dests)
    if begins:
        scratch = [pltpu.VMEM((spectra, 2, rows, samples), jnp.bfloat16)] + scratch
        shapes = shapes + [jax.ShapeDtypeStruct((total, 4 * inner), jnp.bfloat16)]
    args = [*source, coef_table] if begins else [source]
    args += [tables[2 * cut], tables[2 * cut + 1]]
    made = pl.pallas_call(
        kernel,
        grid_spec=pltpu.PrefetchScalarGridSpec(
            num_scalar_prefetch=1,
            grid=(),
            in_specs=[vmem] * len(args) + [pl.BlockSpec(memory_space=pl.ANY)],
            out_specs=[vmem] * len(shapes),
            scratch_shapes=scratch,
        ),
        out_shape=shapes,
        cost_estimate=pl.CostEstimate(
            flops=3 * 2 * total * 4 * inner * LANES, bytes_accessed=6 << 20, transcendentals=0
        ),
        compiler_params=pltpu.CompilerParams(vmem_limit_bytes=VMEM_BYTES // 2),
        name="filter_transform" if begins else "transform_rest",
    )(place, *args, after)
    units = [made[half * dests : (half + 1) * dests] for half in range(halves)]
    return units, made[-1]


def join(pieces, place, before, after):
    count = len(pieces)
    vmem = pl.BlockSpec(memory_space=pltpu.VMEM)
    shapes = [jax.ShapeDtypeStruct((count, *pieces[0].shape), pieces[0].dtype)]
    if before:
        shapes.append(jax.ShapeDtypeStruct((2, *before[0].shape), before[0].dtype))

    def kernel(place_ref, *rest):
        ins, outs = rest[: count + len(before)], rest[count + len(before) + 1 :]
        for shift in range(count):
            outs[0][place_ref[count + shift]] = ins[shift][...]
        for at in range(len(before)):
            outs[1][at] = ins[count + at][...]

    return pl.pallas_call(
        kernel,
        grid_spec=pltpu.PrefetchScalarGridSpec(
            num_scalar_prefetch=1,
            grid=(),
            in_specs=[vmem] * (count + len(before)) + [pl.BlockSpec(memory_space=pl.ANY)],
            out_specs=[vmem] * len(shapes),
        ),
        out_shape=shapes,
        compiler_params=pltpu.CompilerParams(vmem_limit_bytes=VMEM_BYTES // 4),
        name="join_pieces",
    )(place, *pieces, *before, after)


def pair(own, other, after):
    def kernel(own_ref, other_ref, _, out_ref):
        out_ref[0] = own_ref[...]
        out_ref[1] = other_ref[...]

    vmem = pl.BlockSpec(memory_space=pltpu.VMEM)
    return pl.pallas_call(
        kernel,
        in_specs=[vmem, vmem, pl.BlockSpec(memory_space=pl.ANY)],
        out_specs=vmem,
        out_shape=jax.ShapeDtypeStruct((2, *own.shape), own.dtype),
        compiler_params=pltpu.CompilerParams(vmem_limit_bytes=VMEM_BYTES // 4),
        name="pair_blocks",
    )(own, other, after)


def correlate_kernel(chunks, scale, first, table_ref, low_ref, high_ref, *rest):
    o_ref, token_ref, left, tiles, empty, sems = rest[-6:]
    half, senders, _, spectra, rows, lanes = low_ref.shape
    order = block_order(2 * half)
    slots = o_ref.shape[2]
    coarse = lanes // AVG
    side = senders * rows
    run = rows // chunks
    count = table_ref[2 * slots]
    token_ref[...] = jnp.zeros_like(token_ref)
    empty[...] = jnp.zeros_like(empty)

    def copy_out(source, c, slot):
        return pltpu.make_async_copy(source, o_ref.at[:, first + c, slot], sems.at[c, slot])

    for slot in range(slots):

        @pl.when(slot >= count)
        def _(slot=slot):
            for c in range(coarse):
                copy_out(empty, c, slot).start()

    for at, block in enumerate(order):
        source = (low_ref, high_ref)[at // half].at[at % half]
        for sender in range(senders):
            for part in range(2):
                for chunk in range(chunks):
                    row = part * side + (chunk * senders + sender) * run
                    pieces = [
                        source[sender, part, s, chunk * run : (chunk + 1) * run]
                        for s in range(spectra)
                    ]
                    for c in range(coarse):
                        left[c, block, row : row + run, :] = jnp.concatenate(
                            [piece[:, c * AVG : (c + 1) * AVG] for piece in pieces], axis=1
                        )

    for slot in range(slots):

        @pl.when(slot < count)
        def _(slot=slot):
            for c in range(coarse):
                rows_of = left[c, table_ref[slot]]
                with_real, with_imag = [
                    lax.dot_general(
                        rows_of,
                        left[c, table_ref[slots + slot], pl.ds(part * side, side), :],
                        (((1,), (1,)), ((), ())),
                        preferred_element_type=jnp.float32,
                    )
                    for part in range(2)
                ]
                tiles[c, slot, 0] = (with_real[:side] + with_imag[side:]) * scale
                tiles[c, slot, 1] = (with_real[side:] - with_imag[:side]) * scale
                copy_out(tiles.at[c, slot], c, slot).start()

    for slot in range(slots):
        for c in range(coarse):
            copy_out(empty, c, slot).wait()


def correlate(table, gathered, first, channels, chunks, slots, vis):
    half, senders, _, spectra, rows, lanes = gathered[0].shape
    coarse = lanes // AVG
    side = senders * rows
    vmem = pl.BlockSpec(memory_space=pltpu.VMEM)
    anywhere = pl.BlockSpec(memory_space=pl.ANY)
    args = [table, *gathered]
    aliases = {}
    if vis is not None:
        args.append(vis)
        aliases = {len(args) - 1: 0}
    return pl.pallas_call(
        functools.partial(correlate_kernel, chunks, 1.0 / (AVG * spectra), first),
        grid_spec=pltpu.PrefetchScalarGridSpec(
            num_scalar_prefetch=1,
            grid=(),
            in_specs=[vmem, vmem] + [anywhere] * (len(args) - 3),
            out_specs=[anywhere, vmem],
            scratch_shapes=[
                pltpu.VMEM((coarse, 2 * half, 2 * side, spectra * AVG), jnp.bfloat16),
                pltpu.VMEM((coarse, slots, 2, side, side), jnp.float32),
                pltpu.VMEM((2, side, side), jnp.float32),
                pltpu.SemaphoreType.DMA((coarse, slots)),
            ],
        ),
        out_shape=[
            jax.ShapeDtypeStruct((2, channels, slots, side, side), jnp.float32),
            jax.ShapeDtypeStruct((8, LANES), jnp.float32),
        ],
        input_output_aliases=aliases,
        cost_estimate=pl.CostEstimate(flops=0, bytes_accessed=0, transcendentals=0),
        compiler_params=pltpu.CompilerParams(vmem_limit_bytes=VMEM_BYTES),
        name="correlate_tiles",
    )(*args)


def places(count):
    steps = np.arange(count, dtype=np.int32)
    index = lax.axis_index("ft").astype(jnp.int32)
    return jnp.concatenate([(index + steps) % count, (index + count - steps) % count])


def spread(pieces):
    count = len(pieces)
    arrived = [pieces[0]] + [None] * (count - 1)
    for d in sorted(range(1, count), key=lambda d: abs(d - count // 2)):
        arrived[d] = lax.ppermute(pieces[d], "ft", [(i, (i + d) % count) for i in range(count)])
    return arrived


def exchange(own, bit):
    count = lax.axis_size("bl")
    return lax.ppermute(own, "bl", [(i, i ^ bit) for i in range(count)])


def gather_blocks(held, after):
    bit = lax.axis_size("bl") // 4
    other = exchange(held, bit)
    while bit > 1:
        bit //= 2
        held = pair(held, other, after).reshape(-1, *held.shape[1:])
        other = exchange(held, bit)
    return held, other


def block_order(count):
    order, bit = [0], count // 2
    while bit:
        order += [r ^ bit for r in order]
        bit //= 2
    return order


def tile_tables(block_ids, tile_owner):
    block_count = lax.axis_size("bl")
    tile_count = block_count * (block_count + 1) // 2
    slot_cap = 2 * tile_count // block_count
    pairs = [(i, j) for i in range(block_count) for j in range(i, block_count)]
    row_table = np.array([i for i, _ in pairs], np.int32)
    col_table = np.array([j for _, j in pairs], np.int32)
    mine = (tile_owner == lax.axis_index("bl")).astype(jnp.int32)
    earlier = np.tril(np.ones((tile_count, tile_count), np.int32), -1)
    rank = jnp.sum(earlier * mine[None, :], axis=1)
    labels = np.arange(block_count, dtype=np.int32)
    shard_of = jnp.sum(jnp.where(block_ids[None, :] == labels[:, None], labels[None, :], 0), axis=1)
    row_shard = jnp.sum(
        jnp.where(row_table[:, None] == labels[None, :], shard_of[None, :], 0), axis=1
    )
    col_shard = jnp.sum(
        jnp.where(col_table[:, None] == labels[None, :], shard_of[None, :], 0), axis=1
    )
    here = (mine[None, :] == 1) & (rank[None, :] == np.arange(slot_cap, dtype=np.int32)[:, None])
    rows = jnp.sum(jnp.where(here, row_shard[None, :], 0), axis=1)
    cols = jnp.sum(jnp.where(here, col_shard[None, :], 0), axis=1)
    index = lax.axis_index("bl")
    table = jnp.concatenate(
        [rows ^ index, cols ^ index, jnp.sum(mine, keepdims=True)]
    ).astype(jnp.int32)
    return table, slot_cap


def takes_kernels(mesh, voltages, coefs):
    dests = mesh.shape["ft"]
    blocks = mesh.shape["bl"]
    inputs = voltages.shape[2] // mesh.shape["bl"]
    per_dev = voltages.shape[1] // (mesh.shape["grp"] * dests)
    chan_count = coefs.shape[1]
    radix = chan_count // MXU
    return (
        per_dev == chan_count
        and chan_count % MXU == 0
        and radix & (radix - 1) == 0
        and radix % dests == 0
        and radix <= 8
        and blocks & (blocks - 1) == 0
        and blocks > 2
        and inputs % LANES == 0
        and LANES % dests == 0
        and (LANES // dests) % ROWS16 == 0
        and (dests * AVG) % LANES == 0
    )


def per_device_kernels(voltages, coefs, block_ids, tile_owner):
    dests = lax.axis_size("ft")
    taps, chan_count = coefs.shape
    radix = chan_count // MXU
    chunks = voltages.shape[2] // LANES
    coef_table = coefs.reshape(taps, MXU, radix).transpose(0, 2, 1)
    place = places(dests)
    table, slot_cap = tile_tables(block_ids, tile_owner)
    matrix, twiddle = matrix_tables(MXU), twiddle_tables(radix, MXU)
    cuts = MXU // LANES
    tables = []
    for cut in range(cuts):
        at = slice(cut * LANES, (cut + 1) * LANES)
        tables.append(np.ascontiguousarray(twiddle[:, :, at]))
        tables.append(np.concatenate([matrix[:, :MXU][:, at], matrix[:, MXU:][:, at]], axis=1))
    coef_table, *tables = stage(coef_table, *tables)
    arrived = spread(pack(voltages, place, dests, radix))
    _, rows, samples = arrived[0].shape
    sizes = (dests, dests, rows, samples, radix)
    made, split = transform_cut(arrived, place, coef_table, tables, 0, sizes, table)
    firsts = [table]
    for cut in range(1, cuts):
        more, _ = transform_cut(split, place, None, tables, cut, sizes, table)
        made = made + more
        firsts.append(more[0][0])
    half = lax.axis_size("bl") // 2
    units = len(made)
    own, other, arrived, tokens, vis = None, None, None, [], None
    for unit in range(units + 1):
        held = None
        if unit < units:
            parts = made[unit]
            if unit > 1:
                parts, _ = lax.optimization_barrier((parts, arrived))
            arrived = spread(parts)
            after = tokens[-1] if tokens else table
            if unit > 0:
                own, held = join(arrived, place, (own, other), after)
            else:
                (own,) = join(arrived, place, (), firsts[-1])
            other = exchange(own, half)
        else:
            held = pair(own, other, tokens[-1])
        if unit > 0:
            gathered = gather_blocks(held, table)
            cut, part = divmod(unit - 1, radix // dests)
            first = (part * MXU + cut * LANES) // AVG
            vis, token = correlate(
                table, gathered, first, units * LANES // AVG, chunks, slot_cap, vis
            )
            tokens.append(token)
    return vis


def tile_product(row_part, col_part, norm_scale):
    products = jnp.einsum(
        "pscax,qscay->cpqxy", row_part, col_part, preferred_element_type=jnp.float32
    )
    real_part = products[:, 0, 0] + products[:, 1, 1]
    imag_part = products[:, 1, 0] - products[:, 0, 1]
    return jnp.stack([real_part, imag_part]) * norm_scale


def dft_tables(order_len):
    steps_one = jnp.arange(order_len, dtype=jnp.int32)
    phase_grid = steps_one[:, None] * steps_one[None, :] % order_len
    angles = phase_grid.astype(jnp.float32) * (2.0 * math.pi / order_len)
    return (jnp.cos(angles), jnp.sin(angles))


def transform(filtered):
    per_dev = filtered.shape[1]
    chan_count = filtered.shape[2]
    rows_here = filtered.shape[3]
    outer_len = math.isqrt(chan_count)
    while chan_count % outer_len != 0:
        outer_len = outer_len - 1
    inner_len = chan_count // outer_len
    highest = lax.Precision.HIGHEST
    reshaped = filtered.reshape(2, per_dev, outer_len, inner_len, rows_here)
    real_in = reshaped[0]
    imag_in = reshaped[1]
    cos_outer, sin_outer = dft_tables(outer_len)
    section_re = jnp.einsum("snkb,nm->smkb", real_in, cos_outer, precision=highest) + jnp.einsum(
        "snkb,nm->smkb", imag_in, sin_outer, precision=highest
    )
    section_im = jnp.einsum("snkb,nm->smkb", imag_in, cos_outer, precision=highest) - jnp.einsum(
        "snkb,nm->smkb", real_in, sin_outer, precision=highest
    )
    twiddle_grid = (
        jnp.arange(outer_len, dtype=jnp.int32)[:, None]
        * jnp.arange(inner_len, dtype=jnp.int32)[None, :]
        % chan_count
    )
    twiddle_angles = twiddle_grid.astype(jnp.float32) * (2.0 * math.pi / chan_count)
    cos_twiddle = jnp.cos(twiddle_angles)[None, :, :, None]
    sin_twiddle = jnp.sin(twiddle_angles)[None, :, :, None]
    rot_re = section_re * cos_twiddle + section_im * sin_twiddle
    rot_im = section_im * cos_twiddle - section_re * sin_twiddle
    cos_inner, sin_inner = dft_tables(inner_len)
    final_re = jnp.einsum("smkb,kq->sqmb", rot_re, cos_inner, precision=highest) + jnp.einsum(
        "smkb,kq->sqmb", rot_im, sin_inner, precision=highest
    )
    final_im = jnp.einsum("smkb,kq->sqmb", rot_im, cos_inner, precision=highest) - jnp.einsum(
        "smkb,kq->sqmb", rot_re, sin_inner, precision=highest
    )
    stacked = jnp.stack([final_re, final_im]).reshape(2, per_dev, chan_count, rows_here)
    return (stacked * (1.0 / math.sqrt(chan_count))).astype(jnp.bfloat16)


def apply_taps(window, coef_part, taps_count, out_len):
    filtered = jnp.zeros((2, out_len, window.shape[2], window.shape[3]), jnp.float32)
    for tap_index in range(taps_count):
        filtered = filtered + coef_part[tap_index][None, None, :, None] * window[
            :, tap_index : tap_index + out_len
        ].astype(jnp.float32)
    return filtered


def per_device(voltages, coefs, block_ids, tile_owner):
    taps_count = coefs.shape[0]
    chan_count = coefs.shape[1]
    rows_here = voltages.shape[2]
    per_dev = voltages.shape[1] // chan_count
    volt_blocks = voltages.reshape(2, per_dev, chan_count, rows_here)
    phase_block = lax.all_to_all(volt_blocks, "ft", split_axis=2, concat_axis=1, tiled=True)
    spectra_count = phase_block.shape[1]
    phase_here = phase_block.shape[2]
    coef_part = lax.dynamic_slice_in_dim(coefs, lax.axis_index("ft") * phase_here, phase_here, 1)
    zero_front = jnp.zeros((2, taps_count - 1, phase_here, rows_here), phase_block.dtype)
    long_window = jnp.concatenate([zero_front, phase_block], axis=1)
    phase_filtered = apply_taps(long_window, coef_part, taps_count, spectra_count)
    filtered = lax.all_to_all(phase_filtered, "ft", split_axis=1, concat_axis=2, tiled=True)
    spectra = transform(filtered)
    turned = lax.all_to_all(spectra, "ft", split_axis=2, concat_axis=1, tiled=True)
    spectra_all = turned.shape[1]
    chan_here = turned.shape[2]
    coarse_here = chan_here // AVG
    coarse_view = turned.reshape(2, spectra_all, coarse_here, AVG, rows_here)
    norm_scale = 1.0 / (AVG * spectra_all)
    block_count = lax.axis_size("bl")
    my_index = lax.axis_index("bl")
    tile_count = block_count * (block_count + 1) // 2
    slot_cap = 2 * tile_count // block_count
    row_table = jnp.asarray(
        np.array(
            [
                first_id
                for first_id in range(block_count)
                for second_id in range(first_id, block_count)
            ],
            dtype=np.int32,
        )
    )
    col_table = jnp.asarray(
        np.array(
            [
                second_id
                for first_id in range(block_count)
                for second_id in range(first_id, block_count)
            ],
            dtype=np.int32,
        )
    )
    tile_pos = jnp.arange(tile_count, dtype=jnp.int32)
    same_owner = tile_owner[None, :] == tile_owner[:, None]
    before_mask = tile_pos[None, :] < tile_pos[:, None]
    slot_rank = jnp.sum((same_owner & before_mask).astype(jnp.int32), axis=1)
    labels = jnp.arange(block_count, dtype=jnp.int32)
    shard_of = jnp.sum(jnp.where(block_ids[None, :] == labels[:, None], labels[None, :], 0), axis=1)
    gathered = lax.all_gather(coarse_view[None], "bl", axis=0, tiled=True)
    mine_mask = tile_owner == my_index
    own_count = jnp.sum(mine_mask.astype(jnp.int32))
    slot_steps = jnp.arange(slot_cap, dtype=jnp.int32)
    slot_tile = jnp.sum(
        jnp.where(
            mine_mask[None, :] & (slot_rank[None, :] == slot_steps[:, None]), tile_pos[None, :], 0
        ),
        axis=1,
    )

    def one_tile(slot_pos, result_tiles):
        tile_id = slot_tile[slot_pos]
        row_block = gathered[shard_of[row_table[tile_id]]]
        col_block = gathered[shard_of[col_table[tile_id]]]
        tile = tile_product(row_block, col_block, norm_scale)
        return lax.dynamic_update_slice(result_tiles, tile[:, :, None], (0, 0, slot_pos, 0, 0))

    empty_tiles = jnp.zeros((2, coarse_here, slot_cap, rows_here, rows_here), jnp.float32)
    return lax.fori_loop(0, own_count, one_tile, empty_tiles)


def solution(mesh):
    def correlator(voltages, coefs, block_ids, tile_owner):
        fits = takes_kernels(mesh, voltages, coefs)
        return jax.shard_map(
            per_device_kernels if fits else per_device,
            mesh=mesh,
            in_specs=(P(None, ("grp", "ft"), "bl"), P(), P(), P("grp")),
            out_specs=P(None, ("grp", "ft"), "bl", None, None),
            check_vma=False,
        )(voltages, coefs, block_ids, tile_owner)

    return correlator
```

```python
import functools
import math

import jax
import jax.numpy as jnp
import ml_dtypes
import numpy as np
from jax import lax
from jax.experimental import pallas as pl
from jax.experimental.pallas import tpu as pltpu
from jax.sharding import PartitionSpec as P

AVG = 64
MXU = 256
LANES = 128
ROWS16 = 16
VMEM_BYTES = 48 * 1024 * 1024


def split_bf16(table):
    high = table.astype(ml_dtypes.bfloat16)
    low = (table - high.astype(np.float64)).astype(ml_dtypes.bfloat16)
    return high, low


def matrix_tables(inner_len):
    steps = np.arange(inner_len)
    angles = 2.0 * np.pi * (np.outer(steps, steps) % inner_len) / inner_len
    cos_part, sin_part = np.cos(angles), np.sin(angles)
    high, low = split_bf16(np.block([[cos_part, -sin_part], [sin_part, cos_part]]))
    return np.concatenate([high, high, low])


def twiddle_tables(radix, inner_len):
    chan_count = radix * inner_len
    angles = 2.0 * np.pi * np.outer(np.arange(radix), np.arange(inner_len)) / chan_count
    scale = 1.0 / math.sqrt(chan_count)
    return np.stack([np.cos(angles) * scale, np.sin(angles) * scale]).astype(np.float32)


def rotate(real, imag, step, count):
    step = step % count
    if step == 0:
        return real, imag
    if 4 * step == count:
        return imag, -real
    if 2 * step == count:
        return -real, -imag
    if 4 * step == 3 * count:
        return -imag, real
    cos_step = math.cos(2.0 * math.pi * step / count)
    sin_step = math.sin(2.0 * math.pi * step / count)
    if 8 * step == count:
        return cos_step * (real + imag), cos_step * (imag - real)
    return cos_step * real + sin_step * imag, cos_step * imag - sin_step * real


def butterflies(parts):
    count = len(parts)
    if count == 1:
        return parts
    half = count // 2
    sums, diffs = [], []
    for k in range(half):
        (ar, ai), (br, bi) = parts[k], parts[k + half]
        sums.append((ar + br, ai + bi))
        diffs.append(rotate(ar - br, ai - bi, k, count))
    even, odd = butterflies(sums), butterflies(diffs)
    out = []
    for k in range(half):
        out += [even[k], odd[k]]
    return out


def pack_kernel(radix, place_ref, v_ref, *rest):
    o_refs, (wide, turned) = rest[:-2], rest[-2:]
    dests, rows, samples = turned.shape
    inner = samples // radix
    for part in range(2):
        for chunk in range(v_ref.shape[2] // LANES):
            wide[...] = v_ref[part, :, chunk * LANES : (chunk + 1) * LANES].astype(jnp.float32)
            for phase in range(radix):
                here = wide[pl.ds(phase, inner, stride=radix), :].T.astype(jnp.bfloat16)
                for dest in range(dests):
                    turned[dest, :, phase * inner : (phase + 1) * inner] = here[
                        dest * rows : (dest + 1) * rows
                    ]
            for shift in range(dests):
                o_refs[shift][part, chunk * rows : (chunk + 1) * rows] = turned[place_ref[shift]]


def pack(voltages, place, dests, radix):
    _, samples, inputs = voltages.shape
    chunks = inputs // LANES
    rows = LANES // dests
    vmem = pl.BlockSpec(memory_space=pltpu.VMEM)
    return pl.pallas_call(
        functools.partial(pack_kernel, radix),
        grid_spec=pltpu.PrefetchScalarGridSpec(
            num_scalar_prefetch=1,
            grid=(),
            in_specs=[vmem],
            out_specs=[vmem] * dests,
            scratch_shapes=[
                pltpu.VMEM((samples, LANES), jnp.float32),
                pltpu.VMEM((dests, rows, samples), jnp.bfloat16),
            ],
        ),
        out_shape=[jax.ShapeDtypeStruct((2, chunks * rows, samples), jnp.bfloat16)] * dests,
        compiler_params=pltpu.CompilerParams(vmem_limit_bytes=VMEM_BYTES // 2),
        name="pack_inputs",
    )(place, voltages)


def stage_kernel(*refs):
    half = len(refs) // 2
    for source, target in zip(refs[:half], refs[half:]):
        target[...] = source[...]


def stage(*tables):
    vmem = pl.BlockSpec(memory_space=pltpu.VMEM)
    return pl.pallas_call(
        stage_kernel,
        in_specs=[vmem] * len(tables),
        out_specs=[vmem] * len(tables),
        out_shape=[jax.ShapeDtypeStruct(table.shape, table.dtype) for table in tables],
        compiler_params=pltpu.CompilerParams(vmem_limit_bytes=VMEM_BYTES // 4),
        name="stage_tables",
    )(*tables)


def filter_blocks(place_ref, v_refs, c_ref, held, split):
    spectra, _, rows, samples = held.shape
    taps, radix, inner = c_ref.shape
    for shift in range(len(v_refs)):
        held[place_ref[len(v_refs) + shift]] = v_refs[shift][...]

    @pl.loop(0, radix)
    def _(phase):
        lane0 = pl.multiple_of(phase * inner, inner)
        row0 = pl.multiple_of(phase * spectra * rows, spectra * rows)
        for part in range(2):
            for sub in range(0, rows, ROWS16):
                blocks = [
                    held[b, part, pl.ds(sub, ROWS16), pl.ds(lane0, inner)].astype(jnp.float32)
                    for b in range(spectra)
                ]
                for s in range(spectra):
                    total = None
                    for b in range(max(0, s - taps + 1), s + 1):
                        term = c_ref[taps - 1 - s + b, pl.ds(phase, 1), :] * blocks[b]
                        total = term if total is None else total + term
                    high = total.astype(jnp.bfloat16)
                    low = (total - high.astype(jnp.float32)).astype(jnp.bfloat16)
                    at = pl.ds(pl.multiple_of(row0 + s * rows + sub, ROWS16), ROWS16)
                    split[at, part * inner : (part + 1) * inner] = high
                    split[at, (2 + part) * inner : (3 + part) * inner] = low


def transform_lanes(place_ref, split, tw_ref, g_ref, prod, made, out_refs):
    dests, halves, _, spectra, rows, _ = made.shape
    radix = tw_ref.shape[1]
    group = spectra * rows
    depth = split.shape[1] // 2

    @pl.loop(0, radix // 2)
    def _(pair):
        at = pl.ds(pl.multiple_of(pair * 2 * group, 2 * group), 2 * group)
        high = split[at, :depth]
        line = jnp.concatenate([high, split[at, depth:], high], axis=1)
        prod[at, :] = jnp.dot(line, g_ref[...], preferred_element_type=jnp.float32)

    @pl.loop(0, spectra)
    def _(s):
        for sub in range(0, rows, ROWS16):
            parts = []
            for phase in range(radix):
                at = pl.ds(pl.multiple_of(phase * group + s * rows + sub, ROWS16), ROWS16)
                yr, yi = prod[at, :LANES], prod[at, LANES:]
                cos_here = tw_ref[0, phase : phase + 1, :]
                sin_here = tw_ref[1, phase : phase + 1, :]
                if phase == 0:
                    parts.append((yr * cos_here, yi * cos_here))
                else:
                    parts.append((yr * cos_here + yi * sin_here, yi * cos_here - yr * sin_here))
            for step, pair in enumerate(butterflies(parts)):
                for part in range(2):
                    made[step // halves, step % halves, part, s, sub : sub + ROWS16, :] = pair[
                        part
                    ].astype(jnp.bfloat16)

    for shift in range(dests):
        for half in range(halves):
            out_refs[half * dests + shift][...] = made[place_ref[shift], half]


def transform_cut(source, place, coef_table, tables, cut, sizes, after):
    dests, spectra, rows, samples, radix = sizes
    inner = samples // radix
    halves = radix // dests
    total = radix * spectra * rows
    begins = coef_table is not None
    vmem = pl.BlockSpec(memory_space=pltpu.VMEM)

    def kernel(place_ref, *rest):
        if begins:
            v_refs, (c_ref, tw_ref, g_ref) = rest[:dests], rest[dests : dests + 3]
            out_refs, (split, held, prod, made) = rest[dests + 4 : -4], rest[-4:]
            filter_blocks(place_ref, v_refs, c_ref, held, split)
        else:
            split, tw_ref, g_ref = rest[:3]
            out_refs, (prod, made) = rest[4:-2], rest[-2:]
        transform_lanes(place_ref, split, tw_ref, g_ref, prod, made, out_refs)

    scratch = [
        pltpu.VMEM((total, 2 * LANES), jnp.float32),
        pltpu.VMEM((dests, halves, 2, spectra, rows, LANES), jnp.bfloat16),
    ]
    shapes = [jax.ShapeDtypeStruct((2, spectra, rows, LANES), jnp.bfloat16)] * (halves * dests)
    if begins:
        scratch = [pltpu.VMEM((spectra, 2, rows, samples), jnp.bfloat16)] + scratch
        shapes = shapes + [jax.ShapeDtypeStruct((total, 4 * inner), jnp.bfloat16)]
    args = [*source, coef_table] if begins else [source]
    args += [tables[2 * cut], tables[2 * cut + 1]]
    made = pl.pallas_call(
        kernel,
        grid_spec=pltpu.PrefetchScalarGridSpec(
            num_scalar_prefetch=1,
            grid=(),
            in_specs=[vmem] * len(args) + [pl.BlockSpec(memory_space=pl.ANY)],
            out_specs=[vmem] * len(shapes),
            scratch_shapes=scratch,
        ),
        out_shape=shapes,
        cost_estimate=pl.CostEstimate(
            flops=3 * 2 * total * 4 * inner * LANES, bytes_accessed=6 << 20, transcendentals=0
        ),
        compiler_params=pltpu.CompilerParams(vmem_limit_bytes=VMEM_BYTES // 2),
        name="filter_transform" if begins else "transform_rest",
    )(place, *args, after)
    units = [made[half * dests : (half + 1) * dests] for half in range(halves)]
    return units, made[-1]


def join(pieces, place, before, after):
    count = len(pieces)
    vmem = pl.BlockSpec(memory_space=pltpu.VMEM)
    shapes = [jax.ShapeDtypeStruct((count, *pieces[0].shape), pieces[0].dtype)]
    if before:
        shapes.append(jax.ShapeDtypeStruct((2, *before[0].shape), before[0].dtype))

    def kernel(place_ref, *rest):
        ins, outs = rest[: count + len(before)], rest[count + len(before) + 1 :]
        for shift in range(count):
            outs[0][place_ref[count + shift]] = ins[shift][...]
        for at in range(len(before)):
            outs[1][at] = ins[count + at][...]

    return pl.pallas_call(
        kernel,
        grid_spec=pltpu.PrefetchScalarGridSpec(
            num_scalar_prefetch=1,
            grid=(),
            in_specs=[vmem] * (count + len(before)) + [pl.BlockSpec(memory_space=pl.ANY)],
            out_specs=[vmem] * len(shapes),
        ),
        out_shape=shapes,
        compiler_params=pltpu.CompilerParams(vmem_limit_bytes=VMEM_BYTES // 4),
        name="join_pieces",
    )(place, *pieces, *before, after)


def pair(own, other, after):
    def kernel(own_ref, other_ref, _, out_ref):
        out_ref[0] = own_ref[...]
        out_ref[1] = other_ref[...]

    vmem = pl.BlockSpec(memory_space=pltpu.VMEM)
    return pl.pallas_call(
        kernel,
        in_specs=[vmem, vmem, pl.BlockSpec(memory_space=pl.ANY)],
        out_specs=vmem,
        out_shape=jax.ShapeDtypeStruct((2, *own.shape), own.dtype),
        compiler_params=pltpu.CompilerParams(vmem_limit_bytes=VMEM_BYTES // 4),
        name="pair_blocks",
    )(own, other, after)


def correlate_kernel(order, chunks, scale, first, table_ref, *rest):
    o_ref, token_ref, left, tiles, empty, sems = rest[-6:]
    each, senders, _, spectra, rows, lanes = rest[0].shape
    slots = o_ref.shape[2]
    coarse = lanes // AVG
    side = senders * rows
    run = rows // chunks
    count = table_ref[2 * slots]
    token_ref[...] = jnp.zeros_like(token_ref)
    empty[...] = jnp.zeros_like(empty)

    def copy_out(source, c, slot):
        return pltpu.make_async_copy(source, o_ref.at[:, first + c, slot], sems.at[c, slot])

    for slot in range(slots):

        @pl.when(slot >= count)
        def _(slot=slot):
            for c in range(coarse):
                copy_out(empty, c, slot).start()

    for at, block in enumerate(order):
        source = rest[at // each].at[at % each]
        for sender in range(senders):
            for part in range(2):
                for chunk in range(chunks):
                    row = part * side + (chunk * senders + sender) * run
                    pieces = [
                        source[sender, part, s, chunk * run : (chunk + 1) * run]
                        for s in range(spectra)
                    ]
                    for c in range(coarse):
                        left[c, block, row : row + run, :] = jnp.concatenate(
                            [piece[:, c * AVG : (c + 1) * AVG] for piece in pieces], axis=1
                        )

    for slot in range(slots):

        @pl.when(slot < count)
        def _(slot=slot):
            for c in range(coarse):
                rows_of = left[c, table_ref[slot]]
                with_real, with_imag = [
                    lax.dot_general(
                        rows_of,
                        left[c, table_ref[slots + slot], pl.ds(part * side, side), :],
                        (((1,), (1,)), ((), ())),
                        preferred_element_type=jnp.float32,
                    )
                    for part in range(2)
                ]
                tiles[c, slot, 0] = (with_real[:side] + with_imag[side:]) * scale
                tiles[c, slot, 1] = (with_real[side:] - with_imag[:side]) * scale
                copy_out(tiles.at[c, slot], c, slot).start()

    for slot in range(slots):
        for c in range(coarse):
            copy_out(empty, c, slot).wait()


def correlate(table, gathered, after, order, first, channels, chunks, slots, vis):
    _, senders, _, spectra, rows, lanes = gathered[0].shape
    coarse = lanes // AVG
    side = senders * rows
    vmem = pl.BlockSpec(memory_space=pltpu.VMEM)
    anywhere = pl.BlockSpec(memory_space=pl.ANY)
    args = [table, *gathered, after]
    aliases = {}
    if vis is not None:
        args.append(vis)
        aliases = {len(args) - 1: 0}
    return pl.pallas_call(
        functools.partial(correlate_kernel, order, chunks, 1.0 / (AVG * spectra), first),
        grid_spec=pltpu.PrefetchScalarGridSpec(
            num_scalar_prefetch=1,
            grid=(),
            in_specs=[vmem] * len(gathered) + [anywhere] * (len(args) - 1 - len(gathered)),
            out_specs=[anywhere, vmem],
            scratch_shapes=[
                pltpu.VMEM((coarse, len(order), 2 * side, spectra * AVG), jnp.bfloat16),
                pltpu.VMEM((coarse, slots, 2, side, side), jnp.float32),
                pltpu.VMEM((2, side, side), jnp.float32),
                pltpu.SemaphoreType.DMA((coarse, slots)),
            ],
        ),
        out_shape=[
            jax.ShapeDtypeStruct((2, channels, slots, side, side), jnp.float32),
            jax.ShapeDtypeStruct((8, LANES), jnp.float32),
        ],
        input_output_aliases=aliases,
        cost_estimate=pl.CostEstimate(flops=0, bytes_accessed=0, transcendentals=0),
        compiler_params=pltpu.CompilerParams(vmem_limit_bytes=VMEM_BYTES),
        name="correlate_tiles",
    )(*args)


def places(count):
    steps = np.arange(count, dtype=np.int32)
    index = lax.axis_index("ft").astype(jnp.int32)
    return jnp.concatenate([(index + steps) % count, (index + count - steps) % count])


def spread(pieces):
    count = len(pieces)
    return [pieces[0]] + [
        lax.ppermute(pieces[d], "ft", [(i, (i + d) % count) for i in range(count)])
        for d in range(1, count)
    ]


def exchange(own, bit):
    count = lax.axis_size("bl")
    return lax.ppermute(own, "bl", [(i, i ^ bit) for i in range(count)])


def gather_blocks(held, after):
    bit = lax.axis_size("bl") // 4
    other = exchange(held, bit)
    while bit > 1:
        bit //= 2
        held = pair(held, other, after).reshape(-1, *held.shape[1:])
        other = exchange(held, bit)
    return held, other


def gather_apart(own, partner, after):
    bit = lax.axis_size("bl") // 4
    partner, after = lax.optimization_barrier((partner, after))
    held = [own[None], partner[None]]
    while bit:
        held = held + [exchange(block, bit) for block in held]
        bit //= 2
    return held, after


def block_order(count):
    order, bit = [0], count // 2
    while bit:
        order += [r ^ bit for r in order]
        bit //= 2
    return order


def tile_tables(block_ids, tile_owner):
    block_count = lax.axis_size("bl")
    tile_count = block_count * (block_count + 1) // 2
    slot_cap = 2 * tile_count // block_count
    pairs = [(i, j) for i in range(block_count) for j in range(i, block_count)]
    row_table = np.array([i for i, _ in pairs], np.int32)
    col_table = np.array([j for _, j in pairs], np.int32)
    mine = (tile_owner == lax.axis_index("bl")).astype(jnp.int32)
    earlier = np.tril(np.ones((tile_count, tile_count), np.int32), -1)
    rank = jnp.sum(earlier * mine[None, :], axis=1)
    labels = np.arange(block_count, dtype=np.int32)
    shard_of = jnp.sum(jnp.where(block_ids[None, :] == labels[:, None], labels[None, :], 0), axis=1)
    row_shard = jnp.sum(
        jnp.where(row_table[:, None] == labels[None, :], shard_of[None, :], 0), axis=1
    )
    col_shard = jnp.sum(
        jnp.where(col_table[:, None] == labels[None, :], shard_of[None, :], 0), axis=1
    )
    here = (mine[None, :] == 1) & (rank[None, :] == np.arange(slot_cap, dtype=np.int32)[:, None])
    rows = jnp.sum(jnp.where(here, row_shard[None, :], 0), axis=1)
    cols = jnp.sum(jnp.where(here, col_shard[None, :], 0), axis=1)
    index = lax.axis_index("bl")
    table = jnp.concatenate(
        [rows ^ index, cols ^ index, jnp.sum(mine, keepdims=True)]
    ).astype(jnp.int32)
    return table, slot_cap


def takes_kernels(mesh, voltages, coefs):
    dests = mesh.shape["ft"]
    blocks = mesh.shape["bl"]
    inputs = voltages.shape[2] // mesh.shape["bl"]
    per_dev = voltages.shape[1] // (mesh.shape["grp"] * dests)
    chan_count = coefs.shape[1]
    radix = chan_count // MXU
    return (
        per_dev == chan_count
        and chan_count % MXU == 0
        and radix & (radix - 1) == 0
        and radix % dests == 0
        and radix <= 8
        and blocks & (blocks - 1) == 0
        and blocks > 2
        and inputs % LANES == 0
        and LANES % dests == 0
        and (LANES // dests) % ROWS16 == 0
        and (dests * AVG) % LANES == 0
    )


def per_device_kernels(voltages, coefs, block_ids, tile_owner):
    dests = lax.axis_size("ft")
    taps, chan_count = coefs.shape
    radix = chan_count // MXU
    chunks = voltages.shape[2] // LANES
    coef_table = coefs.reshape(taps, MXU, radix).transpose(0, 2, 1)
    place = places(dests)
    table, slot_cap = tile_tables(block_ids, tile_owner)
    matrix, twiddle = matrix_tables(MXU), twiddle_tables(radix, MXU)
    cuts = MXU // LANES
    tables = []
    for cut in range(cuts):
        at = slice(cut * LANES, (cut + 1) * LANES)
        tables.append(np.ascontiguousarray(twiddle[:, :, at]))
        tables.append(np.concatenate([matrix[:, :MXU][:, at], matrix[:, MXU:][:, at]], axis=1))
    coef_table, *tables = stage(coef_table, *tables)
    arrived = spread(pack(voltages, place, dests, radix))
    _, rows, samples = arrived[0].shape
    sizes = (dests, dests, rows, samples, radix)
    made, split = transform_cut(arrived, place, coef_table, tables, 0, sizes, table)
    firsts = [table]
    for cut in range(1, cuts):
        more, _ = transform_cut(split, place, None, tables, cut, sizes, table)
        made = made + more
        firsts.append(more[0][0])
    half = lax.axis_size("bl") // 2
    units = len(made)
    own, other, arrived, tokens, vis = None, None, None, [], None
    for unit in range(units + 1):
        held = None
        if unit < units:
            parts = made[unit]
            if unit > 1:
                parts, _ = lax.optimization_barrier((parts, arrived))
            arrived = spread(parts)
            after = tokens[-1] if tokens else table
            if unit > 0:
                own, held = join(arrived, place, (own, other), after)
            else:
                (own,) = join(arrived, place, (), firsts[-1])
            other = exchange(own, half)
        if unit > 0:
            if unit < units:
                gathered, after = gather_blocks(held, table), table
            else:
                gathered, after = gather_apart(own, other, tokens[-1])
            cut, part = divmod(unit - 1, radix // dests)
            first = (part * MXU + cut * LANES) // AVG
            vis, token = correlate(
                table,
                gathered,
                after,
                block_order(lax.axis_size("bl")),
                first,
                units * LANES // AVG,
                chunks,
                slot_cap,
                vis,
            )
            tokens.append(token)
    return vis


def tile_product(row_part, col_part, norm_scale):
    products = jnp.einsum(
        "pscax,qscay->cpqxy", row_part, col_part, preferred_element_type=jnp.float32
    )
    real_part = products[:, 0, 0] + products[:, 1, 1]
    imag_part = products[:, 1, 0] - products[:, 0, 1]
    return jnp.stack([real_part, imag_part]) * norm_scale


def dft_tables(order_len):
    steps_one = jnp.arange(order_len, dtype=jnp.int32)
    phase_grid = steps_one[:, None] * steps_one[None, :] % order_len
    angles = phase_grid.astype(jnp.float32) * (2.0 * math.pi / order_len)
    return (jnp.cos(angles), jnp.sin(angles))


def transform(filtered):
    per_dev = filtered.shape[1]
    chan_count = filtered.shape[2]
    rows_here = filtered.shape[3]
    outer_len = math.isqrt(chan_count)
    while chan_count % outer_len != 0:
        outer_len = outer_len - 1
    inner_len = chan_count // outer_len
    highest = lax.Precision.HIGHEST
    reshaped = filtered.reshape(2, per_dev, outer_len, inner_len, rows_here)
    real_in = reshaped[0]
    imag_in = reshaped[1]
    cos_outer, sin_outer = dft_tables(outer_len)
    section_re = jnp.einsum("snkb,nm->smkb", real_in, cos_outer, precision=highest) + jnp.einsum(
        "snkb,nm->smkb", imag_in, sin_outer, precision=highest
    )
    section_im = jnp.einsum("snkb,nm->smkb", imag_in, cos_outer, precision=highest) - jnp.einsum(
        "snkb,nm->smkb", real_in, sin_outer, precision=highest
    )
    twiddle_grid = (
        jnp.arange(outer_len, dtype=jnp.int32)[:, None]
        * jnp.arange(inner_len, dtype=jnp.int32)[None, :]
        % chan_count
    )
    twiddle_angles = twiddle_grid.astype(jnp.float32) * (2.0 * math.pi / chan_count)
    cos_twiddle = jnp.cos(twiddle_angles)[None, :, :, None]
    sin_twiddle = jnp.sin(twiddle_angles)[None, :, :, None]
    rot_re = section_re * cos_twiddle + section_im * sin_twiddle
    rot_im = section_im * cos_twiddle - section_re * sin_twiddle
    cos_inner, sin_inner = dft_tables(inner_len)
    final_re = jnp.einsum("smkb,kq->sqmb", rot_re, cos_inner, precision=highest) + jnp.einsum(
        "smkb,kq->sqmb", rot_im, sin_inner, precision=highest
    )
    final_im = jnp.einsum("smkb,kq->sqmb", rot_im, cos_inner, precision=highest) - jnp.einsum(
        "smkb,kq->sqmb", rot_re, sin_inner, precision=highest
    )
    stacked = jnp.stack([final_re, final_im]).reshape(2, per_dev, chan_count, rows_here)
    return (stacked * (1.0 / math.sqrt(chan_count))).astype(jnp.bfloat16)


def apply_taps(window, coef_part, taps_count, out_len):
    filtered = jnp.zeros((2, out_len, window.shape[2], window.shape[3]), jnp.float32)
    for tap_index in range(taps_count):
        filtered = filtered + coef_part[tap_index][None, None, :, None] * window[
            :, tap_index : tap_index + out_len
        ].astype(jnp.float32)
    return filtered


def per_device(voltages, coefs, block_ids, tile_owner):
    taps_count = coefs.shape[0]
    chan_count = coefs.shape[1]
    rows_here = voltages.shape[2]
    per_dev = voltages.shape[1] // chan_count
    volt_blocks = voltages.reshape(2, per_dev, chan_count, rows_here)
    phase_block = lax.all_to_all(volt_blocks, "ft", split_axis=2, concat_axis=1, tiled=True)
    spectra_count = phase_block.shape[1]
    phase_here = phase_block.shape[2]
    coef_part = lax.dynamic_slice_in_dim(coefs, lax.axis_index("ft") * phase_here, phase_here, 1)
    zero_front = jnp.zeros((2, taps_count - 1, phase_here, rows_here), phase_block.dtype)
    long_window = jnp.concatenate([zero_front, phase_block], axis=1)
    phase_filtered = apply_taps(long_window, coef_part, taps_count, spectra_count)
    filtered = lax.all_to_all(phase_filtered, "ft", split_axis=1, concat_axis=2, tiled=True)
    spectra = transform(filtered)
    turned = lax.all_to_all(spectra, "ft", split_axis=2, concat_axis=1, tiled=True)
    spectra_all = turned.shape[1]
    chan_here = turned.shape[2]
    coarse_here = chan_here // AVG
    coarse_view = turned.reshape(2, spectra_all, coarse_here, AVG, rows_here)
    norm_scale = 1.0 / (AVG * spectra_all)
    block_count = lax.axis_size("bl")
    my_index = lax.axis_index("bl")
    tile_count = block_count * (block_count + 1) // 2
    slot_cap = 2 * tile_count // block_count
    row_table = jnp.asarray(
        np.array(
            [
                first_id
                for first_id in range(block_count)
                for second_id in range(first_id, block_count)
            ],
            dtype=np.int32,
        )
    )
    col_table = jnp.asarray(
        np.array(
            [
                second_id
                for first_id in range(block_count)
                for second_id in range(first_id, block_count)
            ],
            dtype=np.int32,
        )
    )
    tile_pos = jnp.arange(tile_count, dtype=jnp.int32)
    same_owner = tile_owner[None, :] == tile_owner[:, None]
    before_mask = tile_pos[None, :] < tile_pos[:, None]
    slot_rank = jnp.sum((same_owner & before_mask).astype(jnp.int32), axis=1)
    labels = jnp.arange(block_count, dtype=jnp.int32)
    shard_of = jnp.sum(jnp.where(block_ids[None, :] == labels[:, None], labels[None, :], 0), axis=1)
    gathered = lax.all_gather(coarse_view[None], "bl", axis=0, tiled=True)
    mine_mask = tile_owner == my_index
    own_count = jnp.sum(mine_mask.astype(jnp.int32))
    slot_steps = jnp.arange(slot_cap, dtype=jnp.int32)
    slot_tile = jnp.sum(
        jnp.where(
            mine_mask[None, :] & (slot_rank[None, :] == slot_steps[:, None]), tile_pos[None, :], 0
        ),
        axis=1,
    )

    def one_tile(slot_pos, result_tiles):
        tile_id = slot_tile[slot_pos]
        row_block = gathered[shard_of[row_table[tile_id]]]
        col_block = gathered[shard_of[col_table[tile_id]]]
        tile = tile_product(row_block, col_block, norm_scale)
        return lax.dynamic_update_slice(result_tiles, tile[:, :, None], (0, 0, slot_pos, 0, 0))

    empty_tiles = jnp.zeros((2, coarse_here, slot_cap, rows_here, rows_here), jnp.float32)
    return lax.fori_loop(0, own_count, one_tile, empty_tiles)


def solution(mesh):
    def correlator(voltages, coefs, block_ids, tile_owner):
        fits = takes_kernels(mesh, voltages, coefs)
        return jax.shard_map(
            per_device_kernels if fits else per_device,
            mesh=mesh,
            in_specs=(P(None, ("grp", "ft"), "bl"), P(), P(), P("grp")),
            out_specs=P(None, ("grp", "ft"), "bl", None, None),
            check_vma=False,
        )(voltages, coefs, block_ids, tile_owner)

    return correlator
```

```python
import functools
import math

import jax
import jax.numpy as jnp
import ml_dtypes
import numpy as np
from jax import lax
from jax.experimental import pallas as pl
from jax.experimental.pallas import tpu as pltpu
from jax.sharding import PartitionSpec as P

AVG = 64
MXU = 256
LANES = 128
ROWS16 = 16
VMEM_BYTES = 48 * 1024 * 1024


def split_bf16(table):
    high = table.astype(ml_dtypes.bfloat16)
    low = (table - high.astype(np.float64)).astype(ml_dtypes.bfloat16)
    return high, low


def matrix_tables(inner_len):
    steps = np.arange(inner_len)
    angles = 2.0 * np.pi * (np.outer(steps, steps) % inner_len) / inner_len
    cos_part, sin_part = np.cos(angles), np.sin(angles)
    high, low = split_bf16(np.block([[cos_part, -sin_part], [sin_part, cos_part]]))
    return np.concatenate([high, high, low])


def twiddle_tables(radix, inner_len):
    chan_count = radix * inner_len
    angles = 2.0 * np.pi * np.outer(np.arange(radix), np.arange(inner_len)) / chan_count
    scale = 1.0 / math.sqrt(chan_count)
    return np.stack([np.cos(angles) * scale, np.sin(angles) * scale]).astype(np.float32)


def rotate(real, imag, step, count):
    step = step % count
    if step == 0:
        return real, imag
    if 4 * step == count:
        return imag, -real
    if 2 * step == count:
        return -real, -imag
    if 4 * step == 3 * count:
        return -imag, real
    cos_step = math.cos(2.0 * math.pi * step / count)
    sin_step = math.sin(2.0 * math.pi * step / count)
    if 8 * step == count:
        return cos_step * (real + imag), cos_step * (imag - real)
    return cos_step * real + sin_step * imag, cos_step * imag - sin_step * real


def butterflies(parts):
    count = len(parts)
    if count == 1:
        return parts
    half = count // 2
    sums, diffs = [], []
    for k in range(half):
        (ar, ai), (br, bi) = parts[k], parts[k + half]
        sums.append((ar + br, ai + bi))
        diffs.append(rotate(ar - br, ai - bi, k, count))
    even, odd = butterflies(sums), butterflies(diffs)
    out = []
    for k in range(half):
        out += [even[k], odd[k]]
    return out


def pack_kernel(radix, place_ref, v_ref, *rest):
    o_refs, (wide, turned) = rest[:-2], rest[-2:]
    dests, rows, samples = turned.shape
    inner = samples // radix
    for part in range(2):
        for chunk in range(v_ref.shape[2] // LANES):
            wide[...] = v_ref[part, :, chunk * LANES : (chunk + 1) * LANES].astype(jnp.float32)
            for phase in range(radix):
                here = wide[pl.ds(phase, inner, stride=radix), :].T.astype(jnp.bfloat16)
                for dest in range(dests):
                    turned[dest, :, phase * inner : (phase + 1) * inner] = here[
                        dest * rows : (dest + 1) * rows
                    ]
            for shift in range(dests):
                o_refs[shift][part, chunk * rows : (chunk + 1) * rows] = turned[place_ref[shift]]


def pack(voltages, place, dests, radix):
    _, samples, inputs = voltages.shape
    chunks = inputs // LANES
    rows = LANES // dests
    vmem = pl.BlockSpec(memory_space=pltpu.VMEM)
    return pl.pallas_call(
        functools.partial(pack_kernel, radix),
        grid_spec=pltpu.PrefetchScalarGridSpec(
            num_scalar_prefetch=1,
            grid=(),
            in_specs=[vmem],
            out_specs=[vmem] * dests,
            scratch_shapes=[
                pltpu.VMEM((samples, LANES), jnp.float32),
                pltpu.VMEM((dests, rows, samples), jnp.bfloat16),
            ],
        ),
        out_shape=[jax.ShapeDtypeStruct((2, chunks * rows, samples), jnp.bfloat16)] * dests,
        compiler_params=pltpu.CompilerParams(vmem_limit_bytes=VMEM_BYTES // 2),
        name="pack_inputs",
    )(place, voltages)


def stage_kernel(*refs):
    half = len(refs) // 2
    for source, target in zip(refs[:half], refs[half:]):
        target[...] = source[...]


def stage(*tables):
    vmem = pl.BlockSpec(memory_space=pltpu.VMEM)
    return pl.pallas_call(
        stage_kernel,
        in_specs=[vmem] * len(tables),
        out_specs=[vmem] * len(tables),
        out_shape=[jax.ShapeDtypeStruct(table.shape, table.dtype) for table in tables],
        compiler_params=pltpu.CompilerParams(vmem_limit_bytes=VMEM_BYTES // 4),
        name="stage_tables",
    )(*tables)


def filter_blocks(place_ref, v_refs, c_ref, held, split):
    spectra, _, rows, samples = held.shape
    taps, radix, inner = c_ref.shape
    for shift in range(len(v_refs)):
        held[place_ref[len(v_refs) + shift]] = v_refs[shift][...]

    @pl.loop(0, radix)
    def _(phase):
        lane0 = pl.multiple_of(phase * inner, inner)
        row0 = pl.multiple_of(phase * spectra * rows, spectra * rows)
        for part in range(2):
            for sub in range(0, rows, ROWS16):
                blocks = [
                    held[b, part, pl.ds(sub, ROWS16), pl.ds(lane0, inner)].astype(jnp.float32)
                    for b in range(spectra)
                ]
                for s in range(spectra):
                    total = None
                    for b in range(max(0, s - taps + 1), s + 1):
                        term = c_ref[taps - 1 - s + b, pl.ds(phase, 1), :] * blocks[b]
                        total = term if total is None else total + term
                    high = total.astype(jnp.bfloat16)
                    low = (total - high.astype(jnp.float32)).astype(jnp.bfloat16)
                    at = pl.ds(pl.multiple_of(row0 + s * rows + sub, ROWS16), ROWS16)
                    split[at, part * inner : (part + 1) * inner] = high
                    split[at, (2 + part) * inner : (3 + part) * inner] = low


def transform_lanes(place_ref, split, tw_ref, g_ref, prod, made, out_refs):
    dests, halves, _, spectra, rows, _ = made.shape
    radix = tw_ref.shape[1]
    group = spectra * rows
    depth = split.shape[1] // 2

    @pl.loop(0, radix // 4)
    def _(four):
        at = pl.ds(pl.multiple_of(four * 4 * group, 4 * group), 4 * group)
        high = split[at, :depth]
        line = jnp.concatenate([high, split[at, depth:], high], axis=1)
        prod[at, :] = jnp.dot(line, g_ref[...], preferred_element_type=jnp.float32)

    @pl.loop(0, spectra)
    def _(s):
        for sub in range(0, rows, ROWS16):
            parts = []
            for phase in range(radix):
                at = pl.ds(pl.multiple_of(phase * group + s * rows + sub, ROWS16), ROWS16)
                yr, yi = prod[at, :LANES], prod[at, LANES:]
                cos_here = tw_ref[0, phase : phase + 1, :]
                sin_here = tw_ref[1, phase : phase + 1, :]
                if phase == 0:
                    parts.append((yr * cos_here, yi * cos_here))
                else:
                    parts.append((yr * cos_here + yi * sin_here, yi * cos_here - yr * sin_here))
            for step, pair in enumerate(butterflies(parts)):
                for part in range(2):
                    made[step // halves, step % halves, part, s, sub : sub + ROWS16, :] = pair[
                        part
                    ].astype(jnp.bfloat16)

    for shift in range(dests):
        for half in range(halves):
            out_refs[half * dests + shift][...] = made[place_ref[shift], half]


def transform_cut(source, place, coef_table, tables, cut, sizes, after):
    dests, spectra, rows, samples, radix = sizes
    inner = samples // radix
    halves = radix // dests
    total = radix * spectra * rows
    begins = coef_table is not None
    vmem = pl.BlockSpec(memory_space=pltpu.VMEM)

    def kernel(place_ref, *rest):
        if begins:
            v_refs, (c_ref, tw_ref, g_ref) = rest[:dests], rest[dests : dests + 3]
            out_refs, (split, held, prod, made) = rest[dests + 4 : -4], rest[-4:]
            filter_blocks(place_ref, v_refs, c_ref, held, split)
        else:
            split, tw_ref, g_ref = rest[:3]
            out_refs, (prod, made) = rest[4:-2], rest[-2:]
        transform_lanes(place_ref, split, tw_ref, g_ref, prod, made, out_refs)

    scratch = [
        pltpu.VMEM((total, 2 * LANES), jnp.float32),
        pltpu.VMEM((dests, halves, 2, spectra, rows, LANES), jnp.bfloat16),
    ]
    shapes = [jax.ShapeDtypeStruct((2, spectra, rows, LANES), jnp.bfloat16)] * (halves * dests)
    if begins:
        scratch = [pltpu.VMEM((spectra, 2, rows, samples), jnp.bfloat16)] + scratch
        shapes = shapes + [jax.ShapeDtypeStruct((total, 4 * inner), jnp.bfloat16)]
    args = [*source, coef_table] if begins else [source]
    args += [tables[2 * cut], tables[2 * cut + 1]]
    made = pl.pallas_call(
        kernel,
        grid_spec=pltpu.PrefetchScalarGridSpec(
            num_scalar_prefetch=1,
            grid=(),
            in_specs=[vmem] * len(args) + [pl.BlockSpec(memory_space=pl.ANY)],
            out_specs=[vmem] * len(shapes),
            scratch_shapes=scratch,
        ),
        out_shape=shapes,
        cost_estimate=pl.CostEstimate(
            flops=3 * 2 * total * 4 * inner * LANES, bytes_accessed=6 << 20, transcendentals=0
        ),
        compiler_params=pltpu.CompilerParams(vmem_limit_bytes=VMEM_BYTES // 2),
        name="filter_transform" if begins else "transform_rest",
    )(place, *args, after)
    units = [made[half * dests : (half + 1) * dests] for half in range(halves)]
    return units, made[-1]


def join(pieces, place, before, after):
    count = len(pieces)
    vmem = pl.BlockSpec(memory_space=pltpu.VMEM)
    shapes = [jax.ShapeDtypeStruct((count, *pieces[0].shape), pieces[0].dtype)]
    if before:
        shapes.append(jax.ShapeDtypeStruct((2, *before[0].shape), before[0].dtype))

    def kernel(place_ref, *rest):
        ins, outs = rest[: count + len(before)], rest[count + len(before) + 1 :]
        for shift in range(count):
            outs[0][place_ref[count + shift]] = ins[shift][...]
        for at in range(len(before)):
            outs[1][at] = ins[count + at][...]

    return pl.pallas_call(
        kernel,
        grid_spec=pltpu.PrefetchScalarGridSpec(
            num_scalar_prefetch=1,
            grid=(),
            in_specs=[vmem] * (count + len(before)) + [pl.BlockSpec(memory_space=pl.ANY)],
            out_specs=[vmem] * len(shapes),
        ),
        out_shape=shapes,
        compiler_params=pltpu.CompilerParams(vmem_limit_bytes=VMEM_BYTES // 4),
        name="join_pieces",
    )(place, *pieces, *before, after)


def pair(own, other, after):
    def kernel(own_ref, other_ref, _, out_ref):
        out_ref[0] = own_ref[...]
        out_ref[1] = other_ref[...]

    vmem = pl.BlockSpec(memory_space=pltpu.VMEM)
    return pl.pallas_call(
        kernel,
        in_specs=[vmem, vmem, pl.BlockSpec(memory_space=pl.ANY)],
        out_specs=vmem,
        out_shape=jax.ShapeDtypeStruct((2, *own.shape), own.dtype),
        compiler_params=pltpu.CompilerParams(vmem_limit_bytes=VMEM_BYTES // 4),
        name="pair_blocks",
    )(own, other, after)


def correlate_kernel(order, chunks, scale, first, table_ref, *rest):
    o_ref, token_ref, left, tiles, empty, sems = rest[-6:]
    each, senders, _, spectra, rows, lanes = rest[0].shape
    slots = o_ref.shape[2]
    coarse = lanes // AVG
    side = senders * rows
    run = rows // chunks
    count = table_ref[2 * slots]
    token_ref[...] = jnp.zeros_like(token_ref)
    empty[...] = jnp.zeros_like(empty)

    def copy_out(source, c, slot):
        return pltpu.make_async_copy(source, o_ref.at[:, first + c, slot], sems.at[c, slot])

    for slot in range(slots):

        @pl.when(slot >= count)
        def _(slot=slot):
            for c in range(coarse):
                copy_out(empty, c, slot).start()

    for at, block in enumerate(order):
        source = rest[at // each].at[at % each]
        for sender in range(senders):
            for part in range(2):
                for chunk in range(chunks):
                    row = part * side + (chunk * senders + sender) * run
                    pieces = [
                        source[sender, part, s, chunk * run : (chunk + 1) * run]
                        for s in range(spectra)
                    ]
                    for c in range(coarse):
                        left[c, block, row : row + run, :] = jnp.concatenate(
                            [piece[:, c * AVG : (c + 1) * AVG] for piece in pieces], axis=1
                        )

    for slot in range(slots):

        @pl.when(slot < count)
        def _(slot=slot):
            for c in range(coarse):
                rows_of = left[c, table_ref[slot]]
                with_real, with_imag = [
                    lax.dot_general(
                        rows_of,
                        left[c, table_ref[slots + slot], pl.ds(part * side, side), :],
                        (((1,), (1,)), ((), ())),
                        preferred_element_type=jnp.float32,
                    )
                    for part in range(2)
                ]
                tiles[c, slot, 0] = (with_real[:side] + with_imag[side:]) * scale
                tiles[c, slot, 1] = (with_real[side:] - with_imag[:side]) * scale
                copy_out(tiles.at[c, slot], c, slot).start()

    for slot in range(slots):
        for c in range(coarse):
            copy_out(empty, c, slot).wait()


def correlate(table, gathered, after, order, first, channels, chunks, slots, vis):
    _, senders, _, spectra, rows, lanes = gathered[0].shape
    coarse = lanes // AVG
    side = senders * rows
    vmem = pl.BlockSpec(memory_space=pltpu.VMEM)
    anywhere = pl.BlockSpec(memory_space=pl.ANY)
    args = [table, *gathered, after]
    aliases = {}
    if vis is not None:
        args.append(vis)
        aliases = {len(args) - 1: 0}
    return pl.pallas_call(
        functools.partial(correlate_kernel, order, chunks, 1.0 / (AVG * spectra), first),
        grid_spec=pltpu.PrefetchScalarGridSpec(
            num_scalar_prefetch=1,
            grid=(),
            in_specs=[vmem] * len(gathered) + [anywhere] * (len(args) - 1 - len(gathered)),
            out_specs=[anywhere, vmem],
            scratch_shapes=[
                pltpu.VMEM((coarse, len(order), 2 * side, spectra * AVG), jnp.bfloat16),
                pltpu.VMEM((coarse, slots, 2, side, side), jnp.float32),
                pltpu.VMEM((2, side, side), jnp.float32),
                pltpu.SemaphoreType.DMA((coarse, slots)),
            ],
        ),
        out_shape=[
            jax.ShapeDtypeStruct((2, channels, slots, side, side), jnp.float32),
            jax.ShapeDtypeStruct((8, LANES), jnp.float32),
        ],
        input_output_aliases=aliases,
        cost_estimate=pl.CostEstimate(flops=0, bytes_accessed=0, transcendentals=0),
        compiler_params=pltpu.CompilerParams(vmem_limit_bytes=VMEM_BYTES),
        name="correlate_tiles",
    )(*args)


def places(count):
    steps = np.arange(count, dtype=np.int32)
    index = lax.axis_index("ft").astype(jnp.int32)
    return jnp.concatenate([(index + steps) % count, (index + count - steps) % count])


def spread(pieces):
    count = len(pieces)
    return [pieces[0]] + [
        lax.ppermute(pieces[d], "ft", [(i, (i + d) % count) for i in range(count)])
        for d in range(1, count)
    ]


def exchange(own, bit):
    count = lax.axis_size("bl")
    return lax.ppermute(own, "bl", [(i, i ^ bit) for i in range(count)])


def gather_blocks(held, after):
    bit = lax.axis_size("bl") // 4
    other = exchange(held, bit)
    while bit > 1:
        bit //= 2
        held = pair(held, other, after).reshape(-1, *held.shape[1:])
        other = exchange(held, bit)
    return held, other


def gather_apart(own, partner, after):
    bit = lax.axis_size("bl") // 4
    partner, after = lax.optimization_barrier((partner, after))
    held = [own[None], partner[None]]
    while bit:
        held = held + [exchange(block, bit) for block in held]
        bit //= 2
    return held, after


def block_order(count):
    order, bit = [0], count // 2
    while bit:
        order += [r ^ bit for r in order]
        bit //= 2
    return order


def tile_tables(block_ids, tile_owner):
    block_count = lax.axis_size("bl")
    tile_count = block_count * (block_count + 1) // 2
    slot_cap = 2 * tile_count // block_count
    pairs = [(i, j) for i in range(block_count) for j in range(i, block_count)]
    row_table = np.array([i for i, _ in pairs], np.int32)
    col_table = np.array([j for _, j in pairs], np.int32)
    mine = (tile_owner == lax.axis_index("bl")).astype(jnp.int32)
    earlier = np.tril(np.ones((tile_count, tile_count), np.int32), -1)
    rank = jnp.sum(earlier * mine[None, :], axis=1)
    labels = np.arange(block_count, dtype=np.int32)
    shard_of = jnp.sum(jnp.where(block_ids[None, :] == labels[:, None], labels[None, :], 0), axis=1)
    row_shard = jnp.sum(
        jnp.where(row_table[:, None] == labels[None, :], shard_of[None, :], 0), axis=1
    )
    col_shard = jnp.sum(
        jnp.where(col_table[:, None] == labels[None, :], shard_of[None, :], 0), axis=1
    )
    here = (mine[None, :] == 1) & (rank[None, :] == np.arange(slot_cap, dtype=np.int32)[:, None])
    rows = jnp.sum(jnp.where(here, row_shard[None, :], 0), axis=1)
    cols = jnp.sum(jnp.where(here, col_shard[None, :], 0), axis=1)
    index = lax.axis_index("bl")
    table = jnp.concatenate(
        [rows ^ index, cols ^ index, jnp.sum(mine, keepdims=True)]
    ).astype(jnp.int32)
    return table, slot_cap


def takes_kernels(mesh, voltages, coefs):
    dests = mesh.shape["ft"]
    blocks = mesh.shape["bl"]
    inputs = voltages.shape[2] // mesh.shape["bl"]
    per_dev = voltages.shape[1] // (mesh.shape["grp"] * dests)
    chan_count = coefs.shape[1]
    radix = chan_count // MXU
    return (
        per_dev == chan_count
        and chan_count % MXU == 0
        and radix & (radix - 1) == 0
        and radix % dests == 0
        and radix % 4 == 0
        and radix <= 8
        and blocks & (blocks - 1) == 0
        and blocks > 2
        and inputs % LANES == 0
        and LANES % dests == 0
        and (LANES // dests) % ROWS16 == 0
        and (dests * AVG) % LANES == 0
    )


def per_device_kernels(voltages, coefs, block_ids, tile_owner):
    dests = lax.axis_size("ft")
    taps, chan_count = coefs.shape
    radix = chan_count // MXU
    chunks = voltages.shape[2] // LANES
    coef_table = coefs.reshape(taps, MXU, radix).transpose(0, 2, 1)
    place = places(dests)
    table, slot_cap = tile_tables(block_ids, tile_owner)
    matrix, twiddle = matrix_tables(MXU), twiddle_tables(radix, MXU)
    cuts = MXU // LANES
    tables = []
    for cut in range(cuts):
        at = slice(cut * LANES, (cut + 1) * LANES)
        tables.append(np.ascontiguousarray(twiddle[:, :, at]))
        tables.append(np.concatenate([matrix[:, :MXU][:, at], matrix[:, MXU:][:, at]], axis=1))
    coef_table, *tables = stage(coef_table, *tables)
    arrived = spread(pack(voltages, place, dests, radix))
    _, rows, samples = arrived[0].shape
    sizes = (dests, dests, rows, samples, radix)
    made, split = transform_cut(arrived, place, coef_table, tables, 0, sizes, table)
    firsts = [table]
    for cut in range(1, cuts):
        more, _ = transform_cut(split, place, None, tables, cut, sizes, table)
        made = made + more
        firsts.append(more[0][0])
    half = lax.axis_size("bl") // 2
    units = len(made)
    own, other, arrived, tokens, vis = None, None, None, [], None
    for unit in range(units + 1):
        held = None
        if unit < units:
            parts = made[unit]
            if unit > 1:
                parts, _ = lax.optimization_barrier((parts, arrived))
            arrived = spread(parts)
            after = tokens[-1] if tokens else table
            if unit > 0:
                own, held = join(arrived, place, (own, other), after)
            else:
                (own,) = join(arrived, place, (), firsts[-1])
            other = exchange(own, half)
        if unit > 0:
            if unit < units:
                gathered, after = gather_blocks(held, table), table
            else:
                gathered, after = gather_apart(own, other, tokens[-1])
            cut, part = divmod(unit - 1, radix // dests)
            first = (part * MXU + cut * LANES) // AVG
            vis, token = correlate(
                table,
                gathered,
                after,
                block_order(lax.axis_size("bl")),
                first,
                units * LANES // AVG,
                chunks,
                slot_cap,
                vis,
            )
            tokens.append(token)
    return vis


def tile_product(row_part, col_part, norm_scale):
    products = jnp.einsum(
        "pscax,qscay->cpqxy", row_part, col_part, preferred_element_type=jnp.float32
    )
    real_part = products[:, 0, 0] + products[:, 1, 1]
    imag_part = products[:, 1, 0] - products[:, 0, 1]
    return jnp.stack([real_part, imag_part]) * norm_scale


def dft_tables(order_len):
    steps_one = jnp.arange(order_len, dtype=jnp.int32)
    phase_grid = steps_one[:, None] * steps_one[None, :] % order_len
    angles = phase_grid.astype(jnp.float32) * (2.0 * math.pi / order_len)
    return (jnp.cos(angles), jnp.sin(angles))


def transform(filtered):
    per_dev = filtered.shape[1]
    chan_count = filtered.shape[2]
    rows_here = filtered.shape[3]
    outer_len = math.isqrt(chan_count)
    while chan_count % outer_len != 0:
        outer_len = outer_len - 1
    inner_len = chan_count // outer_len
    highest = lax.Precision.HIGHEST
    reshaped = filtered.reshape(2, per_dev, outer_len, inner_len, rows_here)
    real_in = reshaped[0]
    imag_in = reshaped[1]
    cos_outer, sin_outer = dft_tables(outer_len)
    section_re = jnp.einsum("snkb,nm->smkb", real_in, cos_outer, precision=highest) + jnp.einsum(
        "snkb,nm->smkb", imag_in, sin_outer, precision=highest
    )
    section_im = jnp.einsum("snkb,nm->smkb", imag_in, cos_outer, precision=highest) - jnp.einsum(
        "snkb,nm->smkb", real_in, sin_outer, precision=highest
    )
    twiddle_grid = (
        jnp.arange(outer_len, dtype=jnp.int32)[:, None]
        * jnp.arange(inner_len, dtype=jnp.int32)[None, :]
        % chan_count
    )
    twiddle_angles = twiddle_grid.astype(jnp.float32) * (2.0 * math.pi / chan_count)
    cos_twiddle = jnp.cos(twiddle_angles)[None, :, :, None]
    sin_twiddle = jnp.sin(twiddle_angles)[None, :, :, None]
    rot_re = section_re * cos_twiddle + section_im * sin_twiddle
    rot_im = section_im * cos_twiddle - section_re * sin_twiddle
    cos_inner, sin_inner = dft_tables(inner_len)
    final_re = jnp.einsum("smkb,kq->sqmb", rot_re, cos_inner, precision=highest) + jnp.einsum(
        "smkb,kq->sqmb", rot_im, sin_inner, precision=highest
    )
    final_im = jnp.einsum("smkb,kq->sqmb", rot_im, cos_inner, precision=highest) - jnp.einsum(
        "smkb,kq->sqmb", rot_re, sin_inner, precision=highest
    )
    stacked = jnp.stack([final_re, final_im]).reshape(2, per_dev, chan_count, rows_here)
    return (stacked * (1.0 / math.sqrt(chan_count))).astype(jnp.bfloat16)


def apply_taps(window, coef_part, taps_count, out_len):
    filtered = jnp.zeros((2, out_len, window.shape[2], window.shape[3]), jnp.float32)
    for tap_index in range(taps_count):
        filtered = filtered + coef_part[tap_index][None, None, :, None] * window[
            :, tap_index : tap_index + out_len
        ].astype(jnp.float32)
    return filtered


def per_device(voltages, coefs, block_ids, tile_owner):
    taps_count = coefs.shape[0]
    chan_count = coefs.shape[1]
    rows_here = voltages.shape[2]
    per_dev = voltages.shape[1] // chan_count
    volt_blocks = voltages.reshape(2, per_dev, chan_count, rows_here)
    phase_block = lax.all_to_all(volt_blocks, "ft", split_axis=2, concat_axis=1, tiled=True)
    spectra_count = phase_block.shape[1]
    phase_here = phase_block.shape[2]
    coef_part = lax.dynamic_slice_in_dim(coefs, lax.axis_index("ft") * phase_here, phase_here, 1)
    zero_front = jnp.zeros((2, taps_count - 1, phase_here, rows_here), phase_block.dtype)
    long_window = jnp.concatenate([zero_front, phase_block], axis=1)
    phase_filtered = apply_taps(long_window, coef_part, taps_count, spectra_count)
    filtered = lax.all_to_all(phase_filtered, "ft", split_axis=1, concat_axis=2, tiled=True)
    spectra = transform(filtered)
    turned = lax.all_to_all(spectra, "ft", split_axis=2, concat_axis=1, tiled=True)
    spectra_all = turned.shape[1]
    chan_here = turned.shape[2]
    coarse_here = chan_here // AVG
    coarse_view = turned.reshape(2, spectra_all, coarse_here, AVG, rows_here)
    norm_scale = 1.0 / (AVG * spectra_all)
    block_count = lax.axis_size("bl")
    my_index = lax.axis_index("bl")
    tile_count = block_count * (block_count + 1) // 2
    slot_cap = 2 * tile_count // block_count
    row_table = jnp.asarray(
        np.array(
            [
                first_id
                for first_id in range(block_count)
                for second_id in range(first_id, block_count)
            ],
            dtype=np.int32,
        )
    )
    col_table = jnp.asarray(
        np.array(
            [
                second_id
                for first_id in range(block_count)
                for second_id in range(first_id, block_count)
            ],
            dtype=np.int32,
        )
    )
    tile_pos = jnp.arange(tile_count, dtype=jnp.int32)
    same_owner = tile_owner[None, :] == tile_owner[:, None]
    before_mask = tile_pos[None, :] < tile_pos[:, None]
    slot_rank = jnp.sum((same_owner & before_mask).astype(jnp.int32), axis=1)
    labels = jnp.arange(block_count, dtype=jnp.int32)
    shard_of = jnp.sum(jnp.where(block_ids[None, :] == labels[:, None], labels[None, :], 0), axis=1)
    gathered = lax.all_gather(coarse_view[None], "bl", axis=0, tiled=True)
    mine_mask = tile_owner == my_index
    own_count = jnp.sum(mine_mask.astype(jnp.int32))
    slot_steps = jnp.arange(slot_cap, dtype=jnp.int32)
    slot_tile = jnp.sum(
        jnp.where(
            mine_mask[None, :] & (slot_rank[None, :] == slot_steps[:, None]), tile_pos[None, :], 0
        ),
        axis=1,
    )

    def one_tile(slot_pos, result_tiles):
        tile_id = slot_tile[slot_pos]
        row_block = gathered[shard_of[row_table[tile_id]]]
        col_block = gathered[shard_of[col_table[tile_id]]]
        tile = tile_product(row_block, col_block, norm_scale)
        return lax.dynamic_update_slice(result_tiles, tile[:, :, None], (0, 0, slot_pos, 0, 0))

    empty_tiles = jnp.zeros((2, coarse_here, slot_cap, rows_here, rows_here), jnp.float32)
    return lax.fori_loop(0, own_count, one_tile, empty_tiles)


def solution(mesh):
    def correlator(voltages, coefs, block_ids, tile_owner):
        fits = takes_kernels(mesh, voltages, coefs)
        return jax.shard_map(
            per_device_kernels if fits else per_device,
            mesh=mesh,
            in_specs=(P(None, ("grp", "ft"), "bl"), P(), P(), P("grp")),
            out_specs=P(None, ("grp", "ft"), "bl", None, None),
            check_vma=False,
        )(voltages, coefs, block_ids, tile_owner)

    return correlator
```
